512 devices in a mesh: gx: 32 (over z, x), gy: 16 (over y, core).
Axes of the slice: x: 4, y: 8, z: 8, core: 2. Of those that a mesh axis runs over, the one named last changes fastest.
Arguments:
- source: float32 [5, 4, 4, 4, 64, 32, 128], P(None, None, None, None, 'gx', 'gy'), may hold values from -18 to 18
- jacobian: float32 [3, 5, 5, 64, 32, 128], P(None, None, None, 'gx', 'gy'), may hold values from -1.8 to 1.8
- damping: float32 [64, 32, 128], P('gx', 'gy'), may hold values from 0.3 to 1.2
- orient: int32 [3, 64, 32, 128], P(None, 'gx', 'gy'), may hold values 0 or 1
- smoother: bfloat16 [5, 5, 4, 4, 4, 64, 32, 128], P(None, None, None, None, None, 'gx', 'gy'), may hold values from -0.4 to 0.4, as said below
- coarse_smoother: bfloat16 [5, 5, 2, 2, 2, 64, 32, 128], P(None, None, None, None, None, 'gx', 'gy'), may hold values from -0.61 to 1.11, as said below
Outputs:
- corrected: float32 [5, 4, 4, 4, 64, 32, 128], P(None, None, None, None, 'gx', 'gy')
The draws below stay inside these ranges and needn't reach their ends.
Inputs may be any that keep to these rules, and one draw needn't show every extreme that they name: `smoother`: each 5 x 5 block is a positive node scale times the identity plus independent entries. `coarse_smoother`: each 5 x 5 block is a positive node scale times the identity plus independent entries.
All inputs are finite; a program needn't handle non-finite values. No bound on the sum of `orient` on one device may be relied on, other than what follows from the above.
Results may differ from the reference program's by a relative error of at most 0.0003.
Values sent between devices are 32-bit elements; how exact they have to be, the bound alone decides.
A program may use at most 64 MiB of HBM per device.

```python
import math
import jax
import jax.numpy as jnp
import numpy as np

VARS = 5
NODES = 4
CNODES = 2
CSWEEPS = 3
NZE = 128
NXE = 64
NYE = 32


def block_inverse(key, node_count, scale_low, scale_high, normal_weight):
    noise_key = jax.random.fold_in(key, 0)
    scale_key = jax.random.fold_in(key, 2)
    shape_full = (5, 5, node_count, node_count, node_count, NXE, NYE, NZE)
    noise = normal_weight * jnp.clip(jax.random.normal(noise_key, shape_full, jnp.float32), -4.0, 4.0)
    scales = jax.random.uniform(scale_key, (1, 1, node_count, node_count, node_count, NXE, NYE, NZE), jnp.float32, scale_low, scale_high)
    identity = jnp.eye(5, dtype=jnp.float32).reshape(5, 5, 1, 1, 1, 1, 1, 1)
    return ((identity + noise) * scales).astype(jnp.bfloat16)


def draw_smoother(key, part):
    key = jax.random.fold_in(key, 5)
    return block_inverse(key, NODES, 0.06, 0.18, 0.3)


def draw_coarse_smoother(key, part):
    key = jax.random.fold_in(key, 9)
    return block_inverse(key, CNODES, 0.25, 0.5, 0.3)


def touch_ends(values, key, low, largest):
    spot = [jax.random.randint(jax.random.fold_in(key, axis), (), 0, length) for axis, length in enumerate(values.shape)]
    widest = values.shape.index(max(values.shape))
    beside = spot[:widest] + [(spot[widest] + 1) % values.shape[widest]] + spot[widest + 1:]
    return values.at[tuple(spot)].set(low).at[tuple(beside)].set(largest)


def block_scale(stream_key, extent, cuts, low, largest):
    gain = 1.0
    for dim, parts in cuts:
        heights = jax.random.uniform(jax.random.fold_in(jax.random.fold_in(stream_key, 6), dim), (parts,), jnp.float32, low / len(cuts), largest / len(cuts))
        gain = gain * jnp.repeat(jnp.exp(heights), extent[dim] // parts).reshape((-1,) + (1,) * (len(extent) - 1 - dim))
    return gain


def normal_values(own_key, shape, deviation, bound, shards=(), held_as=jnp.bfloat16):
    loudness = block_scale(own_key, shape, shards, -0.22, 0.18) if shards else 1.0
    drawn = jax.random.normal(own_key, shape, jnp.float32) * deviation * loudness
    return jnp.minimum(jnp.maximum(drawn, -bound), bound).astype(held_as)


def setup_inputs(seed: int = 0) -> dict:
    keys = jax.random.split(jax.random.key(seed), 7)
    source = normal_values(keys[0], (VARS, NODES, NODES, NODES, NXE, NYE, NZE), 3.0, 18.0, ((4, 32), (5, 16)), jnp.float32)
    jacobian = normal_values(keys[1], (3, VARS, VARS, NXE, NYE, NZE), 0.3, 1.8, ((3, 32), (4, 16)), jnp.float32)
    damping = jnp.clip(0.3 + 0.90000004 * jax.random.uniform(keys[2], (NXE, NYE, NZE), jnp.float32) ** block_scale(keys[2], (NXE, NYE, NZE), ((0, 32), (1, 16)), -0.2, 0.2), 0.3, 1.2)
    orient = touch_ends((jax.random.randint(keys[3], (3, NXE, NYE, NZE), 0, 2) < 1).astype(jnp.int32), jax.random.fold_in(keys[3], 1), 0, 1)
    smoother = draw_smoother(jax.random.fold_in(keys[6], 71), 0)
    coarse_smoother = draw_coarse_smoother(jax.random.fold_in(keys[6], 71), 0)
    return dict(source=source, jacobian=jacobian, damping=damping, orient=orient, smoother=smoother, coarse_smoother=coarse_smoother)


SIGMA_SHIFT = 2.0
OMEGA_DAMP = 0.8

def lobatto(node_count):
    if node_count == 2:
        node_points = np.array([-1.0, 1.0])
    else:
        node_points = np.array([-1.0, -1.0 / math.sqrt(5.0), 1.0 / math.sqrt(5.0), 1.0])
    weights = np.ones(node_count)
    for row_index in range(node_count):
        for col_index in range(node_count):
            if row_index != col_index:
                weights[row_index] = weights[row_index] / (node_points[row_index] - node_points[col_index])
    slopes = np.zeros((node_count, node_count))
    for row_index in range(node_count):
        for col_index in range(node_count):
            if row_index != col_index:
                slopes[row_index, col_index] = weights[col_index] / weights[row_index] / (node_points[row_index] - node_points[col_index])
        slopes[row_index, row_index] = -np.sum(slopes[row_index])
    return (node_points, slopes)

def interp_table():
    node_points = lobatto(4)[0]
    return np.stack([(1.0 - node_points) / 2.0, (1.0 + node_points) / 2.0], 1)

def apply_along(grid_field, matrix, node_axis):
    pieces = [jnp.take(grid_field, column, axis=node_axis) for column in range(matrix.shape[1])]
    outputs = []
    for target in range(matrix.shape[0]):
        running = float(matrix[target, 0]) * pieces[0]
        for column in range(1, matrix.shape[1]):
            running = running + float(matrix[target, column]) * pieces[column]
        outputs.append(running)
    return jnp.stack(outputs, axis=node_axis)

def mix_vars(matrix, grid_field):
    parts_out = []
    for out_var in range(5):
        running = None
        for in_var in range(5):
            weight_now = matrix[out_var, in_var].astype(jnp.float32)
            weight_now = weight_now.reshape((1,) * (grid_field.ndim - 1 - weight_now.ndim) + weight_now.shape)
            product_term = weight_now * grid_field[in_var]
            running = product_term if in_var == 0 else running + product_term
        parts_out.append(running)
    return jnp.stack(parts_out)

def face_slot(direction, node_index):
    return (slice(None),) * (direction + 1) + (node_index,)

def operator_apply(grid_field, jacobian, damping, orient, fetch):
    node_count = grid_field.shape[1]
    slope_table = lobatto(node_count)[1]
    lift_scale = node_count * (node_count - 1) / 2.0
    result_sum = SIGMA_SHIFT * grid_field
    for direction in range(3):
        flux_term = mix_vars(jacobian[direction], grid_field)
        result_sum = result_sum + apply_along(flux_term, slope_table, direction + 1)
        low_trace = jnp.take(grid_field, 0, axis=direction + 1)
        high_trace = jnp.take(grid_field, node_count - 1, axis=direction + 1)
        turned_flag = orient[direction] == 1
        high_turned = jnp.where(turned_flag, jnp.flip(high_trace, 1), high_trace)
        left_in, right_in = fetch(direction, low_trace, high_turned)
        right_in = jnp.where(turned_flag, jnp.flip(right_in, 1), right_in)
        jump_right = right_in - high_trace
        jump_left = left_in - low_trace
        upper_term = 0.5 * lift_scale * (mix_vars(jacobian[direction], jump_right) - damping * jump_right)
        lower_term = -0.5 * lift_scale * (mix_vars(jacobian[direction], jump_left) + damping * jump_left)
        result_sum = result_sum.at[face_slot(direction, node_count - 1)].add(upper_term)
        result_sum = result_sum.at[face_slot(direction, 0)].add(lower_term)
    return result_sum

def roll_fetch(direction, low_trace, high_turned):
    elem_axis = 3 + direction
    return (jnp.roll(high_turned, 1, axis=elem_axis), jnp.roll(low_trace, -1, axis=elem_axis))

def restrict(grid_field):
    interp = interp_table().T
    for node_axis in (1, 2, 3):
        grid_field = apply_along(grid_field, interp, node_axis)
    return grid_field

def prolong(grid_field):
    interp = interp_table()
    for node_axis in (1, 2, 3):
        grid_field = apply_along(grid_field, interp, node_axis)
    return grid_field

def coarse_solve(coarse_rhs, jacobian, damping, orient, inverse, fetch):
    coarse = OMEGA_DAMP * mix_vars(inverse, coarse_rhs)
    for sweep_index in range(CSWEEPS - 1):
        update = coarse_rhs - operator_apply(coarse, jacobian, damping, orient, fetch)
        coarse = coarse + OMEGA_DAMP * mix_vars(inverse, update)
    return coarse

def reference(source, jacobian, damping, orient, smoother, coarse_smoother):
    first_pass = OMEGA_DAMP * mix_vars(smoother, source)
    update = source - operator_apply(first_pass, jacobian, damping, orient, roll_fetch)
    second = first_pass + OMEGA_DAMP * mix_vars(smoother, update)
    residual = source - operator_apply(second, jacobian, damping, orient, roll_fetch)
    coarse_rhs = restrict(residual)
    coarse = coarse_solve(coarse_rhs, jacobian, damping, orient, coarse_smoother, roll_fetch)
    return second + prolong(coarse)
```

```python
import functools
import math

import jax
import jax.numpy as jnp
import numpy as np
from jax import lax
from jax.experimental import pallas as pl
from jax.experimental.pallas import tpu as pltpu
from jax.sharding import PartitionSpec as P

MESH = pl.DeviceIdType.MESH
OMEGA = 0.8
SHIFT = 2.0
F32 = jnp.float32


def lobatto4():
    points = np.array([-1.0, -1.0 / math.sqrt(5.0), 1.0 / math.sqrt(5.0), 1.0])
    weights = np.ones(4)
    for row in range(4):
        for col in range(4):
            if row != col:
                weights[row] /= points[row] - points[col]
    slopes = np.zeros((4, 4))
    for row in range(4):
        for col in range(4):
            if row != col:
                slopes[row, col] = weights[col] / weights[row] / (points[row] - points[col])
        slopes[row, row] = -np.sum(slopes[row])
    return points, slopes


POINTS, SLOPES = lobatto4()
INTERP = np.stack([(1.0 - POINTS) / 2.0, (1.0 + POINTS) / 2.0], 1)
OPEN = SLOPES.copy()
OPEN[0, 0] = OPEN[3, 3] = OPEN[1, 1] = OPEN[2, 2] = 0.0
LIFT = 3.0
EDGE = INTERP.T @ OPEN
P_NEAR, P_FAR = float(INTERP[1, 0]), float(INTERP[2, 0])


def dot_terms(coefs, values):
    total = None
    for coef, value in zip(coefs, values):
        coef = float(coef)
        if coef == 0.0:
            continue
        term = value if coef == 1.0 else coef * value
        total = term if total is None else total + term
    return total


def rows():
    return lax.broadcasted_iota(jnp.int32, (8, 128), 0)


def halves(top, bottom):
    return jnp.where(rows() < 4, jnp.full((8, 128), float(top), F32), jnp.full((8, 128), float(bottom), F32))


def sub_roll(value, shift):
    return pltpu.roll(value, shift % 8, 0)


def lane_roll(value, shift):
    return pltpu.roll(value, shift % 128, 1)


def pack_low(first, second, mask, step):
    return jnp.where(mask, first, sub_roll(second, step))


def pack_high(first, second, mask, step):
    return jnp.where(mask, sub_roll(first, -step), second)


def z_ghosts(traces, turned):
    count = len(traces)
    low = rows() < 4
    flip = jnp.logical_and(turned, rows() >= 4)
    out = []
    for a in range(count):
        swapped = sub_roll(jnp.where(flip, traces[count - 1 - a], traces[a]), 4)
        out.append(jnp.where(low, lane_roll(swapped, 1), lane_roll(swapped, -1)))
    return [jnp.where(flip, out[count - 1 - a], out[a]) for a in range(count)]


def restrict_c(first, second):
    low = rows() < 4
    ends = jnp.where(low, first, second)
    inner_swapped = jnp.where(low, second, first)
    inner = sub_roll(inner_swapped, 4)
    return ends, inner, inner_swapped, ends + P_NEAR * inner + P_FAR * inner_swapped


def restrict_line(values):
    low = values[0] + P_NEAR * values[1] + P_FAR * values[2]
    high = values[3] + P_NEAR * values[2] + P_FAR * values[1]
    return [low, high]


def prolong_line(values):
    return [
        values[0],
        P_NEAR * values[0] + P_FAR * values[1],
        P_FAR * values[0] + P_NEAR * values[1],
        values[1],
    ]


def kernel(
    src_hbm, jac_hbm, damp_hbm, flag_hbm, smo_hbm, csm_hbm, out_hbm,
    src, smo, csm, jraw, jn, draw, fraw, flags, dmp, kfine, csf,
    q, acc, wx, wy, wz, rsrc, rcs, ctr, wc, cfield, crhs,
    s1, r1, s2, r2, in_sem, out_sem, send_sem, recv_sem,
):
    nx, ny = lax.axis_size("gx"), lax.axis_size("gy")
    ix, iy = lax.axis_index("gx"), lax.axis_index("gy")
    x_next, x_prev = lax.rem(ix + 1, nx), lax.rem(ix + nx - 1, nx)
    y_next, y_prev = lax.rem(iy + 1, ny), lax.rem(iy + ny - 1, ny)
    partners = [(x_prev, iy), (x_next, iy), (ix, y_prev), (ix, y_next)]

    loads = []

    def load(source, target):
        copy = pltpu.make_async_copy(source, target, in_sem.at[len(loads)])
        copy.start()
        loads.append(copy)
        return copy

    parts = {}
    for a in (0, 3):
        parts[a] = (load(src_hbm.at[:, a], src.at[:, a]), load(smo_hbm.at[:, a], smo.at[:, a]))
    flag_load = load(flag_hbm, fraw)
    damp_load = load(damp_hbm, draw)
    jac_load = load(jac_hbm, jraw)
    for a in (1, 2):
        parts[a] = (load(src_hbm.at[:, a], src.at[:, a]), load(smo_hbm.at[:, a], smo.at[:, a]))
    csm_load = load(csm_hbm, csm)

    barrier = pltpu.get_barrier_semaphore()
    for partner in partners:
        pl.semaphore_signal(barrier, inc=1, device_id=partner, device_id_type=MESH)

    def remote(source, target, number, partner):
        return pltpu.make_async_remote_copy(
            src_ref=source, dst_ref=target, send_sem=send_sem.at[number], recv_sem=recv_sem.at[number],
            device_id=partner, device_id_type=MESH,
        )

    sends1 = [remote(s1.at[k], r1.at[k], k, partners[k]) for k in range(4)]
    sends2 = [[remote(s2.at[r, k], r2.at[r, k], 4 + 4 * r + k, partners[k]) for k in range(4)] for r in range(3)]

    low = rows() < 4
    x0 = (rows() & 2) == 0
    y0 = (rows() & 1) == 0

    def turned(direction):
        return flags[direction] == 1

    def smooth(a, b, fields):
        outs = []
        for vo in range(5):
            pair = [None, None]
            for vi in range(5):
                block = smo[5 * vo + vi, a, b].astype(F32)
                for half in range(2):
                    term = block[8 * half : 8 * half + 8] * fields[vi][half]
                    pair[half] = term if vi == 0 else pair[half] + term
            outs.append(pair)
        return outs

    def first_pass(a, b):
        fields = [[src[v, a, b, 0], src[v, a, b, 1]] for v in range(5)]
        outs = smooth(a, b, fields)
        for v in range(5):
            q[v, a, b, 0] = outs[v][0]
            q[v, a, b, 1] = outs[v][1]

    for a in (0, 3):
        for copy in parts[a]:
            copy.wait()

        @pl.loop(0, 4)
        def _(b, a=a):
            first_pass(a, b)

    flag_load.wait()
    damp_load.wait()
    for d in range(3):
        flags[d] = jnp.concatenate([fraw[d], fraw[d]], axis=0)
    damping = jnp.concatenate([draw[...], draw[...]], axis=0)
    dmp[0] = (OMEGA * LIFT) * damping
    dmp[1] = (OMEGA * 0.5) * damping
    dmp[2] = OMEGA * SHIFT + (OMEGA * 1.5) * damping
    dmp[3] = jnp.where(low, (OMEGA * LIFT) * damping, 0.0)
    dmp[4] = jnp.where(low, 0.0, (OMEGA * LIFT) * damping)
    for b in range(4):
        for a_end in range(2):
            faces = a_end + (1 if b in (0, 3) else 0)
            base = OMEGA * SHIFT + (OMEGA * LIFT * faces) * damping
            kfine[b, a_end, 0] = base + dmp[3]
            kfine[b, a_end, 1] = base + dmp[4]

    fx, fy, fz = turned(0), turned(1), turned(2)

    @pl.loop(0, 5)
    def _(v):
        for b in range(4):
            s1[0, v, b] = pack_low(q[v, 0, b, 0], q[v, 0, b, 1], x0, 2)
            hi = [jnp.where(fx, q[v, 3, 3 - b, h], q[v, 3, b, h]) for h in range(2)]
            s1[1, v, b] = pack_high(hi[0], hi[1], x0, 2)

    pl.semaphore_wait(barrier, 4)
    sends1[0].start()
    sends1[1].start()

    for a in (1, 2):
        for copy in parts[a]:
            copy.wait()

        @pl.loop(0, 4)
        def _(b, a=a):
            first_pass(a, b)

    @pl.loop(0, 5)
    def _(v):
        for a in range(4):
            s1[2, v, a] = pack_low(q[v, a, 0, 0], q[v, a, 0, 1], y0, 1)
            hi = [jnp.where(fy, q[v, 3 - a, 3, h], q[v, a, 3, h]) for h in range(2)]
            s1[3, v, a] = pack_high(hi[0], hi[1], y0, 1)

    sends1[2].start()
    sends1[3].start()

    jac_load.wait()

    @pl.loop(0, 75)
    def _(i):
        block = jraw[i]
        jn[i] = (-OMEGA) * jnp.concatenate([block, block], axis=0)

    csm_load.wait()

    @pl.loop(0, 25)
    def _(i):
        for n in range(2):
            block = csm[i, n].astype(F32)
            csf[i, n, 0] = block[:8]
            csf[i, n, 1] = block[8:]

    c_first = [halves(OPEN[0, 1], OPEN[1, 0]), halves(OPEN[0, 2], OPEN[1, 3]), halves(OPEN[0, 3], OPEN[1, 2])]
    c_second = [halves(OPEN[2, 3], OPEN[3, 2]), halves(OPEN[2, 0], OPEN[3, 1]), halves(OPEN[2, 1], OPEN[3, 0])]
    c_ghost = [halves(-LIFT, 0.0), halves(0.0, LIFT)]

    @pl.loop(0, 20)
    def _(t):
        v, b = t // 4, t % 4
        first = [q[v, a, b, 0] for a in range(4)]
        second = [q[v, a, b, 1] for a in range(4)]
        for a in range(4):
            for h, line in enumerate((first, second)):
                wx[v, a, b, h] = dot_terms(OPEN[a], line)
        ghosts = z_ghosts([jnp.where(low, first[a], second[a]) for a in range(4)], fz)
        for a in range(4):
            a_end = 1 if a in (0, 3) else 0
            first_sw, second_sw = sub_roll(first[a], 4), sub_roll(second[a], 4)
            wz[v, a, b, 0] = (
                c_first[0] * first_sw + c_first[1] * second[a] + c_first[2] * second_sw + c_ghost[0] * ghosts[a]
            )
            wz[v, a, b, 1] = (
                c_second[0] * second_sw + c_second[1] * first[a] + c_second[2] * first_sw + c_ghost[1] * ghosts[a]
            )
            acc[v, a, b, 0] = src[v, a, b, 0] - kfine[b, a_end, 0] * first[a] + dmp[3] * ghosts[a]
            acc[v, a, b, 1] = src[v, a, b, 1] - kfine[b, a_end, 1] * second[a] + dmp[4] * ghosts[a]

    @pl.loop(0, 20)
    def _(t):
        v, a = t // 4, t % 4
        for h in range(2):
            line = [q[v, a, b, h] for b in range(4)]
            for b in range(4):
                wy[v, a, b, h] = dot_terms(OPEN[b], line)

    @pl.loop(0, 5)
    def _(v):
        by_a = []
        for a in range(4):
            by_a.append(restrict_line([restrict_c(src[v, a, b, 0], src[v, a, b, 1])[3] for b in range(4)]))
        for j in range(2):
            for i, value in enumerate(restrict_line([by_a[a][j] for a in range(4)])):
                rsrc[v, i, j] = value

    lift_damp = dmp[0]

    sends1[2].wait_recv()
    sends1[3].wait_recv()

    @pl.loop(0, 5)
    def _(v):
        for h in range(2):
            lo = [q[v, a, 0, h] for a in range(4)]
            hi = [q[v, a, 3, h] for a in range(4)]
            right = []
            for a in range(4):
                packed = r1[2, v, a]
                right.append(jnp.where(y0, sub_roll(lo[a], -1), sub_roll(packed, 1) if h == 0 else packed))
            for a in range(4):
                packed = r1[3, v, a]
                hi_turned = jnp.where(fy, hi[3 - a], hi[a])
                left = jnp.where(y0, packed if h == 0 else sub_roll(packed, -1), sub_roll(hi_turned, 1))
                ghost = jnp.where(fy, right[3 - a], right[a])
                wy[v, a, 0, h] = wy[v, a, 0, h] - LIFT * left
                wy[v, a, 3, h] = wy[v, a, 3, h] + LIFT * ghost
                acc[v, a, 0, h] = acc[v, a, 0, h] + lift_damp * left
                acc[v, a, 3, h] = acc[v, a, 3, h] + lift_damp * ghost

    sends1[0].wait_recv()
    sends1[1].wait_recv()

    @pl.loop(0, 5)
    def _(v):
        for h in range(2):
            lo = [q[v, 0, b, h] for b in range(4)]
            hi = [q[v, 3, b, h] for b in range(4)]
            right = []
            for b in range(4):
                packed = r1[0, v, b]
                right.append(jnp.where(x0, sub_roll(lo[b], -2), sub_roll(packed, 2) if h == 0 else packed))
            for b in range(4):
                packed = r1[1, v, b]
                hi_turned = jnp.where(fx, hi[3 - b], hi[b])
                left = jnp.where(x0, packed if h == 0 else sub_roll(packed, -2), sub_roll(hi_turned, 2))
                ghost = jnp.where(fx, right[3 - b], right[b])
                wx[v, 0, b, h] = wx[v, 0, b, h] - LIFT * left
                wx[v, 3, b, h] = wx[v, 3, b, h] + LIFT * ghost
                acc[v, 0, b, h] = acc[v, 0, b, h] + lift_damp * left
                acc[v, 3, b, h] = acc[v, 3, b, h] + lift_damp * ghost

    @pl.loop(0, 8)
    def _(t):
        half, b = t // 4, t % 4
        pair = [half, 3 - half]
        total = [[[acc[v, a, b, h] for h in range(2)] for a in pair] for v in range(5)]
        for d, w in enumerate((wx, wy, wz)):
            for vi in range(5):
                flux = [[w[vi, a, b, h] for h in range(2)] for a in pair]
                for vo in range(5):
                    weight = jn[25 * d + 5 * vo + vi]
                    for n in range(2):
                        for h in range(2):
                            total[vo][n][h] = total[vo][n][h] + weight * flux[n][h]
        for n, a in enumerate(pair):
            outs = smooth(a, b, [total[v][n] for v in range(5)])
            for v in range(5):
                for h in range(2):
                    q[v, a, b, h] = q[v, a, b, h] + outs[v][h]

    def send_coarse(level):
        @pl.loop(0, 5)
        def _(v):
            s2[level, 0, v] = pack_low(ctr[0, v, 0], ctr[0, v, 1], x0, 2)
            hi = [jnp.where(fx, ctr[1, v, 1 - j], ctr[1, v, j]) for j in range(2)]
            s2[level, 1, v] = pack_high(hi[0], hi[1], x0, 2)
            s2[level, 2, v] = pack_low(ctr[2, v, 0], ctr[2, v, 1], y0, 1)
            hi = [jnp.where(fy, ctr[3, v, 1 - i], ctr[3, v, i]) for i in range(2)]
            s2[level, 3, v] = pack_high(hi[0], hi[1], y0, 1)

        for copy in sends2[level]:
            copy.start()

    def coarse_ghosts(level, v, slot, mask, step, flip):
        lo = [ctr[slot, v, n] for n in range(2)]
        hi = [ctr[slot + 1, v, n] for n in range(2)]
        packed_lo, packed_hi = r2[level, slot, v], r2[level, slot + 1, v]
        right = [
            jnp.where(mask, sub_roll(lo[0], -step), sub_roll(packed_lo, step)),
            jnp.where(mask, sub_roll(lo[1], -step), packed_lo),
        ]
        right = [jnp.where(flip, right[1 - n], right[n]) for n in range(2)]
        hi = [jnp.where(flip, hi[1 - n], hi[n]) for n in range(2)]
        left = [
            jnp.where(mask, packed_hi, sub_roll(hi[0], step)),
            jnp.where(mask, sub_roll(packed_hi, -step), sub_roll(hi[1], step)),
        ]
        return left, right

    def coarse_mix():
        total = [[[crhs[1, v, i, j] for j in range(2)] for i in range(2)] for v in range(5)]
        for d in range(3):
            for vi in range(5):
                flux = [[wc[d, vi, i, j] for j in range(2)] for i in range(2)]
                for vo in range(5):
                    weight = jn[25 * d + 5 * vo + vi]
                    for i in range(2):
                        for j in range(2):
                            total[vo][i][j] = total[vo][i][j] + weight * flux[i][j]
        return total

    def coarse_smooth(total):
        outs = [[[None, None] for _ in range(2)] for _ in range(5)]
        for vo in range(5):
            for vi in range(5):
                for i in range(2):
                    for j in range(2):
                        term = csf[5 * vo + vi, i, j] * total[vi][i][j]
                        outs[vo][i][j] = term if vi == 0 else outs[vo][i][j] + term
        return outs

    @pl.loop(0, 5)
    def _(v):
        rc = [[restrict_c(q[v, a, b, 0], q[v, a, b, 1])[3] for b in range(4)] for a in range(4)]
        rbc = [restrict_line(rc[a]) for a in range(4)]
        rac = [restrict_line([rc[a][b] for a in range(4)]) for b in range(4)]
        for n in range(2):
            ctr[0, v, n] = rbc[0][n]
            ctr[1, v, n] = rbc[3][n]
            ctr[2, v, n] = rac[0][n]
            ctr[3, v, n] = rac[3][n]
        for i in range(2):
            for j in range(2):
                wc[0, v, i, j] = dot_terms(EDGE[i], [rbc[a][j] for a in range(4)])
                wc[1, v, i, j] = dot_terms(EDGE[j], [rac[b][i] for b in range(4)])

    send_coarse(0)

    e_ends = halves(EDGE[0, 0], EDGE[1, 3])
    e_ends_sw = halves(EDGE[0, 3], EDGE[1, 0])
    e_inner = halves(EDGE[0, 1], EDGE[1, 2])
    e_inner_sw = halves(EDGE[0, 2], EDGE[1, 1])
    z_lift = halves(-LIFT, LIFT)

    @pl.loop(0, 5)
    def _(v):
        ra = [[restrict_line([q[v, a, b, h] for a in range(4)]) for b in range(4)] for h in range(2)]
        traces = [[None, None], [None, None]]
        for i in range(2):
            first = restrict_line([ra[0][b][i] for b in range(4)])
            second = restrict_line([ra[1][b][i] for b in range(4)])
            for j in range(2):
                ends, inner, inner_sw, full = restrict_c(first[j], second[j])
                traces[j][i] = ends
                wc[2, v, i, j] = (
                    e_ends * ends + e_ends_sw * sub_roll(ends, 4) + e_inner * inner + e_inner_sw * inner_sw
                )
                crhs[1, v, i, j] = rsrc[v, i, j] - (OMEGA * SHIFT) * full
        for j in range(2):
            ghosts = z_ghosts(traces[j], fz)
            for i in range(2):
                wc[2, v, i, j] = wc[2, v, i, j] + z_lift * ghosts[i]
                crhs[1, v, i, j] = crhs[1, v, i, j] + lift_damp * (ghosts[i] - traces[j][i])

    for copy in sends2[0]:
        copy.wait_recv()

    @pl.loop(0, 5)
    def _(v):
        left, right = coarse_ghosts(0, v, 0, x0, 2, fx)
        for j in range(2):
            wc[0, v, 0, j] = wc[0, v, 0, j] - LIFT * left[j]
            wc[0, v, 1, j] = wc[0, v, 1, j] + LIFT * right[j]
            crhs[1, v, 0, j] = crhs[1, v, 0, j] + lift_damp * (left[j] - ctr[0, v, j])
            crhs[1, v, 1, j] = crhs[1, v, 1, j] + lift_damp * (right[j] - ctr[1, v, j])
        left, right = coarse_ghosts(0, v, 2, y0, 1, fy)
        for i in range(2):
            wc[1, v, i, 0] = wc[1, v, i, 0] - LIFT * left[i]
            wc[1, v, i, 1] = wc[1, v, i, 1] + LIFT * right[i]
            crhs[1, v, i, 0] = crhs[1, v, i, 0] + lift_damp * (left[i] - ctr[2, v, i])
            crhs[1, v, i, 1] = crhs[1, v, i, 1] + lift_damp * (right[i] - ctr[3, v, i])

    total = coarse_mix()
    for v in range(5):
        for i in range(2):
            for j in range(2):
                crhs[0, v, i, j] = total[v][i][j]
    outs = coarse_smooth(total)
    for v in range(5):
        for i in range(2):
            for j in range(2):
                cfield[v, i, j] = outs[v][i][j]

    half_damp, k_coarse = dmp[1], dmp[2]

    for level in (1, 2):
        @pl.loop(0, 5)
        def _(v):
            for n in range(2):
                ctr[0, v, n] = cfield[v, 0, n]
                ctr[1, v, n] = cfield[v, 1, n]
                ctr[2, v, n] = cfield[v, n, 0]
                ctr[3, v, n] = cfield[v, n, 1]

        send_coarse(level)

        @pl.loop(0, 5)
        def _(v):
            for j in range(2):
                field = [cfield[v, i, j] for i in range(2)]
                ghosts = z_ghosts(field, fz)
                for i in range(2):
                    swapped = sub_roll(field[i], 4)
                    wc[2, v, i, j] = jnp.where(low, 0.5, -0.5) * (swapped - ghosts[i])
                    crhs[1, v, i, j] = crhs[0, v, i, j] - k_coarse * field[i] + half_damp * ghosts[i]

        for copy in sends2[level]:
            copy.wait_recv()

        @pl.loop(0, 5)
        def _(v):
            left, right = coarse_ghosts(level, v, 0, x0, 2, fx)
            for j in range(2):
                wc[0, v, 0, j] = 0.5 * (cfield[v, 1, j] - left[j])
                wc[0, v, 1, j] = 0.5 * (right[j] - cfield[v, 0, j])
                crhs[1, v, 0, j] = crhs[1, v, 0, j] + half_damp * left[j]
                crhs[1, v, 1, j] = crhs[1, v, 1, j] + half_damp * right[j]
            left, right = coarse_ghosts(level, v, 2, y0, 1, fy)
            for i in range(2):
                wc[1, v, i, 0] = 0.5 * (cfield[v, i, 1] - left[i])
                wc[1, v, i, 1] = 0.5 * (right[i] - cfield[v, i, 0])
                crhs[1, v, i, 0] = crhs[1, v, i, 0] + half_damp * left[i]
                crhs[1, v, i, 1] = crhs[1, v, i, 1] + half_damp * right[i]

        outs = coarse_smooth(coarse_mix())
        for v in range(5):
            for i in range(2):
                for j in range(2):
                    cfield[v, i, j] = cfield[v, i, j] + outs[v][i][j]

    t_first = [halves(OMEGA, OMEGA * P_FAR), halves(0.0, OMEGA * P_NEAR)]
    t_second = [halves(OMEGA * P_FAR, OMEGA), halves(OMEGA * P_NEAR, 0.0)]

    @pl.loop(0, 5)
    def _(v):
        by_a = [prolong_line([cfield[v, i, j] for i in range(2)]) for j in range(2)]
        for a in range(4):
            for b, value in enumerate(prolong_line([by_a[j][a] for j in range(2)])):
                swapped = sub_roll(value, 4)
                wx[v, a, b, 0] = OMEGA * q[v, a, b, 0] + (t_first[0] * value + t_first[1] * swapped)
                wx[v, a, b, 1] = OMEGA * q[v, a, b, 1] + (t_second[0] * value + t_second[1] * swapped)

    store = pltpu.make_async_copy(wx, out_hbm, out_sem)
    store.start()
    for copy in sends1:
        copy.wait_send()
    for level in sends2:
        for copy in level:
            copy.wait_send()
    store.wait()


def body(source, jacobian, damping, orient, smoother, coarse_smoother):
    field = (5, 4, 4, 2, 8, 128)
    any_space = pl.BlockSpec(memory_space=pl.ANY)
    vmem = pltpu.VMEM
    out = pl.pallas_call(
        kernel,
        out_shape=jax.ShapeDtypeStruct(field, F32),
        in_specs=[any_space] * 6,
        out_specs=any_space,
        scratch_shapes=[
            vmem(field, F32),
            vmem((25, 4, 4, 16, 128), jnp.bfloat16),
            vmem((25, 2, 16, 128), jnp.bfloat16),
            vmem((75, 4, 128), F32),
            vmem((75, 8, 128), F32),
            vmem((4, 128), F32),
            vmem((3, 4, 128), jnp.int32),
            vmem((3, 8, 128), jnp.int32),
            vmem((5, 8, 128), F32),
            vmem((4, 2, 2, 8, 128), F32),
            vmem((25, 2, 2, 8, 128), F32),
            vmem(field, F32),
            vmem(field, F32),
            vmem(field, F32),
            vmem(field, F32),
            vmem(field, F32),
            vmem((5, 2, 2, 8, 128), F32),
            vmem((8, 128), F32),
            vmem((4, 5, 2, 8, 128), F32),
            vmem((3, 5, 2, 2, 8, 128), F32),
            vmem((5, 2, 2, 8, 128), F32),
            vmem((2, 5, 2, 2, 8, 128), F32),
            vmem((4, 5, 4, 8, 128), F32),
            vmem((4, 5, 4, 8, 128), F32),
            vmem((3, 4, 5, 8, 128), F32),
            vmem((3, 4, 5, 8, 128), F32),
            pltpu.SemaphoreType.DMA((12,)),
            pltpu.SemaphoreType.DMA,
            pltpu.SemaphoreType.DMA((16,)),
            pltpu.SemaphoreType.DMA((16,)),
        ],
        compiler_params=pltpu.CompilerParams(
            collective_id=0, has_side_effects=True, vmem_limit_bytes=40 * 1024 * 1024
        ),
    )(
        source.reshape(field),
        jacobian.reshape(75, 4, 128),
        damping.reshape(4, 128),
        orient.reshape(3, 4, 128),
        smoother.reshape(25, 4, 4, 16, 128),
        coarse_smoother.reshape(25, 2, 16, 128),
    )
    return out.reshape(5, 4, 4, 4, 2, 2, 128)


def solution(mesh):
    in_specs = (
        P(None, None, None, None, "gx", "gy", None),
        P(None, None, None, "gx", "gy", None),
        P("gx", "gy", None),
        P(None, "gx", "gy", None),
        P(None, None, None, None, None, "gx", "gy", None),
        P(None, None, None, None, None, "gx", "gy", None),
    )
    out_specs = P(None, None, None, None, "gx", "gy", None)
    return jax.shard_map(body, mesh=mesh, in_specs=in_specs, out_specs=out_specs, check_vma=False)
```

```python
import functools
import math

import jax
import jax.numpy as jnp
import numpy as np
from jax import lax
from jax.experimental import pallas as pl
from jax.experimental.pallas import tpu as pltpu
from jax.sharding import PartitionSpec as P

MESH = pl.DeviceIdType.MESH
OMEGA = 0.8
SHIFT = 2.0
F32 = jnp.float32


def lobatto4():
    points = np.array([-1.0, -1.0 / math.sqrt(5.0), 1.0 / math.sqrt(5.0), 1.0])
    weights = np.ones(4)
    for row in range(4):
        for col in range(4):
            if row != col:
                weights[row] /= points[row] - points[col]
    slopes = np.zeros((4, 4))
    for row in range(4):
        for col in range(4):
            if row != col:
                slopes[row, col] = weights[col] / weights[row] / (points[row] - points[col])
        slopes[row, row] = -np.sum(slopes[row])
    return points, slopes


POINTS, SLOPES = lobatto4()
INTERP = np.stack([(1.0 - POINTS) / 2.0, (1.0 + POINTS) / 2.0], 1)
OPEN = SLOPES.copy()
OPEN[0, 0] = OPEN[3, 3] = OPEN[1, 1] = OPEN[2, 2] = 0.0
LIFT = 3.0
EDGE = INTERP.T @ OPEN
P_NEAR, P_FAR = float(INTERP[1, 0]), float(INTERP[2, 0])


def dot_terms(coefs, values):
    total = None
    for coef, value in zip(coefs, values):
        coef = float(coef)
        if coef == 0.0:
            continue
        term = value if coef == 1.0 else coef * value
        total = term if total is None else total + term
    return total


def rows():
    return lax.broadcasted_iota(jnp.int32, (8, 128), 0)


def halves(top, bottom):
    return jnp.where(rows() < 4, jnp.full((8, 128), float(top), F32), jnp.full((8, 128), float(bottom), F32))


def sub_roll(value, shift):
    return pltpu.roll(value, shift % 8, 0)


def lane_roll(value, shift):
    return pltpu.roll(value, shift % 128, 1)


def pack_low(first, second, mask, step):
    return jnp.where(mask, first, sub_roll(second, step))


def pack_high(first, second, mask, step):
    return jnp.where(mask, sub_roll(first, -step), second)


def z_ghosts(traces, turned):
    count = len(traces)
    low = rows() < 4
    flip = jnp.logical_and(turned, rows() >= 4)
    out = []
    for a in range(count):
        swapped = sub_roll(jnp.where(flip, traces[count - 1 - a], traces[a]), 4)
        out.append(jnp.where(low, lane_roll(swapped, 1), lane_roll(swapped, -1)))
    return [jnp.where(flip, out[count - 1 - a], out[a]) for a in range(count)]


def restrict_c(first, second):
    low = rows() < 4
    ends = jnp.where(low, first, second)
    inner_swapped = jnp.where(low, second, first)
    inner = sub_roll(inner_swapped, 4)
    return ends, inner, inner_swapped, ends + P_NEAR * inner + P_FAR * inner_swapped


def restrict_line(values):
    low = values[0] + P_NEAR * values[1] + P_FAR * values[2]
    high = values[3] + P_NEAR * values[2] + P_FAR * values[1]
    return [low, high]


def prolong_line(values):
    return [
        values[0],
        P_NEAR * values[0] + P_FAR * values[1],
        P_FAR * values[0] + P_NEAR * values[1],
        values[1],
    ]


def kernel(
    src_hbm, jac_hbm, damp_hbm, flag_hbm, smo_hbm, csm_hbm, out_hbm,
    src, smo, csm, jraw, jn, draw, fraw, flags, dmp, kfine, csf,
    q, acc, wx, wy, wz, rsrc, rcs, ctr, wc, cfield, crhs,
    s1, r1, s2, r2, in_sem, out_sem, send_sem, recv_sem,
):
    nx, ny = lax.axis_size("gx"), lax.axis_size("gy")
    ix, iy = lax.axis_index("gx"), lax.axis_index("gy")
    x_next, x_prev = lax.rem(ix + 1, nx), lax.rem(ix + nx - 1, nx)
    y_next, y_prev = lax.rem(iy + 1, ny), lax.rem(iy + ny - 1, ny)
    partners = [(x_prev, iy), (x_next, iy), (ix, y_prev), (ix, y_next)]

    loads = []

    def load(source, target):
        copy = pltpu.make_async_copy(source, target, in_sem.at[len(loads)])
        copy.start()
        loads.append(copy)
        return copy

    parts = {}
    for a in (0, 3):
        parts[a] = (load(src_hbm.at[:, a], src.at[:, a]), load(smo_hbm.at[:, a], smo.at[:, a]))
    flag_load = load(flag_hbm, fraw)
    damp_load = load(damp_hbm, draw)
    jac_load = load(jac_hbm, jraw)
    for a in (1, 2):
        parts[a] = (load(src_hbm.at[:, a], src.at[:, a]), load(smo_hbm.at[:, a], smo.at[:, a]))
    csm_load = load(csm_hbm, csm)

    barrier = pltpu.get_barrier_semaphore()
    for partner in partners:
        pl.semaphore_signal(barrier, inc=1, device_id=partner, device_id_type=MESH)

    def remote(source, target, number, partner):
        return pltpu.make_async_remote_copy(
            src_ref=source, dst_ref=target, send_sem=send_sem.at[number], recv_sem=recv_sem.at[number],
            device_id=partner, device_id_type=MESH,
        )

    sends1 = [remote(s1.at[k], r1.at[k], k, partners[k]) for k in range(4)]
    sends2 = [[remote(s2.at[r, k], r2.at[r, k], 4 + 4 * r + k, partners[k]) for k in range(4)] for r in range(3)]

    low = rows() < 4
    x0 = (rows() & 2) == 0
    y0 = (rows() & 1) == 0

    def turned(direction):
        return flags[direction] == 1

    def smooth(a, b, fields):
        outs = []
        for vo in range(5):
            pair = [None, None]
            for vi in range(5):
                block = smo[5 * vo + vi, a, b].astype(F32)
                for half in range(2):
                    term = block[8 * half : 8 * half + 8] * fields[vi][half]
                    pair[half] = term if vi == 0 else pair[half] + term
            outs.append(pair)
        return outs

    def first_pass(a, b):
        fields = [[src[v, a, b, 0], src[v, a, b, 1]] for v in range(5)]
        outs = smooth(a, b, fields)
        for v in range(5):
            q[v, a, b, 0] = outs[v][0]
            q[v, a, b, 1] = outs[v][1]

    for a in (0, 3):
        for copy in parts[a]:
            copy.wait()

        @pl.loop(0, 4)
        def _(b, a=a):
            first_pass(a, b)

    flag_load.wait()
    damp_load.wait()
    for d in range(3):
        flags[d] = jnp.concatenate([fraw[d], fraw[d]], axis=0)
    damping = jnp.concatenate([draw[...], draw[...]], axis=0)
    dmp[0] = (OMEGA * LIFT) * damping
    dmp[1] = (OMEGA * 0.5) * damping
    dmp[2] = OMEGA * SHIFT + (OMEGA * 1.5) * damping
    dmp[3] = jnp.where(low, (OMEGA * LIFT) * damping, 0.0)
    dmp[4] = jnp.where(low, 0.0, (OMEGA * LIFT) * damping)
    for b in range(4):
        for a_end in range(2):
            faces = a_end + (1 if b in (0, 3) else 0)
            base = OMEGA * SHIFT + (OMEGA * LIFT * faces) * damping
            kfine[b, a_end, 0] = base + dmp[3]
            kfine[b, a_end, 1] = base + dmp[4]

    fx, fy, fz = turned(0), turned(1), turned(2)

    @pl.loop(0, 5)
    def _(v):
        for b in range(4):
            s1[0, v, b] = pack_low(q[v, 0, b, 0], q[v, 0, b, 1], x0, 2)
            hi = [jnp.where(fx, q[v, 3, 3 - b, h], q[v, 3, b, h]) for h in range(2)]
            s1[1, v, b] = pack_high(hi[0], hi[1], x0, 2)

    pl.semaphore_wait(barrier, 4)
    sends1[0].start()
    sends1[1].start()

    for a in (1, 2):
        for copy in parts[a]:
            copy.wait()

        @pl.loop(0, 4)
        def _(b, a=a):
            first_pass(a, b)

    @pl.loop(0, 5)
    def _(v):
        for a in range(4):
            s1[2, v, a] = pack_low(q[v, a, 0, 0], q[v, a, 0, 1], y0, 1)
            hi = [jnp.where(fy, q[v, 3 - a, 3, h], q[v, a, 3, h]) for h in range(2)]
            s1[3, v, a] = pack_high(hi[0], hi[1], y0, 1)

    sends1[2].start()
    sends1[3].start()

    jac_load.wait()

    @pl.loop(0, 75)
    def _(i):
        block = jraw[i]
        jn[i] = (-OMEGA) * jnp.concatenate([block, block], axis=0)

    csm_load.wait()

    @pl.loop(0, 25)
    def _(i):
        for n in range(2):
            block = csm[i, n].astype(F32)
            csf[i, n, 0] = block[:8]
            csf[i, n, 1] = block[8:]

    c_first = [halves(OPEN[0, 1], OPEN[1, 0]), halves(OPEN[0, 2], OPEN[1, 3]), halves(OPEN[0, 3], OPEN[1, 2])]
    c_second = [halves(OPEN[2, 3], OPEN[3, 2]), halves(OPEN[2, 0], OPEN[3, 1]), halves(OPEN[2, 1], OPEN[3, 0])]
    c_ghost = [halves(-LIFT, 0.0), halves(0.0, LIFT)]

    @pl.loop(0, 20)
    def _(t):
        v, b = t // 4, t % 4
        first = [q[v, a, b, 0] for a in range(4)]
        second = [q[v, a, b, 1] for a in range(4)]
        for a in range(4):
            for h, line in enumerate((first, second)):
                wx[v, a, b, h] = dot_terms(OPEN[a], line)
        ghosts = z_ghosts([jnp.where(low, first[a], second[a]) for a in range(4)], fz)
        for a in range(4):
            a_end = 1 if a in (0, 3) else 0
            first_sw, second_sw = sub_roll(first[a], 4), sub_roll(second[a], 4)
            wz[v, a, b, 0] = (
                c_first[0] * first_sw + c_first[1] * second[a] + c_first[2] * second_sw + c_ghost[0] * ghosts[a]
            )
            wz[v, a, b, 1] = (
                c_second[0] * second_sw + c_second[1] * first[a] + c_second[2] * first_sw + c_ghost[1] * ghosts[a]
            )
            acc[v, a, b, 0] = src[v, a, b, 0] - kfine[b, a_end, 0] * first[a] + dmp[3] * ghosts[a]
            acc[v, a, b, 1] = src[v, a, b, 1] - kfine[b, a_end, 1] * second[a] + dmp[4] * ghosts[a]

    @pl.loop(0, 20)
    def _(t):
        v, a = t // 4, t % 4
        for h in range(2):
            line = [q[v, a, b, h] for b in range(4)]
            for b in range(4):
                wy[v, a, b, h] = dot_terms(OPEN[b], line)

    @pl.loop(0, 5)
    def _(v):
        by_a = []
        for a in range(4):
            by_a.append(restrict_line([restrict_c(src[v, a, b, 0], src[v, a, b, 1])[3] for b in range(4)]))
        for j in range(2):
            for i, value in enumerate(restrict_line([by_a[a][j] for a in range(4)])):
                rsrc[v, i, j] = value

    lift_damp = dmp[0]

    sends1[2].wait_recv()
    sends1[3].wait_recv()

    @pl.loop(0, 5)
    def _(v):
        for h in range(2):
            lo = [q[v, a, 0, h] for a in range(4)]
            hi = [q[v, a, 3, h] for a in range(4)]
            right = []
            for a in range(4):
                packed = r1[2, v, a]
                right.append(jnp.where(y0, sub_roll(lo[a], -1), sub_roll(packed, 1) if h == 0 else packed))
            for a in range(4):
                packed = r1[3, v, a]
                hi_turned = jnp.where(fy, hi[3 - a], hi[a])
                left = jnp.where(y0, packed if h == 0 else sub_roll(packed, -1), sub_roll(hi_turned, 1))
                ghost = jnp.where(fy, right[3 - a], right[a])
                wy[v, a, 0, h] = wy[v, a, 0, h] - LIFT * left
                wy[v, a, 3, h] = wy[v, a, 3, h] + LIFT * ghost
                acc[v, a, 0, h] = acc[v, a, 0, h] + lift_damp * left
                acc[v, a, 3, h] = acc[v, a, 3, h] + lift_damp * ghost

    sends1[0].wait_recv()
    sends1[1].wait_recv()

    @pl.loop(0, 5)
    def _(v):
        for h in range(2):
            lo = [q[v, 0, b, h] for b in range(4)]
            hi = [q[v, 3, b, h] for b in range(4)]
            right = []
            for b in range(4):
                packed = r1[0, v, b]
                right.append(jnp.where(x0, sub_roll(lo[b], -2), sub_roll(packed, 2) if h == 0 else packed))
            for b in range(4):
                packed = r1[1, v, b]
                hi_turned = jnp.where(fx, hi[3 - b], hi[b])
                left = jnp.where(x0, packed if h == 0 else sub_roll(packed, -2), sub_roll(hi_turned, 2))
                ghost = jnp.where(fx, right[3 - b], right[b])
                wx[v, 0, b, h] = wx[v, 0, b, h] - LIFT * left
                wx[v, 3, b, h] = wx[v, 3, b, h] + LIFT * ghost
                acc[v, 0, b, h] = acc[v, 0, b, h] + lift_damp * left
                acc[v, 3, b, h] = acc[v, 3, b, h] + lift_damp * ghost

    @pl.loop(0, 8)
    def _(t):
        half, b = t // 4, t % 4
        pair = [half, 3 - half]
        total = [[[acc[v, a, b, h] for h in range(2)] for a in pair] for v in range(5)]
        for d, w in enumerate((wx, wy, wz)):
            for vi in range(5):
                flux = [[w[vi, a, b, h] for h in range(2)] for a in pair]
                for vo in range(5):
                    weight = jn[25 * d + 5 * vo + vi]
                    for n in range(2):
                        for h in range(2):
                            total[vo][n][h] = total[vo][n][h] + weight * flux[n][h]
        for n, a in enumerate(pair):
            outs = smooth(a, b, [total[v][n] for v in range(5)])
            for v in range(5):
                for h in range(2):
                    q[v, a, b, h] = q[v, a, b, h] + outs[v][h]

    def send_coarse(level):
        @pl.loop(0, 5)
        def _(v):
            s2[level, 0, v] = pack_low(ctr[0, v, 0], ctr[0, v, 1], x0, 2)
            hi = [jnp.where(fx, ctr[1, v, 1 - j], ctr[1, v, j]) for j in range(2)]
            s2[level, 1, v] = pack_high(hi[0], hi[1], x0, 2)
            s2[level, 2, v] = pack_low(ctr[2, v, 0], ctr[2, v, 1], y0, 1)
            hi = [jnp.where(fy, ctr[3, v, 1 - i], ctr[3, v, i]) for i in range(2)]
            s2[level, 3, v] = pack_high(hi[0], hi[1], y0, 1)

        for copy in sends2[level]:
            copy.start()

    def coarse_ghosts(level, v, slot, mask, step, flip):
        lo = [ctr[slot, v, n] for n in range(2)]
        hi = [ctr[slot + 1, v, n] for n in range(2)]
        packed_lo, packed_hi = r2[level, slot, v], r2[level, slot + 1, v]
        right = [
            jnp.where(mask, sub_roll(lo[0], -step), sub_roll(packed_lo, step)),
            jnp.where(mask, sub_roll(lo[1], -step), packed_lo),
        ]
        right = [jnp.where(flip, right[1 - n], right[n]) for n in range(2)]
        hi = [jnp.where(flip, hi[1 - n], hi[n]) for n in range(2)]
        left = [
            jnp.where(mask, packed_hi, sub_roll(hi[0], step)),
            jnp.where(mask, sub_roll(packed_hi, -step), sub_roll(hi[1], step)),
        ]
        return left, right

    def coarse_mix():
        total = [[[crhs[1, v, i, j] for j in range(2)] for i in range(2)] for v in range(5)]
        for d in range(3):
            for vi in range(5):
                flux = [[wc[d, vi, i, j] for j in range(2)] for i in range(2)]
                for vo in range(5):
                    weight = jn[25 * d + 5 * vo + vi]
                    for i in range(2):
                        for j in range(2):
                            total[vo][i][j] = total[vo][i][j] + weight * flux[i][j]
        return total

    def coarse_smooth(total):
        outs = [[[None, None] for _ in range(2)] for _ in range(5)]
        for vo in range(5):
            for vi in range(5):
                for i in range(2):
                    for j in range(2):
                        term = csf[5 * vo + vi, i, j] * total[vi][i][j]
                        outs[vo][i][j] = term if vi == 0 else outs[vo][i][j] + term
        return outs

    @pl.loop(0, 5)
    def _(v):
        rc = [[restrict_c(q[v, a, b, 0], q[v, a, b, 1])[3] for b in range(4)] for a in range(4)]
        rbc = [restrict_line(rc[a]) for a in range(4)]
        rac = [restrict_line([rc[a][b] for a in range(4)]) for b in range(4)]
        for n in range(2):
            ctr[0, v, n] = rbc[0][n]
            ctr[1, v, n] = rbc[3][n]
            ctr[2, v, n] = rac[0][n]
            ctr[3, v, n] = rac[3][n]
        for i in range(2):
            for j in range(2):
                wc[0, v, i, j] = dot_terms(EDGE[i], [rbc[a][j] for a in range(4)])
                wc[1, v, i, j] = dot_terms(EDGE[j], [rac[b][i] for b in range(4)])

    send_coarse(0)

    e_ends = halves(EDGE[0, 0], EDGE[1, 3])
    e_ends_sw = halves(EDGE[0, 3], EDGE[1, 0])
    e_inner = halves(EDGE[0, 1], EDGE[1, 2])
    e_inner_sw = halves(EDGE[0, 2], EDGE[1, 1])
    z_lift = halves(-LIFT, LIFT)

    @pl.loop(0, 5)
    def _(v):
        ra = [[restrict_line([q[v, a, b, h] for a in range(4)]) for b in range(4)] for h in range(2)]
        traces = [[None, None], [None, None]]
        for i in range(2):
            first = restrict_line([ra[0][b][i] for b in range(4)])
            second = restrict_line([ra[1][b][i] for b in range(4)])
            for j in range(2):
                ends, inner, inner_sw, full = restrict_c(first[j], second[j])
                traces[j][i] = ends
                wc[2, v, i, j] = (
                    e_ends * ends + e_ends_sw * sub_roll(ends, 4) + e_inner * inner + e_inner_sw * inner_sw
                )
                crhs[1, v, i, j] = rsrc[v, i, j] - (OMEGA * SHIFT) * full
        for j in range(2):
            ghosts = z_ghosts(traces[j], fz)
            for i in range(2):
                wc[2, v, i, j] = wc[2, v, i, j] + z_lift * ghosts[i]
                crhs[1, v, i, j] = crhs[1, v, i, j] + lift_damp * (ghosts[i] - traces[j][i])

    for copy in sends2[0]:
        copy.wait_recv()

    @pl.loop(0, 5)
    def _(v):
        left, right = coarse_ghosts(0, v, 0, x0, 2, fx)
        for j in range(2):
            wc[0, v, 0, j] = wc[0, v, 0, j] - LIFT * left[j]
            wc[0, v, 1, j] = wc[0, v, 1, j] + LIFT * right[j]
            crhs[1, v, 0, j] = crhs[1, v, 0, j] + lift_damp * (left[j] - ctr[0, v, j])
            crhs[1, v, 1, j] = crhs[1, v, 1, j] + lift_damp * (right[j] - ctr[1, v, j])
        left, right = coarse_ghosts(0, v, 2, y0, 1, fy)
        for i in range(2):
            wc[1, v, i, 0] = wc[1, v, i, 0] - LIFT * left[i]
            wc[1, v, i, 1] = wc[1, v, i, 1] + LIFT * right[i]
            crhs[1, v, i, 0] = crhs[1, v, i, 0] + lift_damp * (left[i] - ctr[2, v, i])
            crhs[1, v, i, 1] = crhs[1, v, i, 1] + lift_damp * (right[i] - ctr[3, v, i])

    total = coarse_mix()
    for v in range(5):
        for i in range(2):
            for j in range(2):
                crhs[0, v, i, j] = total[v][i][j]
    outs = coarse_smooth(total)
    for v in range(5):
        for i in range(2):
            for j in range(2):
                cfield[v, i, j] = outs[v][i][j]

    half_damp, k_coarse = dmp[1], dmp[2]

    for level in (1, 2):
        @pl.loop(0, 5)
        def _(v):
            for n in range(2):
                ctr[0, v, n] = cfield[v, 0, n]
                ctr[1, v, n] = cfield[v, 1, n]
                ctr[2, v, n] = cfield[v, n, 0]
                ctr[3, v, n] = cfield[v, n, 1]

        send_coarse(level)

        @pl.loop(0, 5)
        def _(v):
            for j in range(2):
                field = [cfield[v, i, j] for i in range(2)]
                ghosts = z_ghosts(field, fz)
                for i in range(2):
                    swapped = sub_roll(field[i], 4)
                    wc[2, v, i, j] = jnp.where(low, 0.5, -0.5) * (swapped - ghosts[i])
                    crhs[1, v, i, j] = crhs[0, v, i, j] - k_coarse * field[i] + half_damp * ghosts[i]

        for copy in sends2[level]:
            copy.wait_recv()

        @pl.loop(0, 5)
        def _(v):
            left, right = coarse_ghosts(level, v, 0, x0, 2, fx)
            for j in range(2):
                wc[0, v, 0, j] = 0.5 * (cfield[v, 1, j] - left[j])
                wc[0, v, 1, j] = 0.5 * (right[j] - cfield[v, 0, j])
                crhs[1, v, 0, j] = crhs[1, v, 0, j] + half_damp * left[j]
                crhs[1, v, 1, j] = crhs[1, v, 1, j] + half_damp * right[j]
            left, right = coarse_ghosts(level, v, 2, y0, 1, fy)
            for i in range(2):
                wc[1, v, i, 0] = 0.5 * (cfield[v, i, 1] - left[i])
                wc[1, v, i, 1] = 0.5 * (right[i] - cfield[v, i, 0])
                crhs[1, v, i, 0] = crhs[1, v, i, 0] + half_damp * left[i]
                crhs[1, v, i, 1] = crhs[1, v, i, 1] + half_damp * right[i]

        outs = coarse_smooth(coarse_mix())
        for v in range(5):
            for i in range(2):
                for j in range(2):
                    cfield[v, i, j] = cfield[v, i, j] + outs[v][i][j]

    t_first = [halves(OMEGA, OMEGA * P_FAR), halves(0.0, OMEGA * P_NEAR)]
    t_second = [halves(OMEGA * P_FAR, OMEGA), halves(OMEGA * P_NEAR, 0.0)]

    @pl.loop(0, 5)
    def _(v):
        by_a = [prolong_line([cfield[v, i, j] for i in range(2)]) for j in range(2)]
        for a in range(4):
            for b, value in enumerate(prolong_line([by_a[j][a] for j in range(2)])):
                swapped = sub_roll(value, 4)
                wx[v, a, b, 0] = OMEGA * q[v, a, b, 0] + (t_first[0] * value + t_first[1] * swapped)
                wx[v, a, b, 1] = OMEGA * q[v, a, b, 1] + (t_second[0] * value + t_second[1] * swapped)

    store = pltpu.make_async_copy(wx, out_hbm, out_sem)
    store.start()
    for copy in sends1:
        copy.wait_send()
    for level in sends2:
        for copy in level:
            copy.wait_send()
    store.wait()


def body(source, jacobian, damping, orient, smoother, coarse_smoother):
    field = (5, 4, 4, 2, 8, 128)
    any_space = pl.BlockSpec(memory_space=pl.ANY)
    vmem = pltpu.VMEM
    out = pl.pallas_call(
        kernel,
        out_shape=jax.ShapeDtypeStruct(field, F32),
        in_specs=[any_space] * 6,
        out_specs=any_space,
        scratch_shapes=[
            vmem(field, F32),
            vmem((25, 4, 4, 16, 128), jnp.bfloat16),
            vmem((25, 2, 16, 128), jnp.bfloat16),
            vmem((75, 4, 128), F32),
            vmem((75, 8, 128), F32),
            vmem((4, 128), F32),
            vmem((3, 4, 128), jnp.int32),
            vmem((3, 8, 128), jnp.int32),
            vmem((5, 8, 128), F32),
            vmem((4, 2, 2, 8, 128), F32),
            vmem((25, 2, 2, 8, 128), F32),
            vmem(field, F32),
            vmem(field, F32),
            vmem(field, F32),
            vmem(field, F32),
            vmem(field, F32),
            vmem((5, 2, 2, 8, 128), F32),
            vmem((8, 128), F32),
            vmem((4, 5, 2, 8, 128), F32),
            vmem((3, 5, 2, 2, 8, 128), F32),
            vmem((5, 2, 2, 8, 128), F32),
            vmem((2, 5, 2, 2, 8, 128), F32),
            vmem((4, 5, 4, 8, 128), F32),
            vmem((4, 5, 4, 8, 128), F32),
            vmem((3, 4, 5, 8, 128), F32),
            vmem((3, 4, 5, 8, 128), F32),
            pltpu.SemaphoreType.DMA((12,)),
            pltpu.SemaphoreType.DMA,
            pltpu.SemaphoreType.DMA((16,)),
            pltpu.SemaphoreType.DMA((16,)),
        ],
        compiler_params=pltpu.CompilerParams(
            collective_id=0, has_side_effects=True
        ),
    )(
        source.reshape(field),
        jacobian.reshape(75, 4, 128),
        damping.reshape(4, 128),
        orient.reshape(3, 4, 128),
        smoother.reshape(25, 4, 4, 16, 128),
        coarse_smoother.reshape(25, 2, 16, 128),
    )
    return out.reshape(5, 4, 4, 4, 2, 2, 128)


def solution(mesh):
    in_specs = (
        P(None, None, None, None, "gx", "gy", None),
        P(None, None, None, "gx", "gy", None),
        P("gx", "gy", None),
        P(None, "gx", "gy", None),
        P(None, None, None, None, None, "gx", "gy", None),
        P(None, None, None, None, None, "gx", "gy", None),
    )
    out_specs = P(None, None, None, None, "gx", "gy", None)
    return jax.shard_map(body, mesh=mesh, in_specs=in_specs, out_specs=out_specs, check_vma=False)
```

```python
import functools
import math

import jax
import jax.numpy as jnp
import numpy as np
from jax import lax
from jax.experimental import pallas as pl
from jax.experimental.pallas import tpu as pltpu
from jax.sharding import PartitionSpec as P

MESH = pl.DeviceIdType.MESH
OMEGA = 0.8
SHIFT = 2.0
F32 = jnp.float32


def lobatto4():
    points = np.array([-1.0, -1.0 / math.sqrt(5.0), 1.0 / math.sqrt(5.0), 1.0])
    weights = np.ones(4)
    for row in range(4):
        for col in range(4):
            if row != col:
                weights[row] /= points[row] - points[col]
    slopes = np.zeros((4, 4))
    for row in range(4):
        for col in range(4):
            if row != col:
                slopes[row, col] = weights[col] / weights[row] / (points[row] - points[col])
        slopes[row, row] = -np.sum(slopes[row])
    return points, slopes


POINTS, SLOPES = lobatto4()
INTERP = np.stack([(1.0 - POINTS) / 2.0, (1.0 + POINTS) / 2.0], 1)
OPEN = SLOPES.copy()
OPEN[0, 0] = OPEN[3, 3] = OPEN[1, 1] = OPEN[2, 2] = 0.0
LIFT = 3.0
EDGE = INTERP.T @ OPEN
P_NEAR, P_FAR = float(INTERP[1, 0]), float(INTERP[2, 0])


def dot_terms(coefs, values):
    total = None
    for coef, value in zip(coefs, values):
        coef = float(coef)
        if coef == 0.0:
            continue
        term = value if coef == 1.0 else coef * value
        total = term if total is None else total + term
    return total


def rows():
    return lax.broadcasted_iota(jnp.int32, (8, 128), 0)


def halves(top, bottom):
    return jnp.where(rows() < 4, jnp.full((8, 128), float(top), F32), jnp.full((8, 128), float(bottom), F32))


def sub_roll(value, shift):
    return pltpu.roll(value, shift % 8, 0)


def lane_roll(value, shift):
    return pltpu.roll(value, shift % 128, 1)


def pack_low(first, second, mask, step):
    return jnp.where(mask, first, sub_roll(second, step))


def pack_high(first, second, mask, step):
    return jnp.where(mask, sub_roll(first, -step), second)


def z_ghosts(traces, turned):
    count = len(traces)
    low = rows() < 4
    flip = jnp.logical_and(turned, rows() >= 4)
    out = []
    for a in range(count):
        swapped = sub_roll(jnp.where(flip, traces[count - 1 - a], traces[a]), 4)
        out.append(jnp.where(low, lane_roll(swapped, 1), lane_roll(swapped, -1)))
    return [jnp.where(flip, out[count - 1 - a], out[a]) for a in range(count)]


def restrict_c(first, second):
    low = rows() < 4
    ends = jnp.where(low, first, second)
    inner_swapped = jnp.where(low, second, first)
    inner = sub_roll(inner_swapped, 4)
    return ends, inner, inner_swapped, ends + P_NEAR * inner + P_FAR * inner_swapped


def restrict_line(values):
    low = values[0] + P_NEAR * values[1] + P_FAR * values[2]
    high = values[3] + P_NEAR * values[2] + P_FAR * values[1]
    return [low, high]


def prolong_line(values):
    return [
        values[0],
        P_NEAR * values[0] + P_FAR * values[1],
        P_FAR * values[0] + P_NEAR * values[1],
        values[1],
    ]


def swap_rows(value, step):
    return jnp.where((rows() & step) == 0, sub_roll(value, -step), sub_roll(value, step))


def kernel(
    src_hbm, jac_hbm, damp_hbm, flag_hbm, smo_hbm, csm_hbm, out,
    src, smo, csm, jraw, jn, draw, fraw, flags, dmp, kfine, csf, kface,
    q, acc, wx, wy, wz, rsrc, rcs, ctr, wc, cfield, crhs, gcor,
    s1, r1, s2, r2, s3, r3, sp, rp, sd, rd, sg, rg, in_sem, send_sem, recv_sem,
):
    nx, ny = lax.axis_size("gx"), lax.axis_size("gy")
    ix, iy = lax.axis_index("gx"), lax.axis_index("gy")
    x_next, x_prev = lax.rem(ix + 1, nx), lax.rem(ix + nx - 1, nx)
    y_next, y_prev = lax.rem(iy + 1, ny), lax.rem(iy + ny - 1, ny)
    partners = [(x_prev, iy), (x_next, iy), (ix, y_prev), (ix, y_next)]
    corners = [(x_prev, y_prev), (x_next, y_prev), (x_prev, y_next), (x_next, y_next)]

    barrier = pltpu.get_barrier_semaphore()
    for partner in partners + corners:
        pl.semaphore_signal(barrier, inc=1, device_id=partner, device_id_type=MESH)

    loads = []

    def load(source, target):
        copy = pltpu.make_async_copy(source, target, in_sem.at[len(loads)])
        copy.start()
        loads.append(copy)
        return copy

    parts = {}
    for a in (0, 3):
        parts[a] = (load(src_hbm.at[:, a], src.at[:, a]), load(smo_hbm.at[:, a], smo.at[:, a]))
    flag_load = load(flag_hbm, fraw)
    damp_load = load(damp_hbm, draw)
    jac_load = load(jac_hbm, jraw)
    csm_load = load(csm_hbm, csm)
    for a in (1, 2):
        parts[a] = (load(src_hbm.at[:, a], src.at[:, a]), load(smo_hbm.at[:, a], smo.at[:, a]))

    started = []

    def remote(source, target, number, partner):
        copy = pltpu.make_async_remote_copy(
            src_ref=source, dst_ref=target, send_sem=send_sem.at[number], recv_sem=recv_sem.at[number],
            device_id=partner, device_id_type=MESH,
        )
        started.append(copy)
        return copy

    sends1 = [remote(s1.at[k], r1.at[k], k, partners[k]) for k in range(4)]
    sends2 = [remote(s2.at[k], r2.at[k], 4 + k, partners[k]) for k in range(4)]
    sends3 = [remote(s3.at[k], r3.at[k], 8 + k, partners[k]) for k in range(4)]
    sends_part = [remote(sp.at[k], rp.at[k], 12 + k, partners[k]) for k in range(4)]
    sends_corner = [remote(sd.at[k], rd.at[k], 16 + k, corners[k]) for k in range(4)]
    sends_face = [remote(sg.at[k], rg.at[k], 20 + k, partners[k]) for k in range(4)]

    low = rows() < 4
    x0 = (rows() & 2) == 0
    y0 = (rows() & 1) == 0
    zero = jnp.zeros((8, 128), F32)

    def smooth(a, b, fields):
        outs = []
        for vo in range(5):
            pair = [None, None]
            for vi in range(5):
                block = smo[5 * vo + vi, a, b].astype(F32)
                for half in range(2):
                    term = block[8 * half : 8 * half + 8] * fields[vi][half]
                    pair[half] = term if vi == 0 else pair[half] + term
            outs.append(pair)
        return outs

    def first_pass(a, b):
        fields = [[src[v, a, b, 0], src[v, a, b, 1]] for v in range(5)]
        outs = smooth(a, b, fields)
        for v in range(5):
            q[v, a, b, 0] = outs[v][0]
            q[v, a, b, 1] = outs[v][1]

    for a in (0, 3):
        for copy in parts[a]:
            copy.wait()

        @pl.loop(0, 4)
        def _(b, a=a):
            first_pass(a, b)

    flag_load.wait()
    damp_load.wait()
    for d in range(3):
        flags[d] = jnp.concatenate([fraw[d], fraw[d]], axis=0)
    fx, fy, fz = (flags[d] == 1 for d in range(3))

    @pl.loop(0, 5)
    def _(v):
        for b in range(4):
            s1[0, v, b] = pack_low(q[v, 0, b, 0], q[v, 0, b, 1], x0, 2)
            hi = [jnp.where(fx, q[v, 3, 3 - b, h], q[v, 3, b, h]) for h in range(2)]
            s1[1, v, b] = pack_high(hi[0], hi[1], x0, 2)

    pl.semaphore_wait(barrier, 8)
    sends1[0].start()
    sends1[1].start()

    for a in (1, 2):
        for copy in parts[a]:
            copy.wait()

        @pl.loop(0, 4)
        def _(b, a=a):
            first_pass(a, b)

    @pl.loop(0, 5)
    def _(v):
        for a in range(4):
            s1[2, v, a] = pack_low(q[v, a, 0, 0], q[v, a, 0, 1], y0, 1)
            hi = [jnp.where(fy, q[v, 3 - a, 3, h], q[v, a, 3, h]) for h in range(2)]
            s1[3, v, a] = pack_high(hi[0], hi[1], y0, 1)

    sends1[2].start()
    sends1[3].start()

    damping = jnp.concatenate([draw[...], draw[...]], axis=0)
    dmp[0] = (OMEGA * LIFT) * damping
    dmp[1] = (OMEGA * 0.5) * damping
    dmp[2] = OMEGA * SHIFT + (OMEGA * 1.5) * damping
    dmp[3] = jnp.where(low, (OMEGA * LIFT) * damping, 0.0)
    dmp[4] = jnp.where(low, 0.0, (OMEGA * LIFT) * damping)
    for b in range(4):
        for a_end in range(2):
            faces = a_end + (1 if b in (0, 3) else 0)
            base = OMEGA * SHIFT + (OMEGA * LIFT * faces) * damping
            kfine[b, a_end, 0] = base + dmp[3]
            kfine[b, a_end, 1] = base + dmp[4]

    jac_load.wait()

    @pl.loop(0, 75)
    def _(i):
        block = jraw[i]
        jn[i] = (-OMEGA) * jnp.concatenate([block, block], axis=0)

    csm_load.wait()

    @pl.loop(0, 25)
    def _(i):
        for n in range(2):
            block = csm[i, n].astype(F32)
            csf[i, n, 0] = block[:8]
            csf[i, n, 1] = block[8:]

    half_damp, k_coarse, lift_damp = dmp[1], dmp[2], dmp[0]

    def pack_side(side, first, second):
        mask, step = (x0, 2) if side < 2 else (y0, 1)
        return (pack_low if side % 2 == 0 else pack_high)(first, second, mask, step)

    for side in range(4):
        own, other = (0, 1) if side < 2 else (1, 0)
        sign = -0.5 if side % 2 == 0 else 0.5
        cross_sign = jnp.where(y0 if side < 2 else x0, -0.5, 0.5)

        @pl.loop(0, 5)
        def _(row, side=side, own=own, other=other, sign=sign, cross_sign=cross_sign):
            for col in range(5):
                diag = jnp.where(row == col, half_damp, zero)
                face = diag + sign * jn[25 * own + 5 * row + col]
                cross = diag + cross_sign * jn[25 * other + 5 * row + col]
                kface[0, 5 * row + col] = pack_side(side, face, face)
                kface[1, 5 * row + col] = pack_side(side, cross, cross)

        @pl.loop(0, 5)
        def _(vo, side=side):
            blocks = []
            for m in range(5):
                if side < 2:
                    pair = [csf[5 * vo + m, side, j] for j in range(2)]
                else:
                    pair = [csf[5 * vo + m, i, side - 2] for i in range(2)]
                blocks.append(pack_side(side, pair[0], pair[1]))
            for n in range(2):
                for vi in range(5):
                    total = blocks[0] * kface[n, vi]
                    for m in range(1, 5):
                        total = total + blocks[m] * kface[n, 5 * m + vi]
                    sg[side, 25 * n + 5 * vo + vi] = total

        for n, d in enumerate((own, other)):
            flag = jnp.where(flags[d] == 1, 1.0, 0.0)
            sg[side, 50 + n] = pack_side(side, flag, flag)

    for copy in sends_face:
        copy.start()

    c_first = [halves(OPEN[0, 1], OPEN[1, 0]), halves(OPEN[0, 2], OPEN[1, 3]), halves(OPEN[0, 3], OPEN[1, 2])]
    c_second = [halves(OPEN[2, 3], OPEN[3, 2]), halves(OPEN[2, 0], OPEN[3, 1]), halves(OPEN[2, 1], OPEN[3, 0])]
    c_ghost = [halves(-LIFT, 0.0), halves(0.0, LIFT)]

    @pl.loop(0, 20)
    def _(t):
        v, b = t // 4, t % 4
        first = [q[v, a, b, 0] for a in range(4)]
        second = [q[v, a, b, 1] for a in range(4)]
        for a in range(4):
            for h, line in enumerate((first, second)):
                wx[v, a, b, h] = dot_terms(OPEN[a], line)
        ghosts = z_ghosts([jnp.where(low, first[a], second[a]) for a in range(4)], fz)
        for a in range(4):
            a_end = 1 if a in (0, 3) else 0
            first_sw, second_sw = sub_roll(first[a], 4), sub_roll(second[a], 4)
            wz[v, a, b, 0] = (
                c_first[0] * first_sw + c_first[1] * second[a] + c_first[2] * second_sw + c_ghost[0] * ghosts[a]
            )
            wz[v, a, b, 1] = (
                c_second[0] * second_sw + c_second[1] * first[a] + c_second[2] * first_sw + c_ghost[1] * ghosts[a]
            )
            acc[v, a, b, 0] = src[v, a, b, 0] - kfine[b, a_end, 0] * first[a] + dmp[3] * ghosts[a]
            acc[v, a, b, 1] = src[v, a, b, 1] - kfine[b, a_end, 1] * second[a] + dmp[4] * ghosts[a]

    @pl.loop(0, 20)
    def _(t):
        v, a = t // 4, t % 4
        for h in range(2):
            line = [q[v, a, b, h] for b in range(4)]
            for b in range(4):
                wy[v, a, b, h] = dot_terms(OPEN[b], line)

    def mix(pair, directions, last):
        @pl.loop(0, 4)
        def _(b):
            total = [[[acc[v, a, b, h] for h in range(2)] for a in pair] for v in range(5)]
            for d in directions:
                w = (wx, wy, wz)[d]
                for vi in range(5):
                    flux = [[w[vi, a, b, h] for h in range(2)] for a in pair]
                    for vo in range(5):
                        weight = jn[25 * d + 5 * vo + vi]
                        for n in range(2):
                            for h in range(2):
                                total[vo][n][h] = total[vo][n][h] + weight * flux[n][h]
            for n, a in enumerate(pair):
                if last:
                    outs = smooth(a, b, [total[v][n] for v in range(5)])
                for v in range(5):
                    for h in range(2):
                        if last:
                            q[v, a, b, h] = q[v, a, b, h] + outs[v][h]
                        else:
                            acc[v, a, b, h] = total[v][n][h]

    mix((0, 3), (2,), False)
    mix((1, 2), (0, 2), False)

    @pl.loop(0, 5)
    def _(v):
        by_a = []
        for a in range(4):
            by_a.append(restrict_line([restrict_c(src[v, a, b, 0], src[v, a, b, 1])[3] for b in range(4)]))
        for j in range(2):
            for i, value in enumerate(restrict_line([by_a[a][j] for a in range(4)])):
                rsrc[v, i, j] = value

    sends1[2].wait_recv()
    sends1[3].wait_recv()

    @pl.loop(0, 5)
    def _(v):
        for h in range(2):
            lo = [q[v, a, 0, h] for a in range(4)]
            hi = [q[v, a, 3, h] for a in range(4)]
            right = []
            for a in range(4):
                packed = r1[2, v, a]
                right.append(jnp.where(y0, sub_roll(lo[a], -1), sub_roll(packed, 1) if h == 0 else packed))
            for a in range(4):
                packed = r1[3, v, a]
                hi_turned = jnp.where(fy, hi[3 - a], hi[a])
                left = jnp.where(y0, packed if h == 0 else sub_roll(packed, -1), sub_roll(hi_turned, 1))
                ghost = jnp.where(fy, right[3 - a], right[a])
                wy[v, a, 0, h] = wy[v, a, 0, h] - LIFT * left
                wy[v, a, 3, h] = wy[v, a, 3, h] + LIFT * ghost
                acc[v, a, 0, h] = acc[v, a, 0, h] + lift_damp * left
                acc[v, a, 3, h] = acc[v, a, 3, h] + lift_damp * ghost

    mix((0, 3), (1,), False)
    mix((1, 2), (1,), True)

    def restrict_c_into(v, a_list):
        for a in a_list:
            for b in range(4):
                rcs[v, a, b] = restrict_c(q[v, a, b, 0], q[v, a, b, 1])[3]

    @pl.loop(0, 5)
    def _(v):
        restrict_c_into(v, (1, 2))

    sends1[0].wait_recv()
    sends1[1].wait_recv()

    @pl.loop(0, 5)
    def _(v):
        for h in range(2):
            lo = [q[v, 0, b, h] for b in range(4)]
            hi = [q[v, 3, b, h] for b in range(4)]
            right = []
            for b in range(4):
                packed = r1[0, v, b]
                right.append(jnp.where(x0, sub_roll(lo[b], -2), sub_roll(packed, 2) if h == 0 else packed))
            for b in range(4):
                packed = r1[1, v, b]
                hi_turned = jnp.where(fx, hi[3 - b], hi[b])
                left = jnp.where(x0, packed if h == 0 else sub_roll(packed, -2), sub_roll(hi_turned, 2))
                ghost = jnp.where(fx, right[3 - b], right[b])
                wx[v, 0, b, h] = wx[v, 0, b, h] - LIFT * left
                wx[v, 3, b, h] = wx[v, 3, b, h] + LIFT * ghost
                acc[v, 0, b, h] = acc[v, 0, b, h] + lift_damp * left
                acc[v, 3, b, h] = acc[v, 3, b, h] + lift_damp * ghost

    mix((0, 3), (0,), True)

    def pack_traces(v, target, turn):
        for side in range(4):
            pair = [ctr[side, v, n] for n in range(2)]
            if turn and side % 2 == 1:
                flip = fx if side < 2 else fy
                pair = [jnp.where(flip, pair[1 - n], pair[n]) for n in range(2)]
            target[side, v] = pack_side(side, pair[0], pair[1])

    @pl.loop(0, 5)
    def _(v):
        restrict_c_into(v, (0, 3))
        for slot, a in ((0, 0), (1, 3)):
            for n, value in enumerate(restrict_line([rcs[v, a, b] for b in range(4)])):
                ctr[slot, v, n] = value
        for slot, b in ((2, 0), (3, 3)):
            for n, value in enumerate(restrict_line([rcs[v, a, b] for a in range(4)])):
                ctr[slot, v, n] = value
        pack_traces(v, s2, True)

    for copy in sends2:
        copy.start()

    def inner_ghosts(v, slot, mask, step, flip):
        lo = [ctr[slot, v, n] for n in range(2)]
        hi = [ctr[slot + 1, v, n] for n in range(2)]
        right = [jnp.where(mask, sub_roll(value, -step), zero) for value in lo]
        right = [jnp.where(flip, right[1 - n], right[n]) for n in range(2)]
        hi = [jnp.where(flip, hi[1 - n], hi[n]) for n in range(2)]
        left = [jnp.where(mask, zero, sub_roll(value, step)) for value in hi]
        return left, right

    def coarse_sweep():
        total = [[[crhs[v, i, j] for j in range(2)] for i in range(2)] for v in range(5)]
        for d in range(3):
            for vi in range(5):
                flux = [[wc[d, vi, i, j] for j in range(2)] for i in range(2)]
                for vo in range(5):
                    weight = jn[25 * d + 5 * vo + vi]
                    for i in range(2):
                        for j in range(2):
                            total[vo][i][j] = total[vo][i][j] + weight * flux[i][j]
        outs = [[[None, None] for _ in range(2)] for _ in range(5)]
        for vo in range(5):
            for vi in range(5):
                for i in range(2):
                    for j in range(2):
                        term = csf[5 * vo + vi, i, j] * total[vi][i][j]
                        outs[vo][i][j] = term if vi == 0 else outs[vo][i][j] + term
        return outs

    e_ends = halves(EDGE[0, 0], EDGE[1, 3])
    e_ends_sw = halves(EDGE[0, 3], EDGE[1, 0])
    e_inner = halves(EDGE[0, 1], EDGE[1, 2])
    e_inner_sw = halves(EDGE[0, 2], EDGE[1, 1])
    z_lift = halves(-LIFT, LIFT)

    @pl.loop(0, 5)
    def _(v):
        rbc = [restrict_line([rcs[v, a, b] for b in range(4)]) for a in range(4)]
        rac = [restrict_line([rcs[v, a, b] for a in range(4)]) for b in range(4)]
        for i in range(2):
            for j in range(2):
                wc[0, v, i, j] = dot_terms(EDGE[i], [rbc[a][j] for a in range(4)])
                wc[1, v, i, j] = dot_terms(EDGE[j], [rac[b][i] for b in range(4)])
        ra = [[restrict_line([q[v, a, b, h] for a in range(4)]) for b in range(4)] for h in range(2)]
        traces = [[None, None], [None, None]]
        for i in range(2):
            first = restrict_line([ra[0][b][i] for b in range(4)])
            second = restrict_line([ra[1][b][i] for b in range(4)])
            for j in range(2):
                ends, inner, inner_sw, full = restrict_c(first[j], second[j])
                traces[j][i] = ends
                wc[2, v, i, j] = (
                    e_ends * ends + e_ends_sw * sub_roll(ends, 4) + e_inner * inner + e_inner_sw * inner_sw
                )
                crhs[v, i, j] = rsrc[v, i, j] - (OMEGA * SHIFT) * full
        for j in range(2):
            ghosts = z_ghosts(traces[j], fz)
            for i in range(2):
                wc[2, v, i, j] = wc[2, v, i, j] + z_lift * ghosts[i]
                crhs[v, i, j] = crhs[v, i, j] + lift_damp * (ghosts[i] - traces[j][i])

    @pl.loop(0, 5)
    def _(v):
        left, right = inner_ghosts(v, 0, x0, 2, fx)
        for j in range(2):
            wc[0, v, 0, j] = wc[0, v, 0, j] - LIFT * left[j]
            wc[0, v, 1, j] = wc[0, v, 1, j] + LIFT * right[j]
            crhs[v, 0, j] = crhs[v, 0, j] + lift_damp * (left[j] - ctr[0, v, j])
            crhs[v, 1, j] = crhs[v, 1, j] + lift_damp * (right[j] - ctr[1, v, j])
        left, right = inner_ghosts(v, 2, y0, 1, fy)
        for i in range(2):
            wc[1, v, i, 0] = wc[1, v, i, 0] - LIFT * left[i]
            wc[1, v, i, 1] = wc[1, v, i, 1] + LIFT * right[i]
            crhs[v, i, 0] = crhs[v, i, 0] + lift_damp * (left[i] - ctr[2, v, i])
            crhs[v, i, 1] = crhs[v, i, 1] + lift_damp * (right[i] - ctr[3, v, i])

    outs = coarse_sweep()
    for v in range(5):
        for i in range(2):
            for j in range(2):
                cfield[0, v, i, j] = outs[v][i][j]

    @pl.loop(0, 20)
    def _(t):
        v, b = t // 4, t % 4
        for a in range(4):
            for h in range(2):
                out[v, a, b, h] = OMEGA * q[v, a, b, h]

    def face_product(ref, side, base, vectors):
        outs = []
        for vo in range(5):
            total = ref[side, base + 5 * vo] * vectors[0]
            for vi in range(1, 5):
                total = total + ref[side, base + 5 * vo + vi] * vectors[vi]
            outs.append(total)
        return outs

    def own_ghost(side, value):
        if side % 2 == 0:
            return value
        return jnp.where(sg[side, 50] == 1.0, swap_rows(value, 2 if side < 2 else 1), value)

    def add_faces(slot, scale, ghosts):
        for side in range(4):
            mask, step = (x0, 2) if side < 2 else (y0, 1)
            for v, delta in enumerate(face_product(sg, side, 0, ghosts[side])):
                if scale != 1.0:
                    delta = scale * delta
                if side % 2 == 0:
                    pair = [jnp.where(mask, delta, zero), jnp.where(mask, sub_roll(delta, -step), zero)]
                else:
                    pair = [jnp.where(mask, zero, sub_roll(delta, step)), jnp.where(mask, zero, delta)]
                for n in range(2):
                    i, j = (side, n) if side < 2 else (n, side - 2)
                    cfield[slot, v, i, j] = cfield[slot, v, i, j] + pair[n]

    def inner_operator(slot):
        @pl.loop(0, 5)
        def _(v):
            field = [[cfield[slot, v, i, j] for j in range(2)] for i in range(2)]
            for n in range(2):
                ctr[0, v, n] = field[0][n]
                ctr[1, v, n] = field[1][n]
                ctr[2, v, n] = field[n][0]
                ctr[3, v, n] = field[n][1]
            rhs = [[(-k_coarse) * field[i][j] for j in range(2)] for i in range(2)]
            for j in range(2):
                ghosts = z_ghosts([field[i][j] for i in range(2)], fz)
                for i in range(2):
                    swapped = sub_roll(field[i][j], 4)
                    wc[2, v, i, j] = jnp.where(low, 0.5, -0.5) * (swapped - ghosts[i])
                    rhs[i][j] = rhs[i][j] + half_damp * ghosts[i]
            left, right = inner_ghosts(v, 0, x0, 2, fx)
            for j in range(2):
                wc[0, v, 0, j] = 0.5 * (field[1][j] - left[j])
                wc[0, v, 1, j] = 0.5 * (right[j] - field[0][j])
                rhs[0][j] = rhs[0][j] + half_damp * left[j]
                rhs[1][j] = rhs[1][j] + half_damp * right[j]
            left, right = inner_ghosts(v, 2, y0, 1, fy)
            for i in range(2):
                wc[1, v, i, 0] = 0.5 * (field[i][1] - left[i])
                wc[1, v, i, 1] = 0.5 * (right[i] - field[i][0])
                rhs[i][0] = rhs[i][0] + half_damp * left[i]
                rhs[i][1] = rhs[i][1] + half_damp * right[i]
            for i in range(2):
                for j in range(2):
                    crhs[v, i, j] = rhs[i][j]

        return coarse_sweep()

    for copy in sends2:
        copy.wait_recv()
    add_faces(0, 6.0, [[own_ghost(side, r2[side ^ 1, v]) for v in range(5)] for side in range(4)])

    row4 = rows() & 3

    @pl.loop(0, 5)
    def _(v):
        for n in range(2):
            ctr[0, v, n] = cfield[0, v, 0, n]
            ctr[1, v, n] = cfield[0, v, 1, n]
            ctr[2, v, n] = cfield[0, v, n, 0]
            ctr[3, v, n] = cfield[0, v, n, 1]
        pack_traces(v, s3, True)
        x_lo, x_hi, y_lo, y_hi = (s3[side, v] for side in range(4))
        sd[0, v] = jnp.where(x0, y_lo, jnp.where(row4 == 2, x_lo, sub_roll(x_lo, 3)))
        sd[1, v] = jnp.where(x0, x_hi, y_lo)
        sd[2, v] = jnp.where(row4 == 0, y_hi, x_lo)
        sd[3, v] = jnp.where(row4 == 3, y_hi, sub_roll(x_hi, -3))

    for copy in sends3 + sends_corner:
        copy.start()

    outs = inner_operator(0)
    for v in range(5):
        for i in range(2):
            for j in range(2):
                cfield[1, v, i, j] = 2.0 * cfield[0, v, i, j] + outs[v][i][j]

    @pl.loop(0, 5)
    def _(v):
        for n in range(2):
            ctr[0, v, n] = cfield[1, v, 0, n]
            ctr[1, v, n] = cfield[1, v, 1, n]
            ctr[2, v, n] = cfield[1, v, n, 0]
            ctr[3, v, n] = cfield[1, v, n, 1]
        pack_traces(v, sp, False)

    for copy in sends_part:
        copy.start()

    for copy in sends_face + sends3 + sends_corner:
        copy.wait_recv()

    def corner_ghosts(side, v):
        prev_prev, next_prev, prev_next, next_next = (rd[k, v] for k in (3, 2, 1, 0))
        flip = rg[side ^ 1, 51] == 1.0
        if side == 1:
            lower = next_prev
            upper = jnp.where(flip, sub_roll(next_next, 2), sub_roll(next_next, 3))
        elif side == 0:
            lower = sub_roll(prev_prev, -3)
            upper = jnp.where(flip, sub_roll(prev_next, 1), prev_next)
        elif side == 3:
            lower = prev_next
            upper = jnp.where(flip, sub_roll(next_next, 1), next_next)
        else:
            lower = prev_prev
            upper = jnp.where(flip, sub_roll(next_prev, 2), next_prev)
        return jnp.where(row4 == 0, lower, jnp.where(row4 == 3, upper, zero))

    for side in range(4):
        step = 2 if side < 2 else 1
        mine = [s3[side, v] for v in range(5)]
        if side % 2 == 0:
            turn = rg[side ^ 1, 50] == 1.0
            mine = [jnp.where(turn, swap_rows(value, step), value) for value in mine]
        first = face_product(rg, side ^ 1, 0, mine)
        second = face_product(rg, side ^ 1, 25, [corner_ghosts(side, v) for v in range(5)])
        for v in range(5):
            gcor[side, v] = first[v] + second[v]

    add_faces(1, 1.0, [[own_ghost(side, r3[side ^ 1, v]) for v in range(5)] for side in range(4)])
    outs = inner_operator(1)
    for v in range(5):
        for i in range(2):
            for j in range(2):
                cfield[0, v, i, j] = cfield[0, v, i, j] + cfield[1, v, i, j] + outs[v][i][j]

    for copy in sends_part:
        copy.wait_recv()

    ghosts = []
    for side in range(4):
        step = 2 if side < 2 else 1
        values = [rp[side ^ 1, v] + gcor[side, v] for v in range(5)]
        if side % 2 == 0:
            turn = rg[side ^ 1, 50] == 1.0
            values = [jnp.where(turn, swap_rows(value, step), value) for value in values]
        else:
            values = [own_ghost(side, value) for value in values]
        ghosts.append(values)
    add_faces(0, 1.0, ghosts)

    t_first = [halves(OMEGA, OMEGA * P_FAR), halves(0.0, OMEGA * P_NEAR)]
    t_second = [halves(OMEGA * P_FAR, OMEGA), halves(OMEGA * P_NEAR, 0.0)]

    @pl.loop(0, 5)
    def _(v):
        by_a = [prolong_line([cfield[0, v, i, j] for i in range(2)]) for j in range(2)]
        for a in range(4):
            for b, value in enumerate(prolong_line([by_a[j][a] for j in range(2)])):
                swapped = sub_roll(value, 4)
                out[v, a, b, 0] = out[v, a, b, 0] + (t_first[0] * value + t_first[1] * swapped)
                out[v, a, b, 1] = out[v, a, b, 1] + (t_second[0] * value + t_second[1] * swapped)

    for copy in started:
        copy.wait_send()


def body(source, jacobian, damping, orient, smoother, coarse_smoother):
    field = (5, 4, 4, 2, 8, 128)
    vmem = pltpu.VMEM
    hbm = pl.BlockSpec(memory_space=pltpu.HBM)
    out = pl.pallas_call(
        kernel,
        out_shape=pltpu.VMEM(field, F32),
        in_specs=[hbm] * 6,
        out_specs=pl.BlockSpec(memory_space=pltpu.VMEM),
        scratch_shapes=[
            vmem(field, F32),
            vmem((25, 4, 4, 16, 128), jnp.bfloat16),
            vmem((25, 2, 16, 128), jnp.bfloat16),
            vmem((75, 4, 128), F32),
            vmem((75, 8, 128), F32),
            vmem((4, 128), F32),
            vmem((3, 4, 128), jnp.int32),
            vmem((3, 8, 128), jnp.int32),
            vmem((5, 8, 128), F32),
            vmem((4, 2, 2, 8, 128), F32),
            vmem((25, 2, 2, 8, 128), F32),
            vmem((2, 25, 8, 128), F32),
            vmem(field, F32),
            vmem(field, F32),
            vmem(field, F32),
            vmem(field, F32),
            vmem(field, F32),
            vmem((5, 2, 2, 8, 128), F32),
            vmem((5, 4, 4, 8, 128), F32),
            vmem((4, 5, 2, 8, 128), F32),
            vmem((3, 5, 2, 2, 8, 128), F32),
            vmem((2, 5, 2, 2, 8, 128), F32),
            vmem((5, 2, 2, 8, 128), F32),
            vmem((4, 5, 8, 128), F32),
            vmem((4, 5, 4, 8, 128), F32),
            vmem((4, 5, 4, 8, 128), F32),
            vmem((4, 5, 8, 128), F32),
            vmem((4, 5, 8, 128), F32),
            vmem((4, 5, 8, 128), F32),
            vmem((4, 5, 8, 128), F32),
            vmem((4, 5, 8, 128), F32),
            vmem((4, 5, 8, 128), F32),
            vmem((4, 5, 8, 128), F32),
            vmem((4, 5, 8, 128), F32),
            vmem((4, 52, 8, 128), F32),
            vmem((4, 52, 8, 128), F32),
            pltpu.SemaphoreType.DMA((12,)),
            pltpu.SemaphoreType.DMA((24,)),
            pltpu.SemaphoreType.DMA((24,)),
        ],
        compiler_params=pltpu.CompilerParams(collective_id=0, has_side_effects=True),
    )(
        source.reshape(field),
        jacobian.reshape(75, 4, 128),
        damping.reshape(4, 128),
        orient.reshape(3, 4, 128),
        smoother.reshape(25, 4, 4, 16, 128),
        coarse_smoother.reshape(25, 2, 16, 128),
    )
    return out.reshape(5, 4, 4, 4, 2, 2, 128)


def solution(mesh):
    in_specs = (
        P(None, None, None, None, "gx", "gy", None),
        P(None, None, None, "gx", "gy", None),
        P("gx", "gy", None),
        P(None, "gx", "gy", None),
        P(None, None, None, None, None, "gx", "gy", None),
        P(None, None, None, None, None, "gx", "gy", None),
    )
    out_specs = P(None, None, None, None, "gx", "gy", None)
    return jax.shard_map(body, mesh=mesh, in_specs=in_specs, out_specs=out_specs, check_vma=False)
```

```python
import functools
import math

import jax
import jax.numpy as jnp
import numpy as np
from jax import lax
from jax.experimental import pallas as pl
from jax.experimental.pallas import tpu as pltpu
from jax.sharding import PartitionSpec as P

MESH = pl.DeviceIdType.MESH
OMEGA = 0.8
SHIFT = 2.0
F32 = jnp.float32


def lobatto4():
    points = np.array([-1.0, -1.0 / math.sqrt(5.0), 1.0 / math.sqrt(5.0), 1.0])
    weights = np.ones(4)
    for row in range(4):
        for col in range(4):
            if row != col:
                weights[row] /= points[row] - points[col]
    slopes = np.zeros((4, 4))
    for row in range(4):
        for col in range(4):
            if row != col:
                slopes[row, col] = weights[col] / weights[row] / (points[row] - points[col])
        slopes[row, row] = -np.sum(slopes[row])
    return points, slopes


POINTS, SLOPES = lobatto4()
INTERP = np.stack([(1.0 - POINTS) / 2.0, (1.0 + POINTS) / 2.0], 1)
OPEN = SLOPES.copy()
OPEN[0, 0] = OPEN[3, 3] = OPEN[1, 1] = OPEN[2, 2] = 0.0
LIFT = 3.0
EDGE = INTERP.T @ OPEN
P_NEAR, P_FAR = float(INTERP[1, 0]), float(INTERP[2, 0])


def dot_terms(coefs, values):
    total = None
    for coef, value in zip(coefs, values):
        coef = float(coef)
        if coef == 0.0:
            continue
        term = value if coef == 1.0 else coef * value
        total = term if total is None else total + term
    return total


def rows():
    return lax.broadcasted_iota(jnp.int32, (8, 128), 0)


def halves(top, bottom):
    return jnp.where(rows() < 4, jnp.full((8, 128), float(top), F32), jnp.full((8, 128), float(bottom), F32))


def sub_roll(value, shift):
    return pltpu.roll(value, shift % 8, 0)


def lane_roll(value, shift):
    return pltpu.roll(value, shift % 128, 1)


def pack_low(first, second, mask, step):
    return jnp.where(mask, first, sub_roll(second, step))


def pack_high(first, second, mask, step):
    return jnp.where(mask, sub_roll(first, -step), second)


def z_ghosts(traces, turned):
    count = len(traces)
    low = rows() < 4
    flip = jnp.logical_and(turned, rows() >= 4)
    out = []
    for a in range(count):
        swapped = sub_roll(jnp.where(flip, traces[count - 1 - a], traces[a]), 4)
        out.append(jnp.where(low, lane_roll(swapped, 1), lane_roll(swapped, -1)))
    return [jnp.where(flip, out[count - 1 - a], out[a]) for a in range(count)]


def restrict_c(first, second):
    low = rows() < 4
    ends = jnp.where(low, first, second)
    inner_swapped = jnp.where(low, second, first)
    inner = sub_roll(inner_swapped, 4)
    return ends, inner, inner_swapped, ends + P_NEAR * inner + P_FAR * inner_swapped


def restrict_line(values):
    low = values[0] + P_NEAR * values[1] + P_FAR * values[2]
    high = values[3] + P_NEAR * values[2] + P_FAR * values[1]
    return [low, high]


def prolong_line(values):
    return [
        values[0],
        P_NEAR * values[0] + P_FAR * values[1],
        P_FAR * values[0] + P_NEAR * values[1],
        values[1],
    ]


def swap_rows(value, step):
    return jnp.where((rows() & step) == 0, sub_roll(value, -step), sub_roll(value, step))


def kernel(
    src_hbm, jac_hbm, damp_hbm, flag_hbm, smo_hbm, csm_hbm, out,
    src, smo, csm, jraw, jn, draw, fraw, flags, dmp, kfine, csf, kface,
    q, acc, wx, wy, wz, rsrc, rcs, cloc, cpart, gcor, wc, crhs,
    s1, r1, s2, r2, s3, r3, sp, rp, sd, rd, sg, rg, in_sem, send_sem, recv_sem,
):
    nx, ny = lax.axis_size("gx"), lax.axis_size("gy")
    ix, iy = lax.axis_index("gx"), lax.axis_index("gy")
    x_next, x_prev = lax.rem(ix + 1, nx), lax.rem(ix + nx - 1, nx)
    y_next, y_prev = lax.rem(iy + 1, ny), lax.rem(iy + ny - 1, ny)
    partners = [(x_prev, iy), (x_next, iy), (ix, y_prev), (ix, y_next)]
    corners = [(x_prev, y_prev), (x_next, y_prev), (x_prev, y_next), (x_next, y_next)]

    barrier = pltpu.get_barrier_semaphore()
    for partner in partners:
        pl.semaphore_signal(barrier, inc=1, device_id=partner, device_id_type=MESH)

    loads = []

    def load(source, target):
        copy = pltpu.make_async_copy(source, target, in_sem.at[len(loads)])
        copy.start()
        loads.append(copy)
        return copy

    parts = {}
    flag_load = load(flag_hbm, fraw)
    damp_load = load(damp_hbm, draw)
    jac_load = load(jac_hbm, jraw)
    csm_load = load(csm_hbm, csm)
    for a in (0, 3, 1, 2):
        parts[a] = (load(src_hbm.at[:, a], src.at[:, a]), load(smo_hbm.at[:, a], smo.at[:, a]))

    started = []

    def remote(source, target, number, partner):
        copy = pltpu.make_async_remote_copy(
            src_ref=source, dst_ref=target, send_sem=send_sem.at[number], recv_sem=recv_sem.at[number],
            device_id=partner, device_id_type=MESH,
        )
        started.append(copy)
        return copy

    sends1 = [remote(s1.at[k], r1.at[k], k, partners[k]) for k in range(4)]
    sends2 = [remote(s2.at[k], r2.at[k], 4 + k, partners[k]) for k in range(4)]
    sends3 = [remote(s3.at[k], r3.at[k], 8 + k, partners[k]) for k in range(4)]
    sends_part = [remote(sp.at[k], rp.at[k], 12 + k, partners[k]) for k in range(4)]
    sends_corner = [remote(sd.at[k], rd.at[k], 16 + k, corners[k]) for k in range(4)]
    sends_face = [remote(sg.at[k], rg.at[k], 20 + k, partners[k]) for k in range(4)]

    low = rows() < 4
    x0 = (rows() & 2) == 0
    y0 = (rows() & 1) == 0
    zero = jnp.zeros((8, 128), F32)
    row4 = rows() & 3
    edge_rows = jnp.logical_or(row4 == 0, row4 == 3)

    def smooth(a, b, fields):
        outs = []
        for vo in range(5):
            pair = [None, None]
            for vi in range(5):
                block = smo[5 * vo + vi, a, b].astype(F32)
                for half in range(2):
                    term = block[8 * half : 8 * half + 8] * fields[vi][half]
                    pair[half] = term if vi == 0 else pair[half] + term
            outs.append(pair)
        return outs

    def first_pass(a, b):
        fields = [[src[v, a, b, 0], src[v, a, b, 1]] for v in range(5)]
        outs = smooth(a, b, fields)
        for v in range(5):
            q[v, a, b, 0] = outs[v][0]
            q[v, a, b, 1] = outs[v][1]

    flag_load.wait()
    damp_load.wait()
    for d in range(3):
        flags[d] = jnp.concatenate([fraw[d], fraw[d]], axis=0)
    fx, fy, fz = (flags[d] == 1 for d in range(3))
    damping = jnp.concatenate([draw[...], draw[...]], axis=0)
    dmp[0] = (OMEGA * LIFT) * damping
    dmp[1] = (OMEGA * 0.5) * damping
    dmp[2] = OMEGA * SHIFT + (OMEGA * 1.5) * damping
    dmp[3] = jnp.where(low, (OMEGA * LIFT) * damping, 0.0)
    dmp[4] = jnp.where(low, 0.0, (OMEGA * LIFT) * damping)
    for b in range(4):
        for a_end in range(2):
            faces = a_end + (1 if b in (0, 3) else 0)
            base = OMEGA * SHIFT + (OMEGA * LIFT * faces) * damping
            kfine[b, a_end, 0] = base + dmp[3]
            kfine[b, a_end, 1] = base + dmp[4]

    jac_load.wait()

    @pl.loop(0, 75, unroll=15)
    def _(i):
        block = jraw[i]
        jn[i] = (-OMEGA) * jnp.concatenate([block, block], axis=0)

    csm_load.wait()

    @pl.loop(0, 25, unroll=5)
    def _(i):
        for n in range(2):
            block = csm[i, n].astype(F32)
            csf[i, n, 0] = block[:8]
            csf[i, n, 1] = block[8:]

    half_damp, k_coarse, lift_damp = dmp[1], dmp[2], dmp[0]

    def pack_side(side, first, second):
        mask, step = (x0, 2) if side < 2 else (y0, 1)
        return (pack_low if side % 2 == 0 else pack_high)(first, second, mask, step)

    for side in range(4):
        own, other = (0, 1) if side < 2 else (1, 0)
        sign = -0.5 if side % 2 == 0 else 0.5
        cross_sign = jnp.where(y0 if side < 2 else x0, -0.5, 0.5)

        @pl.loop(0, 5, unroll=True)
        def _(row, side=side, own=own, other=other, sign=sign, cross_sign=cross_sign):
            for col in range(5):
                diag = jnp.where(row == col, half_damp, zero)
                face = diag + sign * jn[25 * own + 5 * row + col]
                cross = diag + cross_sign * jn[25 * other + 5 * row + col]
                kface[0, 5 * row + col] = pack_side(side, face, face)
                kface[1, 5 * row + col] = pack_side(side, cross, cross)

        @pl.loop(0, 5, unroll=True)
        def _(vo, side=side):
            blocks = []
            for m in range(5):
                if side < 2:
                    pair = [csf[5 * vo + m, side, j] for j in range(2)]
                else:
                    pair = [csf[5 * vo + m, i, side - 2] for i in range(2)]
                blocks.append(pack_side(side, pair[0], pair[1]))
            tiles = [[], []]
            for n in range(2):
                for vi in range(5):
                    total = blocks[0] * kface[n, vi]
                    for m in range(1, 5):
                        total = total + blocks[m] * kface[n, 5 * m + vi]
                    tiles[n].append(total)
            for vi in range(5):
                sg[side, 5 * vo + vi] = tiles[0][vi]
            for n in range(3):
                tile = tiles[1][2 * n]
                if n < 2:
                    other = tiles[1][2 * n + 1]
                    tile = jnp.where(
                        edge_rows, tile, jnp.where(row4 == 1, sub_roll(other, 1), sub_roll(other, -1))
                    )
                sg[side, 25 + 3 * vo + n] = tile

        for n, d in enumerate((own, other)):
            flag = jnp.where(flags[d] == 1, 1.0, 0.0)
            sg[side, 40 + n] = pack_side(side, flag, flag)

    for a in (0, 3):
        for copy in parts[a]:
            copy.wait()

        @pl.loop(0, 4)
        def _(b, a=a):
            first_pass(a, b)

    @pl.loop(0, 5, unroll=True)
    def _(v):
        for b in range(4):
            s1[0, v, b] = pack_low(q[v, 0, b, 0], q[v, 0, b, 1], x0, 2)
            hi = [jnp.where(fx, q[v, 3, 3 - b, h], q[v, 3, b, h]) for h in range(2)]
            s1[1, v, b] = pack_high(hi[0], hi[1], x0, 2)

    pl.semaphore_wait(barrier, 4)
    sends1[0].start()
    sends1[1].start()

    for a in (1, 2):
        for copy in parts[a]:
            copy.wait()

        @pl.loop(0, 4)
        def _(b, a=a):
            first_pass(a, b)

    @pl.loop(0, 5, unroll=True)
    def _(v):
        for a in range(4):
            s1[2, v, a] = pack_low(q[v, a, 0, 0], q[v, a, 0, 1], y0, 1)
            hi = [jnp.where(fy, q[v, 3 - a, 3, h], q[v, a, 3, h]) for h in range(2)]
            s1[3, v, a] = pack_high(hi[0], hi[1], y0, 1)

    sends1[2].start()
    sends1[3].start()

    for copy in sends_face:
        copy.start()

    c_first = [halves(OPEN[0, 1], OPEN[1, 0]), halves(OPEN[0, 2], OPEN[1, 3]), halves(OPEN[0, 3], OPEN[1, 2])]
    c_second = [halves(OPEN[2, 3], OPEN[3, 2]), halves(OPEN[2, 0], OPEN[3, 1]), halves(OPEN[2, 1], OPEN[3, 0])]
    c_ghost = [halves(-LIFT, 0.0), halves(0.0, LIFT)]

    @pl.loop(0, 20, unroll=4)
    def _(t):
        v, b = t // 4, t % 4
        first = [q[v, a, b, 0] for a in range(4)]
        second = [q[v, a, b, 1] for a in range(4)]
        for a in range(4):
            for h, line in enumerate((first, second)):
                wx[v, a, b, h] = dot_terms(OPEN[a], line)
        ghosts = z_ghosts([jnp.where(low, first[a], second[a]) for a in range(4)], fz)
        for a in range(4):
            a_end = 1 if a in (0, 3) else 0
            first_sw, second_sw = sub_roll(first[a], 4), sub_roll(second[a], 4)
            wz[v, a, b, 0] = (
                c_first[0] * first_sw + c_first[1] * second[a] + c_first[2] * second_sw + c_ghost[0] * ghosts[a]
            )
            wz[v, a, b, 1] = (
                c_second[0] * second_sw + c_second[1] * first[a] + c_second[2] * first_sw + c_ghost[1] * ghosts[a]
            )
            acc[v, a, b, 0] = src[v, a, b, 0] - kfine[b, a_end, 0] * first[a] + dmp[3] * ghosts[a]
            acc[v, a, b, 1] = src[v, a, b, 1] - kfine[b, a_end, 1] * second[a] + dmp[4] * ghosts[a]

    @pl.loop(0, 20, unroll=4)
    def _(t):
        v, a = t // 4, t % 4
        for h in range(2):
            line = [q[v, a, b, h] for b in range(4)]
            for b in range(4):
                wy[v, a, b, h] = dot_terms(OPEN[b], line)

    def mix(pair, directions, last):
        @pl.loop(0, 4)
        def _(b):
            total = [[[acc[v, a, b, h] for h in range(2)] for a in pair] for v in range(5)]
            for d in directions:
                w = (wx, wy, wz)[d]
                for vi in range(5):
                    flux = [[w[vi, a, b, h] for h in range(2)] for a in pair]
                    for vo in range(5):
                        weight = jn[25 * d + 5 * vo + vi]
                        for n in range(2):
                            for h in range(2):
                                total[vo][n][h] = total[vo][n][h] + weight * flux[n][h]
            for n, a in enumerate(pair):
                if last:
                    outs = smooth(a, b, [total[v][n] for v in range(5)])
                for v in range(5):
                    for h in range(2):
                        if last:
                            q[v, a, b, h] = q[v, a, b, h] + outs[v][h]
                        else:
                            acc[v, a, b, h] = total[v][n][h]

    mix((0, 3), (2,), False)
    mix((1, 2), (0, 2), False)

    @pl.loop(0, 5, unroll=True)
    def _(v):
        by_a = []
        for a in range(4):
            by_a.append(restrict_line([restrict_c(src[v, a, b, 0], src[v, a, b, 1])[3] for b in range(4)]))
        for j in range(2):
            for i, value in enumerate(restrict_line([by_a[a][j] for a in range(4)])):
                rsrc[v, i, j] = value

    sends1[2].wait_recv()
    sends1[3].wait_recv()

    @pl.loop(0, 5, unroll=True)
    def _(v):
        for h in range(2):
            lo = [q[v, a, 0, h] for a in range(4)]
            hi = [q[v, a, 3, h] for a in range(4)]
            right = []
            for a in range(4):
                packed = r1[2, v, a]
                right.append(jnp.where(y0, sub_roll(lo[a], -1), sub_roll(packed, 1) if h == 0 else packed))
            for a in range(4):
                packed = r1[3, v, a]
                hi_turned = jnp.where(fy, hi[3 - a], hi[a])
                left = jnp.where(y0, packed if h == 0 else sub_roll(packed, -1), sub_roll(hi_turned, 1))
                ghost = jnp.where(fy, right[3 - a], right[a])
                wy[v, a, 0, h] = wy[v, a, 0, h] - LIFT * left
                wy[v, a, 3, h] = wy[v, a, 3, h] + LIFT * ghost
                acc[v, a, 0, h] = acc[v, a, 0, h] + lift_damp * left
                acc[v, a, 3, h] = acc[v, a, 3, h] + lift_damp * ghost

    mix((0, 3), (1,), False)
    mix((1, 2), (1,), True)

    def restrict_c_into(v, a_list):
        for a in a_list:
            for b in range(4):
                rcs[v, a, b] = restrict_c(q[v, a, b, 0], q[v, a, b, 1])[3]

    @pl.loop(0, 5, unroll=True)
    def _(v):
        restrict_c_into(v, (1, 2))

    sends1[0].wait_recv()
    sends1[1].wait_recv()

    @pl.loop(0, 5, unroll=True)
    def _(v):
        for h in range(2):
            lo = [q[v, 0, b, h] for b in range(4)]
            hi = [q[v, 3, b, h] for b in range(4)]
            right = []
            for b in range(4):
                packed = r1[0, v, b]
                right.append(jnp.where(x0, sub_roll(lo[b], -2), sub_roll(packed, 2) if h == 0 else packed))
            for b in range(4):
                packed = r1[1, v, b]
                hi_turned = jnp.where(fx, hi[3 - b], hi[b])
                left = jnp.where(x0, packed if h == 0 else sub_roll(packed, -2), sub_roll(hi_turned, 2))
                ghost = jnp.where(fx, right[3 - b], right[b])
                wx[v, 0, b, h] = wx[v, 0, b, h] - LIFT * left
                wx[v, 3, b, h] = wx[v, 3, b, h] + LIFT * ghost
                acc[v, 0, b, h] = acc[v, 0, b, h] + lift_damp * left
                acc[v, 3, b, h] = acc[v, 3, b, h] + lift_damp * ghost

    mix((0, 3), (0,), True)

    def traces_of(field):
        return [
            [[field[v][0][n] for n in range(2)] for v in range(5)],
            [[field[v][1][n] for n in range(2)] for v in range(5)],
            [[field[v][n][0] for n in range(2)] for v in range(5)],
            [[field[v][n][1] for n in range(2)] for v in range(5)],
        ]

    def pack_traces(traces, target, turn):
        for v in range(5):
            for side in range(4):
                pair = traces[side][v]
                if turn and side % 2 == 1:
                    flip = fx if side < 2 else fy
                    pair = [jnp.where(flip, pair[1 - n], pair[n]) for n in range(2)]
                target[side, v] = pack_side(side, pair[0], pair[1])

    traces = [[None] * 5 for _ in range(4)]
    for v in range(5):
        restrict_c_into(v, (0, 3))
        for slot, a in ((0, 0), (1, 3)):
            traces[slot][v] = restrict_line([rcs[v, a, b] for b in range(4)])
        for slot, b in ((2, 0), (3, 3)):
            traces[slot][v] = restrict_line([rcs[v, a, b] for a in range(4)])
    pack_traces(traces, s2, True)

    for copy in sends2:
        copy.start()

    def inner_ghosts(lo, hi, mask, step, flip):
        right = [jnp.where(mask, sub_roll(value, -step), zero) for value in lo]
        right = [jnp.where(flip, right[1 - n], right[n]) for n in range(2)]
        hi = [jnp.where(flip, hi[1 - n], hi[n]) for n in range(2)]
        left = [jnp.where(mask, zero, sub_roll(value, step)) for value in hi]
        return left, right

    def coarse_sweep():
        total = [[[crhs[v, i, j] for j in range(2)] for i in range(2)] for v in range(5)]
        for d in range(3):
            for vi in range(5):
                flux = [[wc[d, vi, i, j] for j in range(2)] for i in range(2)]
                for vo in range(5):
                    weight = jn[25 * d + 5 * vo + vi]
                    for i in range(2):
                        for j in range(2):
                            total[vo][i][j] = total[vo][i][j] + weight * flux[i][j]
        outs = [[[None, None] for _ in range(2)] for _ in range(5)]
        for vo in range(5):
            for vi in range(5):
                for i in range(2):
                    for j in range(2):
                        term = csf[5 * vo + vi, i, j] * total[vi][i][j]
                        outs[vo][i][j] = term if vi == 0 else outs[vo][i][j] + term
        return outs

    e_ends = halves(EDGE[0, 0], EDGE[1, 3])
    e_ends_sw = halves(EDGE[0, 3], EDGE[1, 0])
    e_inner = halves(EDGE[0, 1], EDGE[1, 2])
    e_inner_sw = halves(EDGE[0, 2], EDGE[1, 1])
    z_lift = halves(-LIFT, LIFT)

    for v in range(5):
        rbc = [restrict_line([rcs[v, a, b] for b in range(4)]) for a in range(4)]
        rac = [restrict_line([rcs[v, a, b] for a in range(4)]) for b in range(4)]
        ra = [[restrict_line([q[v, a, b, h] for a in range(4)]) for b in range(4)] for h in range(2)]
        ends_of = [[None, None], [None, None]]
        rhs = [[None, None], [None, None]]
        w = [[[None, None], [None, None]] for _ in range(3)]
        for i in range(2):
            first = restrict_line([ra[0][b][i] for b in range(4)])
            second = restrict_line([ra[1][b][i] for b in range(4)])
            for j in range(2):
                w[0][i][j] = dot_terms(EDGE[i], [rbc[a][j] for a in range(4)])
                w[1][i][j] = dot_terms(EDGE[j], [rac[b][i] for b in range(4)])
                ends, inner, inner_sw, full = restrict_c(first[j], second[j])
                ends_of[j][i] = ends
                w[2][i][j] = (
                    e_ends * ends + e_ends_sw * sub_roll(ends, 4) + e_inner * inner + e_inner_sw * inner_sw
                )
                rhs[i][j] = rsrc[v, i, j] - (OMEGA * SHIFT) * full
        for j in range(2):
            ghosts = z_ghosts(ends_of[j], fz)
            for i in range(2):
                w[2][i][j] = w[2][i][j] + z_lift * ghosts[i]
                rhs[i][j] = rhs[i][j] + lift_damp * (ghosts[i] - ends_of[j][i])
        left, right = inner_ghosts(traces[0][v], traces[1][v], x0, 2, fx)
        for j in range(2):
            w[0][0][j] = w[0][0][j] - LIFT * left[j]
            w[0][1][j] = w[0][1][j] + LIFT * right[j]
            rhs[0][j] = rhs[0][j] + lift_damp * (left[j] - traces[0][v][j])
            rhs[1][j] = rhs[1][j] + lift_damp * (right[j] - traces[1][v][j])
        left, right = inner_ghosts(traces[2][v], traces[3][v], y0, 1, fy)
        for i in range(2):
            w[1][i][0] = w[1][i][0] - LIFT * left[i]
            w[1][i][1] = w[1][i][1] + LIFT * right[i]
            rhs[i][0] = rhs[i][0] + lift_damp * (left[i] - traces[2][v][i])
            rhs[i][1] = rhs[i][1] + lift_damp * (right[i] - traces[3][v][i])
        for i in range(2):
            for j in range(2):
                crhs[v, i, j] = rhs[i][j]
                for d in range(3):
                    wc[d, v, i, j] = w[d][i][j]

    outs = coarse_sweep()
    for v in range(5):
        for i in range(2):
            for j in range(2):
                cloc[v, i, j] = outs[v][i][j]

    @pl.loop(0, 20, unroll=4)
    def _(t):
        v, b = t // 4, t % 4
        for a in range(4):
            for h in range(2):
                out[v, a, b, h] = OMEGA * q[v, a, b, h]

    def face_product(ref, side, vectors):
        outs = []
        for vo in range(5):
            total = ref[side, 5 * vo] * vectors[0]
            for vi in range(1, 5):
                total = total + ref[side, 5 * vo + vi] * vectors[vi]
            outs.append(total)
        return outs

    def corner_product(ref, side, vectors):
        moved = [jnp.where(edge_rows, zero, jnp.where(row4 == 1, sub_roll(x, 1), sub_roll(x, -1))) for x in vectors]
        joined = [vectors[0] + moved[1], vectors[2] + moved[3], vectors[4]]
        outs = []
        for vo in range(5):
            total = ref[side, 25 + 3 * vo] * joined[0]
            for n in range(1, 3):
                total = total + ref[side, 25 + 3 * vo + n] * joined[n]
            back = total + jnp.where(row4 == 0, sub_roll(total, -1), sub_roll(total, 1))
            outs.append(jnp.where(edge_rows, back, zero))
        return outs

    def own_ghost(side, value):
        if side % 2 == 0:
            return value
        return jnp.where(sg[side, 40] == 1.0, swap_rows(value, 2 if side < 2 else 1), value)

    def face_terms(ghosts):
        pairs = [[None] * 5 for _ in range(4)]
        for side in range(4):
            mask, step = (x0, 2) if side < 2 else (y0, 1)
            for v, delta in enumerate(face_product(sg, side, ghosts[side])):
                if side % 2 == 0:
                    pairs[side][v] = [
                        jnp.where(mask, delta, zero), jnp.where(mask, sub_roll(delta, -step), zero)
                    ]
                else:
                    pairs[side][v] = [
                        jnp.where(mask, zero, sub_roll(delta, step)), jnp.where(mask, zero, delta)
                    ]
        return [[[pairs[i][v][j] + pairs[2 + j][v][i] for j in range(2)] for i in range(2)] for v in range(5)]

    def inner_operator(field):
        for v in range(5):
            here = field[v]
            rhs = [[(-k_coarse) * here[i][j] for j in range(2)] for i in range(2)]
            for j in range(2):
                ghosts = z_ghosts([here[i][j] for i in range(2)], fz)
                for i in range(2):
                    swapped = sub_roll(here[i][j], 4)
                    wc[2, v, i, j] = jnp.where(low, 0.5, -0.5) * (swapped - ghosts[i])
                    rhs[i][j] = rhs[i][j] + half_damp * ghosts[i]
            left, right = inner_ghosts(here[0], here[1], x0, 2, fx)
            for j in range(2):
                wc[0, v, 0, j] = 0.5 * (here[1][j] - left[j])
                wc[0, v, 1, j] = 0.5 * (right[j] - here[0][j])
                rhs[0][j] = rhs[0][j] + half_damp * left[j]
                rhs[1][j] = rhs[1][j] + half_damp * right[j]
            left, right = inner_ghosts([here[i][0] for i in range(2)], [here[i][1] for i in range(2)], y0, 1, fy)
            for i in range(2):
                wc[1, v, i, 0] = 0.5 * (here[i][1] - left[i])
                wc[1, v, i, 1] = 0.5 * (right[i] - here[i][0])
                rhs[i][0] = rhs[i][0] + half_damp * left[i]
                rhs[i][1] = rhs[i][1] + half_damp * right[i]
            for i in range(2):
                for j in range(2):
                    crhs[v, i, j] = rhs[i][j]
        return coarse_sweep()

    def combine(function, *fields):
        return [
            [[function(*(f[v][i][j] for f in fields)) for j in range(2)] for i in range(2)] for v in range(5)
        ]

    def load_field(ref):
        return [[[ref[v, i, j] for j in range(2)] for i in range(2)] for v in range(5)]

    for copy in sends2:
        copy.wait_recv()
    terms = face_terms([[own_ghost(side, r2[side ^ 1, v]) for v in range(5)] for side in range(4)])
    coarse = combine(lambda x, y: x + 6.0 * y, load_field(cloc), terms)
    pack_traces(traces_of(coarse), s3, True)
    for v in range(5):
        x_lo, x_hi, y_lo, y_hi = (s3[side, v] for side in range(4))
        sd[0, v] = jnp.where(x0, y_lo, jnp.where(row4 == 2, x_lo, sub_roll(x_lo, 3)))
        sd[1, v] = jnp.where(x0, x_hi, y_lo)
        sd[2, v] = jnp.where(row4 == 0, y_hi, x_lo)
        sd[3, v] = jnp.where(row4 == 3, y_hi, sub_roll(x_hi, -3))

    for copy in sends_corner + sends3:
        copy.start()

    outs = inner_operator(coarse)
    partial = combine(lambda x, y: 2.0 * x + y, coarse, outs)
    pack_traces(traces_of(partial), sp, False)

    for copy in sends_part:
        copy.start()

    for v in range(5):
        for i in range(2):
            for j in range(2):
                cloc[v, i, j] = coarse[v][i][j]
                cpart[v, i, j] = partial[v][i][j]

    for copy in sends_face:
        copy.wait_recv()

    for side in range(4):
        mine = [s3[side, v] for v in range(5)]
        if side % 2 == 0:
            turn = rg[side ^ 1, 40] == 1.0
            mine = [jnp.where(turn, swap_rows(value, 2 if side < 2 else 1), value) for value in mine]
        for v, value in enumerate(face_product(rg, side ^ 1, mine)):
            gcor[side, v] = value

    for copy in sends3:
        copy.wait_recv()

    terms = face_terms([[own_ghost(side, r3[side ^ 1, v]) for v in range(5)] for side in range(4)])
    middle = combine(lambda x, y: x + y, load_field(cpart), terms)
    outs = inner_operator(middle)
    coarse = combine(lambda x, y, z: x + y + z, load_field(cloc), middle, outs)

    for copy in sends_corner:
        copy.wait_recv()

    def corner_ghosts(side, v):
        prev_prev, next_prev, prev_next, next_next = (rd[k, v] for k in (3, 2, 1, 0))
        flip = rg[side ^ 1, 41] == 1.0
        if side == 1:
            lower = next_prev
            upper = jnp.where(flip, sub_roll(next_next, 2), sub_roll(next_next, 3))
        elif side == 0:
            lower = sub_roll(prev_prev, -3)
            upper = jnp.where(flip, sub_roll(prev_next, 1), prev_next)
        elif side == 3:
            lower = prev_next
            upper = jnp.where(flip, sub_roll(next_next, 1), next_next)
        else:
            lower = prev_prev
            upper = jnp.where(flip, sub_roll(next_prev, 2), next_prev)
        return jnp.where(row4 == 0, lower, jnp.where(row4 == 3, upper, zero))

    beside = [corner_product(rg, side ^ 1, [corner_ghosts(side, v) for v in range(5)]) for side in range(4)]

    for copy in sends_part:
        copy.wait_recv()

    ghosts = []
    for side in range(4):
        values = [rp[side ^ 1, v] + (gcor[side, v] + beside[side][v]) for v in range(5)]
        if side % 2 == 0:
            turn = rg[side ^ 1, 40] == 1.0
            values = [jnp.where(turn, swap_rows(value, 2 if side < 2 else 1), value) for value in values]
        else:
            values = [own_ghost(side, value) for value in values]
        ghosts.append(values)
    coarse = combine(lambda x, y: x + y, coarse, face_terms(ghosts))

    t_first = [halves(OMEGA, OMEGA * P_FAR), halves(0.0, OMEGA * P_NEAR)]
    t_second = [halves(OMEGA * P_FAR, OMEGA), halves(OMEGA * P_NEAR, 0.0)]

    for v in range(5):
        by_a = [prolong_line([coarse[v][i][j] for i in range(2)]) for j in range(2)]
        for a in range(4):
            for b, value in enumerate(prolong_line([by_a[j][a] for j in range(2)])):
                swapped = sub_roll(value, 4)
                out[v, a, b, 0] = out[v, a, b, 0] + (t_first[0] * value + t_first[1] * swapped)
                out[v, a, b, 1] = out[v, a, b, 1] + (t_second[0] * value + t_second[1] * swapped)

    for copy in started:
        copy.wait_send()


def body(source, jacobian, damping, orient, smoother, coarse_smoother):
    field = (5, 4, 4, 2, 8, 128)
    vmem = pltpu.VMEM
    hbm = pl.BlockSpec(memory_space=pltpu.HBM)
    out = pl.pallas_call(
        kernel,
        out_shape=pltpu.VMEM(field, F32),
        in_specs=[hbm] * 6,
        out_specs=pl.BlockSpec(memory_space=pltpu.VMEM),
        scratch_shapes=[
            vmem(field, F32),
            vmem((25, 4, 4, 16, 128), jnp.bfloat16),
            vmem((25, 2, 16, 128), jnp.bfloat16),
            vmem((75, 4, 128), F32),
            vmem((75, 8, 128), F32),
            vmem((4, 128), F32),
            vmem((3, 4, 128), jnp.int32),
            vmem((3, 8, 128), jnp.int32),
            vmem((5, 8, 128), F32),
            vmem((4, 2, 2, 8, 128), F32),
            vmem((25, 2, 2, 8, 128), F32),
            vmem((2, 25, 8, 128), F32),
            vmem(field, F32),
            vmem(field, F32),
            vmem(field, F32),
            vmem(field, F32),
            vmem(field, F32),
            vmem((5, 2, 2, 8, 128), F32),
            vmem((5, 4, 4, 8, 128), F32),
            vmem((5, 2, 2, 8, 128), F32),
            vmem((5, 2, 2, 8, 128), F32),
            vmem((4, 5, 8, 128), F32),
            vmem((3, 5, 2, 2, 8, 128), F32),
            vmem((5, 2, 2, 8, 128), F32),
            vmem((4, 5, 4, 8, 128), F32),
            vmem((4, 5, 4, 8, 128), F32),
            vmem((4, 5, 8, 128), F32),
            vmem((4, 5, 8, 128), F32),
            vmem((4, 5, 8, 128), F32),
            vmem((4, 5, 8, 128), F32),
            vmem((4, 5, 8, 128), F32),
            vmem((4, 5, 8, 128), F32),
            vmem((4, 5, 8, 128), F32),
            vmem((4, 5, 8, 128), F32),
            vmem((4, 42, 8, 128), F32),
            vmem((4, 42, 8, 128), F32),
            pltpu.SemaphoreType.DMA((12,)),
            pltpu.SemaphoreType.DMA((24,)),
            pltpu.SemaphoreType.DMA((24,)),
        ],
        compiler_params=pltpu.CompilerParams(collective_id=0, has_side_effects=True),
    )(
        source.reshape(field),
        jacobian.reshape(75, 4, 128),
        damping.reshape(4, 128),
        orient.reshape(3, 4, 128),
        smoother.reshape(25, 4, 4, 16, 128),
        coarse_smoother.reshape(25, 2, 16, 128),
    )
    return out.reshape(5, 4, 4, 4, 2, 2, 128)


def solution(mesh):
    in_specs = (
        P(None, None, None, None, "gx", "gy", None),
        P(None, None, None, "gx", "gy", None),
        P("gx", "gy", None),
        P(None, "gx", "gy", None),
        P(None, None, None, None, None, "gx", "gy", None),
        P(None, None, None, None, None, "gx", "gy", None),
    )
    out_specs = P(None, None, None, None, "gx", "gy", None)
    return jax.shard_map(body, mesh=mesh, in_specs=in_specs, out_specs=out_specs, check_vma=False)
```

```python
import functools
import math

import jax
import jax.numpy as jnp
import numpy as np
from jax import lax
from jax.experimental import pallas as pl
from jax.experimental.pallas import tpu as pltpu
from jax.sharding import PartitionSpec as P

MESH = pl.DeviceIdType.MESH
OMEGA = 0.8
SHIFT = 2.0
F32 = jnp.float32


def lobatto4():
    points = np.array([-1.0, -1.0 / math.sqrt(5.0), 1.0 / math.sqrt(5.0), 1.0])
    weights = np.ones(4)
    for row in range(4):
        for col in range(4):
            if row != col:
                weights[row] /= points[row] - points[col]
    slopes = np.zeros((4, 4))
    for row in range(4):
        for col in range(4):
            if row != col:
                slopes[row, col] = weights[col] / weights[row] / (points[row] - points[col])
        slopes[row, row] = -np.sum(slopes[row])
    return points, slopes


POINTS, SLOPES = lobatto4()
INTERP = np.stack([(1.0 - POINTS) / 2.0, (1.0 + POINTS) / 2.0], 1)
OPEN = SLOPES.copy()
OPEN[0, 0] = OPEN[3, 3] = OPEN[1, 1] = OPEN[2, 2] = 0.0
LIFT = 3.0
EDGE = INTERP.T @ OPEN
P_NEAR, P_FAR = float(INTERP[1, 0]), float(INTERP[2, 0])


def dot_terms(coefs, values):
    total = None
    for coef, value in zip(coefs, values):
        coef = float(coef)
        if coef == 0.0:
            continue
        term = value if coef == 1.0 else coef * value
        total = term if total is None else total + term
    return total


def rows():
    return lax.broadcasted_iota(jnp.int32, (8, 128), 0)


def halves(top, bottom):
    return jnp.where(rows() < 4, jnp.full((8, 128), float(top), F32), jnp.full((8, 128), float(bottom), F32))


def sub_roll(value, shift):
    return pltpu.roll(value, shift % 8, 0)


def lane_roll(value, shift):
    return pltpu.roll(value, shift % 128, 1)


def pack_low(first, second, mask, step):
    return jnp.where(mask, first, sub_roll(second, step))


def pack_high(first, second, mask, step):
    return jnp.where(mask, sub_roll(first, -step), second)


def z_ghosts(traces, turned):
    count = len(traces)
    low = rows() < 4
    flip = jnp.logical_and(turned, rows() >= 4)
    out = []
    for a in range(count):
        swapped = sub_roll(jnp.where(flip, traces[count - 1 - a], traces[a]), 4)
        out.append(jnp.where(low, lane_roll(swapped, 1), lane_roll(swapped, -1)))
    return [jnp.where(flip, out[count - 1 - a], out[a]) for a in range(count)]


def restrict_c(first, second):
    low = rows() < 4
    ends = jnp.where(low, first, second)
    inner_swapped = jnp.where(low, second, first)
    inner = sub_roll(inner_swapped, 4)
    return ends, inner, inner_swapped, ends + P_NEAR * inner + P_FAR * inner_swapped


def restrict_line(values):
    low = values[0] + P_NEAR * values[1] + P_FAR * values[2]
    high = values[3] + P_NEAR * values[2] + P_FAR * values[1]
    return [low, high]


def prolong_line(values):
    return [
        values[0],
        P_NEAR * values[0] + P_FAR * values[1],
        P_FAR * values[0] + P_NEAR * values[1],
        values[1],
    ]


CORNERS = ((2, 0, 0, 0), (2, 1, 3, 0), (3, 0, 0, 3), (3, 1, 3, 3))


def swap_rows(value, step):
    return jnp.where((rows() & step) == 0, sub_roll(value, -step), sub_roll(value, step))


def kernel(
    src_hbm, jac_hbm, damp_hbm, flag_hbm, smo_hbm, csm_hbm, out,
    src, smo, csm, jraw, jn, draw, fraw, flags, dmp, kfine, csf, kface,
    q, acc, wx, wy, wz, rsrc, rcs, cloc, cpart, gcor, wc, crhs,
    s1, r1, s2, r2, s3, r3, sp, rp, sd, rd, sg, rg, in_sem, send_sem, recv_sem,
):
    nx, ny = lax.axis_size("gx"), lax.axis_size("gy")
    ix, iy = lax.axis_index("gx"), lax.axis_index("gy")
    x_next, x_prev = lax.rem(ix + 1, nx), lax.rem(ix + nx - 1, nx)
    y_next, y_prev = lax.rem(iy + 1, ny), lax.rem(iy + ny - 1, ny)
    partners = [(x_prev, iy), (x_next, iy), (ix, y_prev), (ix, y_next)]
    corners = [(x_prev, y_prev), (x_next, y_prev), (x_prev, y_next), (x_next, y_next)]

    barrier = pltpu.get_barrier_semaphore()
    for partner in partners:
        pl.semaphore_signal(barrier, inc=1, device_id=partner, device_id_type=MESH)

    loads = []

    def load(source, target):
        copy = pltpu.make_async_copy(source, target, in_sem.at[len(loads)])
        copy.start()
        loads.append(copy)
        return copy

    parts = {}
    flag_load = load(flag_hbm, fraw)
    damp_load = load(damp_hbm, draw)
    jac_load = load(jac_hbm, jraw)
    csm_load = load(csm_hbm, csm)
    for a in (0, 3, 1, 2):
        parts[a] = (load(src_hbm.at[:, a], src.at[:, a]), load(smo_hbm.at[:, a], smo.at[:, a]))

    started = []

    def remote(source, target, number, partner):
        copy = pltpu.make_async_remote_copy(
            src_ref=source, dst_ref=target, send_sem=send_sem.at[number], recv_sem=recv_sem.at[number],
            device_id=partner, device_id_type=MESH,
        )
        started.append(copy)
        return copy

    sends1 = [[remote(s1.at[k, h], r1.at[k, h], 2 * k + h, partners[k]) for h in range(2)] for k in range(2)]
    sends1 += [[remote(s1.at[k], r1.at[k], 2 * k, partners[k])] for k in range(2, 4)]
    sends2 = [remote(s2.at[k], r2.at[k], 8 + k, partners[k]) for k in range(4)]
    sends3 = [remote(s3.at[k], r3.at[k], 12 + k, partners[k]) for k in range(4)]
    sends_part = [remote(sp.at[k], rp.at[k], 16 + k, partners[k]) for k in range(4)]
    sends_corner = [remote(sd.at[k], rd.at[k], 20 + k, corners[k]) for k in range(4)]
    sends_face = [remote(sg.at[k], rg.at[k], 24 + k, partners[k]) for k in range(4)]

    low = rows() < 4
    x0 = (rows() & 2) == 0
    y0 = (rows() & 1) == 0
    zero = jnp.zeros((8, 128), F32)
    row4 = rows() & 3

    def smooth(a, b, fields):
        outs = []
        for vo in range(5):
            pair = [None, None]
            for vi in range(5):
                block = smo[5 * vo + vi, a, b].astype(F32)
                for half in range(2):
                    term = block[8 * half : 8 * half + 8] * fields[vi][half]
                    pair[half] = term if vi == 0 else pair[half] + term
            outs.append(pair)
        return outs

    def first_pass(a, b):
        fields = [[src[v, a, b, 0], src[v, a, b, 1]] for v in range(5)]
        outs = smooth(a, b, fields)
        for v in range(5):
            q[v, a, b, 0] = outs[v][0]
            q[v, a, b, 1] = outs[v][1]

    flag_load.wait()
    damp_load.wait()
    for d in range(3):
        flags[d] = jnp.concatenate([fraw[d], fraw[d]], axis=0)
    fx, fy, fz = (flags[d] == 1 for d in range(3))
    damping = jnp.concatenate([draw[...], draw[...]], axis=0)
    dmp[0] = (OMEGA * LIFT) * damping
    dmp[1] = (OMEGA * 0.5) * damping
    dmp[2] = OMEGA * SHIFT + (OMEGA * 1.5) * damping
    dmp[3] = jnp.where(low, (OMEGA * LIFT) * damping, 0.0)
    dmp[4] = jnp.where(low, 0.0, (OMEGA * LIFT) * damping)
    for b in range(4):
        for a_end in range(2):
            faces = a_end + (1 if b in (0, 3) else 0)
            base = OMEGA * SHIFT + (OMEGA * LIFT * faces) * damping
            kfine[b, a_end, 0] = base + dmp[3]
            kfine[b, a_end, 1] = base + dmp[4]

    jac_load.wait()

    @pl.loop(0, 75, unroll=15)
    def _(i):
        block = jraw[i]
        jn[i] = (-OMEGA) * jnp.concatenate([block, block], axis=0)

    csm_load.wait()

    @pl.loop(0, 25, unroll=5)
    def _(i):
        for n in range(2):
            block = csm[i, n].astype(F32)
            csf[i, n, 0] = block[:8]
            csf[i, n, 1] = block[8:]

    half_damp, k_coarse, lift_damp = dmp[1], dmp[2], dmp[0]

    def pack_side(side, first, second):
        mask, step = (x0, 2) if side < 2 else (y0, 1)
        return (pack_low if side % 2 == 0 else pack_high)(first, second, mask, step)

    for side in range(4):
        own = 0 if side < 2 else 1
        sign = -0.5 if side % 2 == 0 else 0.5

        @pl.loop(0, 5, unroll=True)
        def _(row, side=side, own=own, sign=sign):
            for col in range(5):
                diag = jnp.where(row == col, half_damp, zero)
                face = diag + sign * jn[25 * own + 5 * row + col]
                kface[5 * row + col] = pack_side(side, face, face)

        @pl.loop(0, 5, unroll=True)
        def _(vo, side=side):
            blocks = []
            for m in range(5):
                if side < 2:
                    pair = [csf[5 * vo + m, side, j] for j in range(2)]
                else:
                    pair = [csf[5 * vo + m, i, side - 2] for i in range(2)]
                blocks.append(pack_side(side, pair[0], pair[1]))
            for vi in range(5):
                total = blocks[0] * kface[vi]
                for m in range(1, 5):
                    total = total + blocks[m] * kface[5 * m + vi]
                sg[side, 5 * vo + vi] = total

        flag = jnp.where(flags[own] == 1, 1.0, 0.0)
        sg[side, 25] = pack_side(side, flag, flag)

    for a in (0, 3):
        for copy in parts[a]:
            copy.wait()

        @pl.loop(0, 4)
        def _(b, a=a):
            first_pass(a, b)

    HALF = {0: (0, 0), 3: (0, 1), 1: (1, 0), 2: (1, 1)}

    @pl.loop(0, 5, unroll=True)
    def _(v):
        for b in range(4):
            half, place = HALF[b]
            s1[0, half, v, place] = pack_low(q[v, 0, b, 0], q[v, 0, b, 1], x0, 2)
            hi = [jnp.where(fx, q[v, 3, 3 - b, h], q[v, 3, b, h]) for h in range(2)]
            s1[1, half, v, place] = pack_high(hi[0], hi[1], x0, 2)

    pl.semaphore_wait(barrier, 4)
    for half in range(2):
        for k in range(2):
            sends1[k][half].start()

    for a in (1, 2):
        for copy in parts[a]:
            copy.wait()

        @pl.loop(0, 4)
        def _(b, a=a):
            first_pass(a, b)

    @pl.loop(0, 5, unroll=True)
    def _(v):
        for a in range(4):
            s1[2, a // 2, v, a % 2] = pack_low(q[v, a, 0, 0], q[v, a, 0, 1], y0, 1)
            hi = [jnp.where(fy, q[v, 3 - a, 3, h], q[v, a, 3, h]) for h in range(2)]
            s1[3, a // 2, v, a % 2] = pack_high(hi[0], hi[1], y0, 1)

    sends1[2][0].start()
    sends1[3][0].start()

    for copy in sends_face:
        copy.start()

    c_first = [halves(OPEN[0, 1], OPEN[1, 0]), halves(OPEN[0, 2], OPEN[1, 3]), halves(OPEN[0, 3], OPEN[1, 2])]
    c_second = [halves(OPEN[2, 3], OPEN[3, 2]), halves(OPEN[2, 0], OPEN[3, 1]), halves(OPEN[2, 1], OPEN[3, 0])]
    c_ghost = [halves(-LIFT, 0.0), halves(0.0, LIFT)]

    @pl.loop(0, 20, unroll=4)
    def _(t):
        v, b = t // 4, t % 4
        first = [q[v, a, b, 0] for a in range(4)]
        second = [q[v, a, b, 1] for a in range(4)]
        for a in range(4):
            for h, line in enumerate((first, second)):
                wx[v, a, b, h] = dot_terms(OPEN[a], line)
        ghosts = z_ghosts([jnp.where(low, first[a], second[a]) for a in range(4)], fz)
        for a in range(4):
            a_end = 1 if a in (0, 3) else 0
            first_sw, second_sw = sub_roll(first[a], 4), sub_roll(second[a], 4)
            wz[v, a, b, 0] = (
                c_first[0] * first_sw + c_first[1] * second[a] + c_first[2] * second_sw + c_ghost[0] * ghosts[a]
            )
            wz[v, a, b, 1] = (
                c_second[0] * second_sw + c_second[1] * first[a] + c_second[2] * first_sw + c_ghost[1] * ghosts[a]
            )
            acc[v, a, b, 0] = src[v, a, b, 0] - kfine[b, a_end, 0] * first[a] + dmp[3] * ghosts[a]
            acc[v, a, b, 1] = src[v, a, b, 1] - kfine[b, a_end, 1] * second[a] + dmp[4] * ghosts[a]

    @pl.loop(0, 20, unroll=4)
    def _(t):
        v, a = t // 4, t % 4
        for h in range(2):
            line = [q[v, a, b, h] for b in range(4)]
            for b in range(4):
                wy[v, a, b, h] = dot_terms(OPEN[b], line)

    def mix_at(b, pair, directions, last):
        total = [[[acc[v, a, b, h] for h in range(2)] for a in pair] for v in range(5)]
        for d in directions:
            w = (wx, wy, wz)[d]
            for vi in range(5):
                flux = [[w[vi, a, b, h] for h in range(2)] for a in pair]
                for vo in range(5):
                    weight = jn[25 * d + 5 * vo + vi]
                    for n in range(2):
                        for h in range(2):
                            total[vo][n][h] = total[vo][n][h] + weight * flux[n][h]
        for n, a in enumerate(pair):
            if last:
                outs = smooth(a, b, [total[v][n] for v in range(5)])
            for v in range(5):
                for h in range(2):
                    if last:
                        q[v, a, b, h] = q[v, a, b, h] + outs[v][h]
                    else:
                        acc[v, a, b, h] = total[v][n][h]

    def mix(pair, directions, last):
        @pl.loop(0, 4)
        def _(b):
            mix_at(b, pair, directions, last)

    mix((0, 3), (2,), False)
    mix((1, 2), (0, 2), False)

    @pl.loop(0, 5, unroll=True)
    def _(v):
        by_a = []
        for a in range(4):
            by_a.append(restrict_line([restrict_c(src[v, a, b, 0], src[v, a, b, 1])[3] for b in range(4)]))
        for j in range(2):
            for i, value in enumerate(restrict_line([by_a[a][j] for a in range(4)])):
                rsrc[v, i, j] = value

    sends1[2][0].wait_recv()
    sends1[3][0].wait_recv()

    @pl.loop(0, 5, unroll=True)
    def _(v):
        for h in range(2):
            lo = [q[v, a, 0, h] for a in range(4)]
            hi = [q[v, a, 3, h] for a in range(4)]
            right = []
            for a in range(4):
                packed = r1[2, a // 2, v, a % 2]
                right.append(jnp.where(y0, sub_roll(lo[a], -1), sub_roll(packed, 1) if h == 0 else packed))
            for a in range(4):
                packed = r1[3, a // 2, v, a % 2]
                hi_turned = jnp.where(fy, hi[3 - a], hi[a])
                left = jnp.where(y0, packed if h == 0 else sub_roll(packed, -1), sub_roll(hi_turned, 1))
                ghost = jnp.where(fy, right[3 - a], right[a])
                wy[v, a, 0, h] = wy[v, a, 0, h] - LIFT * left
                wy[v, a, 3, h] = wy[v, a, 3, h] + LIFT * ghost
                acc[v, a, 0, h] = acc[v, a, 0, h] + lift_damp * left
                acc[v, a, 3, h] = acc[v, a, 3, h] + lift_damp * ghost

    mix((0, 3), (1,), False)
    mix((1, 2), (1,), True)

    def restrict_c_into(v, a_list):
        for a in a_list:
            for b in range(4):
                rcs[v, a, b] = restrict_c(q[v, a, b, 0], q[v, a, b, 1])[3]

    @pl.loop(0, 5, unroll=True)
    def _(v):
        restrict_c_into(v, (1, 2))

    for half, nodes in enumerate(((0, 3), (1, 2))):
        sends1[0][half].wait_recv()
        sends1[1][half].wait_recv()

        @pl.loop(0, 5, unroll=True)
        def _(v, half=half, nodes=nodes):
            for h in range(2):
                lo = [q[v, 0, b, h] for b in nodes]
                hi = [q[v, 3, b, h] for b in nodes]
                right = []
                for n in range(2):
                    packed = r1[0, half, v, n]
                    right.append(jnp.where(x0, sub_roll(lo[n], -2), sub_roll(packed, 2) if h == 0 else packed))
                for n, b in enumerate(nodes):
                    packed = r1[1, half, v, n]
                    hi_turned = jnp.where(fx, hi[1 - n], hi[n])
                    left = jnp.where(x0, packed if h == 0 else sub_roll(packed, -2), sub_roll(hi_turned, 2))
                    ghost = jnp.where(fx, right[1 - n], right[n])
                    wx[v, 0, b, h] = wx[v, 0, b, h] - LIFT * left
                    wx[v, 3, b, h] = wx[v, 3, b, h] + LIFT * ghost
                    acc[v, 0, b, h] = acc[v, 0, b, h] + lift_damp * left
                    acc[v, 3, b, h] = acc[v, 3, b, h] + lift_damp * ghost

        for b in nodes:
            mix_at(b, (0, 3), (0,), True)

    def traces_of(field):
        return [
            [[field[v][0][n] for n in range(2)] for v in range(5)],
            [[field[v][1][n] for n in range(2)] for v in range(5)],
            [[field[v][n][0] for n in range(2)] for v in range(5)],
            [[field[v][n][1] for n in range(2)] for v in range(5)],
        ]

    def pack_traces(traces, target, turn):
        for v in range(5):
            for side in range(4):
                pair = traces[side][v]
                if turn and side % 2 == 1:
                    flip = fx if side < 2 else fy
                    pair = [jnp.where(flip, pair[1 - n], pair[n]) for n in range(2)]
                target[side, v] = pack_side(side, pair[0], pair[1])

    traces = [[None] * 5 for _ in range(4)]
    for v in range(5):
        restrict_c_into(v, (0, 3))
        for slot, a in ((0, 0), (1, 3)):
            traces[slot][v] = restrict_line([rcs[v, a, b] for b in range(4)])
        for slot, b in ((2, 0), (3, 3)):
            traces[slot][v] = restrict_line([rcs[v, a, b] for a in range(4)])
    pack_traces(traces, s2, True)

    for copy in sends2:
        copy.start()

    def inner_ghosts(lo, hi, mask, step, flip):
        right = [jnp.where(mask, sub_roll(value, -step), zero) for value in lo]
        right = [jnp.where(flip, right[1 - n], right[n]) for n in range(2)]
        hi = [jnp.where(flip, hi[1 - n], hi[n]) for n in range(2)]
        left = [jnp.where(mask, zero, sub_roll(value, step)) for value in hi]
        return left, right

    def coarse_sweep():
        total = [[[crhs[v, i, j] for j in range(2)] for i in range(2)] for v in range(5)]
        for d in range(3):
            for vi in range(5):
                flux = [[wc[d, vi, i, j] for j in range(2)] for i in range(2)]
                for vo in range(5):
                    weight = jn[25 * d + 5 * vo + vi]
                    for i in range(2):
                        for j in range(2):
                            total[vo][i][j] = total[vo][i][j] + weight * flux[i][j]
        outs = [[[None, None] for _ in range(2)] for _ in range(5)]
        for vo in range(5):
            for vi in range(5):
                for i in range(2):
                    for j in range(2):
                        term = csf[5 * vo + vi, i, j] * total[vi][i][j]
                        outs[vo][i][j] = term if vi == 0 else outs[vo][i][j] + term
        return outs

    e_ends = halves(EDGE[0, 0], EDGE[1, 3])
    e_ends_sw = halves(EDGE[0, 3], EDGE[1, 0])
    e_inner = halves(EDGE[0, 1], EDGE[1, 2])
    e_inner_sw = halves(EDGE[0, 2], EDGE[1, 1])
    z_lift = halves(-LIFT, LIFT)

    for v in range(5):
        rbc = [restrict_line([rcs[v, a, b] for b in range(4)]) for a in range(4)]
        rac = [restrict_line([rcs[v, a, b] for a in range(4)]) for b in range(4)]
        ra = [[restrict_line([q[v, a, b, h] for a in range(4)]) for b in range(4)] for h in range(2)]
        ends_of = [[None, None], [None, None]]
        rhs = [[None, None], [None, None]]
        w = [[[None, None], [None, None]] for _ in range(3)]
        for i in range(2):
            first = restrict_line([ra[0][b][i] for b in range(4)])
            second = restrict_line([ra[1][b][i] for b in range(4)])
            for j in range(2):
                w[0][i][j] = dot_terms(EDGE[i], [rbc[a][j] for a in range(4)])
                w[1][i][j] = dot_terms(EDGE[j], [rac[b][i] for b in range(4)])
                ends, inner, inner_sw, full = restrict_c(first[j], second[j])
                ends_of[j][i] = ends
                w[2][i][j] = (
                    e_ends * ends + e_ends_sw * sub_roll(ends, 4) + e_inner * inner + e_inner_sw * inner_sw
                )
                rhs[i][j] = rsrc[v, i, j] - (OMEGA * SHIFT) * full
        for j in range(2):
            ghosts = z_ghosts(ends_of[j], fz)
            for i in range(2):
                w[2][i][j] = w[2][i][j] + z_lift * ghosts[i]
                rhs[i][j] = rhs[i][j] + lift_damp * (ghosts[i] - ends_of[j][i])
        left, right = inner_ghosts(traces[0][v], traces[1][v], x0, 2, fx)
        for j in range(2):
            w[0][0][j] = w[0][0][j] - LIFT * left[j]
            w[0][1][j] = w[0][1][j] + LIFT * right[j]
            rhs[0][j] = rhs[0][j] + lift_damp * (left[j] - traces[0][v][j])
            rhs[1][j] = rhs[1][j] + lift_damp * (right[j] - traces[1][v][j])
        left, right = inner_ghosts(traces[2][v], traces[3][v], y0, 1, fy)
        for i in range(2):
            w[1][i][0] = w[1][i][0] - LIFT * left[i]
            w[1][i][1] = w[1][i][1] + LIFT * right[i]
            rhs[i][0] = rhs[i][0] + lift_damp * (left[i] - traces[2][v][i])
            rhs[i][1] = rhs[i][1] + lift_damp * (right[i] - traces[3][v][i])
        for i in range(2):
            for j in range(2):
                crhs[v, i, j] = rhs[i][j]
                for d in range(3):
                    wc[d, v, i, j] = w[d][i][j]

    outs = coarse_sweep()
    for v in range(5):
        for i in range(2):
            for j in range(2):
                cloc[v, i, j] = outs[v][i][j]

    @pl.loop(0, 20, unroll=4)
    def _(t):
        v, b = t // 4, t % 4
        for a in range(4):
            for h in range(2):
                out[v, a, b, h] = OMEGA * q[v, a, b, h]

    def face_product(ref, side, vectors):
        outs = []
        for vo in range(5):
            total = ref[side, 5 * vo] * vectors[0]
            for vi in range(1, 5):
                total = total + ref[side, 5 * vo + vi] * vectors[vi]
            outs.append(total)
        return outs

    def own_ghost(side, value):
        if side % 2 == 0:
            return value
        return jnp.where(sg[side, 25] == 1.0, swap_rows(value, 2 if side < 2 else 1), value)

    def face_terms(ghosts):
        pairs = [[None] * 5 for _ in range(4)]
        for side in range(4):
            mask, step = (x0, 2) if side < 2 else (y0, 1)
            for v, delta in enumerate(face_product(sg, side, ghosts[side])):
                if side % 2 == 0:
                    pairs[side][v] = [
                        jnp.where(mask, delta, zero), jnp.where(mask, sub_roll(delta, -step), zero)
                    ]
                else:
                    pairs[side][v] = [
                        jnp.where(mask, zero, sub_roll(delta, step)), jnp.where(mask, zero, delta)
                    ]
        return [[[pairs[i][v][j] + pairs[2 + j][v][i] for j in range(2)] for i in range(2)] for v in range(5)]

    def inner_operator(field):
        for v in range(5):
            here = field[v]
            rhs = [[(-k_coarse) * here[i][j] for j in range(2)] for i in range(2)]
            for j in range(2):
                ghosts = z_ghosts([here[i][j] for i in range(2)], fz)
                for i in range(2):
                    swapped = sub_roll(here[i][j], 4)
                    wc[2, v, i, j] = jnp.where(low, 0.5, -0.5) * (swapped - ghosts[i])
                    rhs[i][j] = rhs[i][j] + half_damp * ghosts[i]
            left, right = inner_ghosts(here[0], here[1], x0, 2, fx)
            for j in range(2):
                wc[0, v, 0, j] = 0.5 * (here[1][j] - left[j])
                wc[0, v, 1, j] = 0.5 * (right[j] - here[0][j])
                rhs[0][j] = rhs[0][j] + half_damp * left[j]
                rhs[1][j] = rhs[1][j] + half_damp * right[j]
            left, right = inner_ghosts([here[i][0] for i in range(2)], [here[i][1] for i in range(2)], y0, 1, fy)
            for i in range(2):
                wc[1, v, i, 0] = 0.5 * (here[i][1] - left[i])
                wc[1, v, i, 1] = 0.5 * (right[i] - here[i][0])
                rhs[i][0] = rhs[i][0] + half_damp * left[i]
                rhs[i][1] = rhs[i][1] + half_damp * right[i]
            for i in range(2):
                for j in range(2):
                    crhs[v, i, j] = rhs[i][j]
        return coarse_sweep()

    def combine(function, *fields):
        return [
            [[function(*(f[v][i][j] for f in fields)) for j in range(2)] for i in range(2)] for v in range(5)
        ]

    def load_field(ref):
        return [[[ref[v, i, j] for j in range(2)] for i in range(2)] for v in range(5)]

    for copy in sends2:
        copy.wait_recv()
    terms = face_terms([[own_ghost(side, r2[side ^ 1, v]) for v in range(5)] for side in range(4)])
    coarse = combine(lambda x, y: x + 6.0 * y, load_field(cloc), terms)
    pack_traces(traces_of(coarse), s3, True)
    for copy in sends3:
        copy.start()

    for copy in sends_face:
        copy.wait_recv()

    added = []
    for side in range(4):
        mine = [s3[side, v] for v in range(5)]
        if side % 2 == 0:
            turn = rg[side ^ 1, 25] == 1.0
            mine = [jnp.where(turn, swap_rows(value, 2 if side < 2 else 1), value) for value in mine]
        added.append(face_product(rg, side ^ 1, mine))
    for k, (along_y, along_x, y_row, x_row) in enumerate(CORNERS):
        slots = []
        for v in range(5):
            slots += [(added[along_y][v], y_row), (added[along_x][v], x_row)]
        for n in range(3):
            tile = zero
            for place, (value, source) in enumerate(slots[4 * n : 4 * n + 4]):
                tile = jnp.where(row4 == place, sub_roll(value, place - source), tile)
            sd[k, n] = tile

    for copy in sends_corner:
        copy.start()

    outs = inner_operator(coarse)
    partial = combine(lambda x, y: 2.0 * x + y, coarse, outs)
    pack_traces(traces_of(partial), sp, False)

    for copy in sends_part:
        copy.start()

    for v in range(5):
        for side in range(4):
            gcor[side, v] = added[side][v]
        for i in range(2):
            for j in range(2):
                cloc[v, i, j] = coarse[v][i][j]
                cpart[v, i, j] = partial[v][i][j]

    for copy in sends3:
        copy.wait_recv()

    terms = face_terms([[own_ghost(side, r3[side ^ 1, v]) for v in range(5)] for side in range(4)])
    middle = combine(lambda x, y: x + y, load_field(cpart), terms)
    outs = inner_operator(middle)
    coarse = combine(lambda x, y, z: x + y + z, load_field(cloc), middle, outs)

    for copy in sends_corner:
        copy.wait_recv()

    def corner_rows(side, v):
        lower, upper = ((3, 1), (2, 0), (3, 2), (1, 0))[side]
        slot = 2 * v + (0 if side < 2 else 1)
        tile, place = slot // 4, slot % 4
        lower, upper = sub_roll(rd[lower, tile], -place), sub_roll(rd[upper, tile], 3 - place)
        return jnp.where(row4 == 0, lower, jnp.where(row4 == 3, upper, zero))

    beside = [[corner_rows(side, v) for v in range(5)] for side in range(4)]

    for copy in sends_part:
        copy.wait_recv()

    ghosts = []
    for side in range(4):
        values = [rp[side ^ 1, v] + (gcor[side, v] + beside[side][v]) for v in range(5)]
        if side % 2 == 0:
            turn = rg[side ^ 1, 25] == 1.0
            values = [jnp.where(turn, swap_rows(value, 2 if side < 2 else 1), value) for value in values]
        else:
            values = [own_ghost(side, value) for value in values]
        ghosts.append(values)
    coarse = combine(lambda x, y: x + y, coarse, face_terms(ghosts))

    t_first = [halves(OMEGA, OMEGA * P_FAR), halves(0.0, OMEGA * P_NEAR)]
    t_second = [halves(OMEGA * P_FAR, OMEGA), halves(OMEGA * P_NEAR, 0.0)]

    for v in range(5):
        by_a = [prolong_line([coarse[v][i][j] for i in range(2)]) for j in range(2)]
        for a in range(4):
            for b, value in enumerate(prolong_line([by_a[j][a] for j in range(2)])):
                swapped = sub_roll(value, 4)
                out[v, a, b, 0] = out[v, a, b, 0] + (t_first[0] * value + t_first[1] * swapped)
                out[v, a, b, 1] = out[v, a, b, 1] + (t_second[0] * value + t_second[1] * swapped)

    for copy in started:
        copy.wait_send()


def body(source, jacobian, damping, orient, smoother, coarse_smoother):
    field = (5, 4, 4, 2, 8, 128)
    vmem = pltpu.VMEM
    hbm = pl.BlockSpec(memory_space=pltpu.HBM)
    out = pl.pallas_call(
        kernel,
        out_shape=pltpu.VMEM(field, F32),
        in_specs=[hbm] * 6,
        out_specs=pl.BlockSpec(memory_space=pltpu.VMEM),
        scratch_shapes=[
            vmem(field, F32),
            vmem((25, 4, 4, 16, 128), jnp.bfloat16),
            vmem((25, 2, 16, 128), jnp.bfloat16),
            vmem((75, 4, 128), F32),
            vmem((75, 8, 128), F32),
            vmem((4, 128), F32),
            vmem((3, 4, 128), jnp.int32),
            vmem((3, 8, 128), jnp.int32),
            vmem((5, 8, 128), F32),
            vmem((4, 2, 2, 8, 128), F32),
            vmem((25, 2, 2, 8, 128), F32),
            vmem((25, 8, 128), F32),
            vmem(field, F32),
            vmem(field, F32),
            vmem(field, F32),
            vmem(field, F32),
            vmem(field, F32),
            vmem((5, 2, 2, 8, 128), F32),
            vmem((5, 4, 4, 8, 128), F32),
            vmem((5, 2, 2, 8, 128), F32),
            vmem((5, 2, 2, 8, 128), F32),
            vmem((4, 5, 8, 128), F32),
            vmem((3, 5, 2, 2, 8, 128), F32),
            vmem((5, 2, 2, 8, 128), F32),
            vmem((4, 2, 5, 2, 8, 128), F32),
            vmem((4, 2, 5, 2, 8, 128), F32),
            vmem((4, 5, 8, 128), F32),
            vmem((4, 5, 8, 128), F32),
            vmem((4, 5, 8, 128), F32),
            vmem((4, 5, 8, 128), F32),
            vmem((4, 5, 8, 128), F32),
            vmem((4, 5, 8, 128), F32),
            vmem((4, 3, 8, 128), F32),
            vmem((4, 3, 8, 128), F32),
            vmem((4, 26, 8, 128), F32),
            vmem((4, 26, 8, 128), F32),
            pltpu.SemaphoreType.DMA((12,)),
            pltpu.SemaphoreType.DMA((28,)),
            pltpu.SemaphoreType.DMA((28,)),
        ],
        compiler_params=pltpu.CompilerParams(collective_id=0, has_side_effects=True),
    )(
        source.reshape(field),
        jacobian.reshape(75, 4, 128),
        damping.reshape(4, 128),
        orient.reshape(3, 4, 128),
        smoother.reshape(25, 4, 4, 16, 128),
        coarse_smoother.reshape(25, 2, 16, 128),
    )
    return out.reshape(5, 4, 4, 4, 2, 2, 128)


def solution(mesh):
    in_specs = (
        P(None, None, None, None, "gx", "gy", None),
        P(None, None, None, "gx", "gy", None),
        P("gx", "gy", None),
        P(None, "gx", "gy", None),
        P(None, None, None, None, None, "gx", "gy", None),
        P(None, None, None, None, None, "gx", "gy", None),
    )
    out_specs = P(None, None, None, None, "gx", "gy", None)
    return jax.shard_map(body, mesh=mesh, in_specs=in_specs, out_specs=out_specs, check_vma=False)
```

```python
import functools
import math

import jax
import jax.numpy as jnp
import numpy as np
from jax import lax
from jax.experimental import pallas as pl
from jax.experimental.pallas import tpu as pltpu
from jax.sharding import PartitionSpec as P

MESH = pl.DeviceIdType.MESH
OMEGA = 0.8
SHIFT = 2.0
F32 = jnp.float32


def lobatto4():
    points = np.array([-1.0, -1.0 / math.sqrt(5.0), 1.0 / math.sqrt(5.0), 1.0])
    weights = np.ones(4)
    for row in range(4):
        for col in range(4):
            if row != col:
                weights[row] /= points[row] - points[col]
    slopes = np.zeros((4, 4))
    for row in range(4):
        for col in range(4):
            if row != col:
                slopes[row, col] = weights[col] / weights[row] / (points[row] - points[col])
        slopes[row, row] = -np.sum(slopes[row])
    return points, slopes


POINTS, SLOPES = lobatto4()
INTERP = np.stack([(1.0 - POINTS) / 2.0, (1.0 + POINTS) / 2.0], 1)
OPEN = SLOPES.copy()
OPEN[0, 0] = OPEN[3, 3] = OPEN[1, 1] = OPEN[2, 2] = 0.0
LIFT = 3.0
EDGE = INTERP.T @ OPEN
P_NEAR, P_FAR = float(INTERP[1, 0]), float(INTERP[2, 0])


def dot_terms(coefs, values):
    total = None
    for coef, value in zip(coefs, values):
        coef = float(coef)
        if coef == 0.0:
            continue
        term = value if coef == 1.0 else coef * value
        total = term if total is None else total + term
    return total


def rows():
    return lax.broadcasted_iota(jnp.int32, (8, 128), 0)


def halves(top, bottom):
    return jnp.where(rows() < 4, jnp.full((8, 128), float(top), F32), jnp.full((8, 128), float(bottom), F32))


def sub_roll(value, shift):
    return pltpu.roll(value, shift % 8, 0)


def lane_roll(value, shift):
    return pltpu.roll(value, shift % 128, 1)


def pack_low(first, second, mask, step):
    return jnp.where(mask, first, sub_roll(second, step))


def pack_high(first, second, mask, step):
    return jnp.where(mask, sub_roll(first, -step), second)


def z_ghosts(traces, turned):
    count = len(traces)
    low = rows() < 4
    flip = jnp.logical_and(turned, rows() >= 4)
    out = []
    for a in range(count):
        swapped = sub_roll(jnp.where(flip, traces[count - 1 - a], traces[a]), 4)
        out.append(jnp.where(low, lane_roll(swapped, 1), lane_roll(swapped, -1)))
    return [jnp.where(flip, out[count - 1 - a], out[a]) for a in range(count)]


def restrict_c(first, second):
    low = rows() < 4
    ends = jnp.where(low, first, second)
    inner_swapped = jnp.where(low, second, first)
    inner = sub_roll(inner_swapped, 4)
    return ends, inner, inner_swapped, ends + P_NEAR * inner + P_FAR * inner_swapped


def restrict_line(values):
    low = values[0] + P_NEAR * values[1] + P_FAR * values[2]
    high = values[3] + P_NEAR * values[2] + P_FAR * values[1]
    return [low, high]


def prolong_line(values):
    return [
        values[0],
        P_NEAR * values[0] + P_FAR * values[1],
        P_FAR * values[0] + P_NEAR * values[1],
        values[1],
    ]


CORNERS = ((2, 0, 0, 0), (2, 1, 3, 0), (3, 0, 0, 3), (3, 1, 3, 3))


def swap_rows(value, step):
    return jnp.where((rows() & step) == 0, sub_roll(value, -step), sub_roll(value, step))


def kernel(
    src_hbm, jac_hbm, damp_hbm, flag_hbm, smo_hbm, csm_hbm, out,
    src, smo, csm, jraw, jn, draw, fraw, flags, dmp, kfine, csf, kface,
    q, acc, wx, wy, wz, rsrc, rcs, cloc, cpart, gcor, wc, crhs,
    s1, r1, s2, r2, s3, r3, sp, rp, sd, rd, sg, rg, in_sem, send_sem, recv_sem,
):
    nx, ny = lax.axis_size("gx"), lax.axis_size("gy")
    ix, iy = lax.axis_index("gx"), lax.axis_index("gy")
    x_next, x_prev = lax.rem(ix + 1, nx), lax.rem(ix + nx - 1, nx)
    y_next, y_prev = lax.rem(iy + 1, ny), lax.rem(iy + ny - 1, ny)
    partners = [(x_prev, iy), (x_next, iy), (ix, y_prev), (ix, y_next)]
    corners = [(x_prev, y_prev), (x_next, y_prev), (x_prev, y_next), (x_next, y_next)]

    barrier = pltpu.get_barrier_semaphore()
    for partner in partners:
        pl.semaphore_signal(barrier, inc=1, device_id=partner, device_id_type=MESH)

    loads = []

    def load(source, target):
        copy = pltpu.make_async_copy(source, target, in_sem.at[len(loads)])
        copy.start()
        loads.append(copy)
        return copy

    parts = {}
    flag_load = load(flag_hbm, fraw)
    damp_load = load(damp_hbm, draw)
    jac_load = load(jac_hbm, jraw)
    csm_load = load(csm_hbm, csm)
    for a in (0, 3, 1, 2):
        parts[a] = (load(src_hbm.at[:, a], src.at[:, a]), load(smo_hbm.at[:, a], smo.at[:, a]))

    started = []

    def remote(source, target, number, partner):
        copy = pltpu.make_async_remote_copy(
            src_ref=source, dst_ref=target, send_sem=send_sem.at[number], recv_sem=recv_sem.at[number],
            device_id=partner, device_id_type=MESH,
        )
        started.append(copy)
        return copy

    sends1 = [[remote(s1.at[k, h], r1.at[k, h], 2 * k + h, partners[k]) for h in range(2)] for k in range(2)]
    sends1 += [[remote(s1.at[k], r1.at[k], 2 * k, partners[k])] for k in range(2, 4)]
    sends2 = [remote(s2.at[k], r2.at[k], 8 + k, partners[k]) for k in range(4)]
    sends3 = [remote(s3.at[k], r3.at[k], 12 + k, partners[k]) for k in range(4)]
    sends_part = [remote(sp.at[k], rp.at[k], 16 + k, partners[k]) for k in range(4)]
    sends_corner = [remote(sd.at[k], rd.at[k], 20 + k, corners[k]) for k in range(4)]
    sends_face = [remote(sg.at[k], rg.at[k], 24 + k, partners[k]) for k in range(4)]

    low = rows() < 4
    x0 = (rows() & 2) == 0
    y0 = (rows() & 1) == 0
    zero = jnp.zeros((8, 128), F32)
    row4 = rows() & 3

    def smooth(a, b, fields):
        outs = []
        for vo in range(5):
            pair = [None, None]
            for vi in range(5):
                block = smo[5 * vo + vi, a, b].astype(F32)
                for half in range(2):
                    term = block[8 * half : 8 * half + 8] * fields[vi][half]
                    pair[half] = term if vi == 0 else pair[half] + term
            outs.append(pair)
        return outs

    def first_pass(a, b):
        fields = [[src[v, a, b, 0], src[v, a, b, 1]] for v in range(5)]
        outs = smooth(a, b, fields)
        for v in range(5):
            q[v, a, b, 0] = outs[v][0]
            q[v, a, b, 1] = outs[v][1]

    flag_load.wait()
    damp_load.wait()
    for d in range(3):
        flags[d] = jnp.concatenate([fraw[d], fraw[d]], axis=0)
    fx, fy, fz = (flags[d] == 1 for d in range(3))
    damping = jnp.concatenate([draw[...], draw[...]], axis=0)
    dmp[0] = (OMEGA * LIFT) * damping
    dmp[1] = (OMEGA * 0.5) * damping
    dmp[2] = OMEGA * SHIFT + (OMEGA * 1.5) * damping
    dmp[3] = jnp.where(low, (OMEGA * LIFT) * damping, 0.0)
    dmp[4] = jnp.where(low, 0.0, (OMEGA * LIFT) * damping)
    for b in range(4):
        for a_end in range(2):
            faces = a_end + (1 if b in (0, 3) else 0)
            base = OMEGA * SHIFT + (OMEGA * LIFT * faces) * damping
            kfine[b, a_end, 0] = base + dmp[3]
            kfine[b, a_end, 1] = base + dmp[4]

    jac_load.wait()

    @pl.loop(0, 75, unroll=15)
    def _(i):
        block = jraw[i]
        jn[i] = (-OMEGA) * jnp.concatenate([block, block], axis=0)

    csm_load.wait()

    @pl.loop(0, 25, unroll=5)
    def _(i):
        for n in range(2):
            block = csm[i, n].astype(F32)
            csf[i, n, 0] = block[:8]
            csf[i, n, 1] = block[8:]

    half_damp, k_coarse, lift_damp = dmp[1], dmp[2], dmp[0]

    def pack_side(side, first, second):
        mask, step = (x0, 2) if side < 2 else (y0, 1)
        return (pack_low if side % 2 == 0 else pack_high)(first, second, mask, step)

    for side in range(4):
        own = 0 if side < 2 else 1
        sign = -0.5 if side % 2 == 0 else 0.5

        @pl.loop(0, 5, unroll=True)
        def _(row, side=side, own=own, sign=sign):
            for col in range(5):
                diag = jnp.where(row == col, half_damp, zero)
                face = diag + sign * jn[25 * own + 5 * row + col]
                kface[5 * row + col] = pack_side(side, face, face)

        @pl.loop(0, 5, unroll=True)
        def _(vo, side=side):
            blocks = []
            for m in range(5):
                if side < 2:
                    pair = [csf[5 * vo + m, side, j] for j in range(2)]
                else:
                    pair = [csf[5 * vo + m, i, side - 2] for i in range(2)]
                blocks.append(pack_side(side, pair[0], pair[1]))
            for vi in range(5):
                total = blocks[0] * kface[vi]
                for m in range(1, 5):
                    total = total + blocks[m] * kface[5 * m + vi]
                sg[side, 5 * vo + vi] = total

        flag = jnp.where(flags[own] == 1, 1.0, 0.0)
        sg[side, 25] = pack_side(side, flag, flag)

    for a in (0, 3):
        for copy in parts[a]:
            copy.wait()

        @pl.loop(0, 4)
        def _(b, a=a):
            first_pass(a, b)

    HALF = {0: (0, 0), 3: (0, 1), 1: (1, 0), 2: (1, 1)}

    @pl.loop(0, 5, unroll=True)
    def _(v):
        for b in range(4):
            half, place = HALF[b]
            s1[0, half, v, place] = pack_low(q[v, 0, b, 0], q[v, 0, b, 1], x0, 2)
            hi = [jnp.where(fx, q[v, 3, 3 - b, h], q[v, 3, b, h]) for h in range(2)]
            s1[1, half, v, place] = pack_high(hi[0], hi[1], x0, 2)

    pl.semaphore_wait(barrier, 4)
    for half in range(2):
        for k in range(2):
            sends1[k][half].start()

    for a in (1, 2):
        for copy in parts[a]:
            copy.wait()

        @pl.loop(0, 4)
        def _(b, a=a):
            first_pass(a, b)

    @pl.loop(0, 5, unroll=True)
    def _(v):
        for a in range(4):
            s1[2, a // 2, v, a % 2] = pack_low(q[v, a, 0, 0], q[v, a, 0, 1], y0, 1)
            hi = [jnp.where(fy, q[v, 3 - a, 3, h], q[v, a, 3, h]) for h in range(2)]
            s1[3, a // 2, v, a % 2] = pack_high(hi[0], hi[1], y0, 1)

    sends1[2][0].start()
    sends1[3][0].start()


    c_first = [halves(OPEN[0, 1], OPEN[1, 0]), halves(OPEN[0, 2], OPEN[1, 3]), halves(OPEN[0, 3], OPEN[1, 2])]
    c_second = [halves(OPEN[2, 3], OPEN[3, 2]), halves(OPEN[2, 0], OPEN[3, 1]), halves(OPEN[2, 1], OPEN[3, 0])]
    c_ghost = [halves(-LIFT, 0.0), halves(0.0, LIFT)]

    @pl.loop(0, 20, unroll=4)
    def _(t):
        v, b = t // 4, t % 4
        first = [q[v, a, b, 0] for a in range(4)]
        second = [q[v, a, b, 1] for a in range(4)]
        for a in range(4):
            for h, line in enumerate((first, second)):
                wx[v, a, b, h] = dot_terms(OPEN[a], line)
        ghosts = z_ghosts([jnp.where(low, first[a], second[a]) for a in range(4)], fz)
        for a in range(4):
            a_end = 1 if a in (0, 3) else 0
            first_sw, second_sw = sub_roll(first[a], 4), sub_roll(second[a], 4)
            wz[v, a, b, 0] = (
                c_first[0] * first_sw + c_first[1] * second[a] + c_first[2] * second_sw + c_ghost[0] * ghosts[a]
            )
            wz[v, a, b, 1] = (
                c_second[0] * second_sw + c_second[1] * first[a] + c_second[2] * first_sw + c_ghost[1] * ghosts[a]
            )
            acc[v, a, b, 0] = src[v, a, b, 0] - kfine[b, a_end, 0] * first[a] + dmp[3] * ghosts[a]
            acc[v, a, b, 1] = src[v, a, b, 1] - kfine[b, a_end, 1] * second[a] + dmp[4] * ghosts[a]

    @pl.loop(0, 20, unroll=4)
    def _(t):
        v, a = t // 4, t % 4
        for h in range(2):
            line = [q[v, a, b, h] for b in range(4)]
            for b in range(4):
                wy[v, a, b, h] = dot_terms(OPEN[b], line)

    def mix_at(b, pair, directions, last):
        total = [[[acc[v, a, b, h] for h in range(2)] for a in pair] for v in range(5)]
        for d in directions:
            w = (wx, wy, wz)[d]
            for vi in range(5):
                flux = [[w[vi, a, b, h] for h in range(2)] for a in pair]
                for vo in range(5):
                    weight = jn[25 * d + 5 * vo + vi]
                    for n in range(2):
                        for h in range(2):
                            total[vo][n][h] = total[vo][n][h] + weight * flux[n][h]
        for n, a in enumerate(pair):
            if last:
                outs = smooth(a, b, [total[v][n] for v in range(5)])
            for v in range(5):
                for h in range(2):
                    if last:
                        q[v, a, b, h] = q[v, a, b, h] + outs[v][h]
                    else:
                        acc[v, a, b, h] = total[v][n][h]

    def mix(first, step, pair, directions, last):
        @pl.loop(0, 2)
        def _(t):
            mix_at(first + step * t, pair, directions, last)

    mix(0, 3, (0, 3), (2,), False)
    mix(0, 3, (1, 2), (0, 2), False)

    for copy in sends_face:
        copy.start()

    @pl.loop(0, 5, unroll=True)
    def _(v):
        by_a = []
        for a in range(4):
            by_a.append(restrict_line([restrict_c(src[v, a, b, 0], src[v, a, b, 1])[3] for b in range(4)]))
        for j in range(2):
            for i, value in enumerate(restrict_line([by_a[a][j] for a in range(4)])):
                rsrc[v, i, j] = value

    mix(1, 1, (0, 3), (1, 2), False)
    mix(1, 1, (1, 2), (0, 1, 2), True)

    sends1[2][0].wait_recv()
    sends1[3][0].wait_recv()

    @pl.loop(0, 5, unroll=True)
    def _(v):
        for h in range(2):
            lo = [q[v, a, 0, h] for a in range(4)]
            hi = [q[v, a, 3, h] for a in range(4)]
            right = []
            for a in range(4):
                packed = r1[2, a // 2, v, a % 2]
                right.append(jnp.where(y0, sub_roll(lo[a], -1), sub_roll(packed, 1) if h == 0 else packed))
            for a in range(4):
                packed = r1[3, a // 2, v, a % 2]
                hi_turned = jnp.where(fy, hi[3 - a], hi[a])
                left = jnp.where(y0, packed if h == 0 else sub_roll(packed, -1), sub_roll(hi_turned, 1))
                ghost = jnp.where(fy, right[3 - a], right[a])
                wy[v, a, 0, h] = wy[v, a, 0, h] - LIFT * left
                wy[v, a, 3, h] = wy[v, a, 3, h] + LIFT * ghost
                acc[v, a, 0, h] = acc[v, a, 0, h] + lift_damp * left
                acc[v, a, 3, h] = acc[v, a, 3, h] + lift_damp * ghost

    mix(0, 3, (0, 3), (1,), False)
    mix(0, 3, (1, 2), (1,), True)

    def restrict_c_into(v, a_list):
        for a in a_list:
            for b in range(4):
                rcs[v, a, b] = restrict_c(q[v, a, b, 0], q[v, a, b, 1])[3]

    @pl.loop(0, 5, unroll=True)
    def _(v):
        restrict_c_into(v, (1, 2))

    for half, nodes in enumerate(((0, 3), (1, 2))):
        sends1[0][half].wait_recv()
        sends1[1][half].wait_recv()

        @pl.loop(0, 5, unroll=True)
        def _(v, half=half, nodes=nodes):
            for h in range(2):
                lo = [q[v, 0, b, h] for b in nodes]
                hi = [q[v, 3, b, h] for b in nodes]
                right = []
                for n in range(2):
                    packed = r1[0, half, v, n]
                    right.append(jnp.where(x0, sub_roll(lo[n], -2), sub_roll(packed, 2) if h == 0 else packed))
                for n, b in enumerate(nodes):
                    packed = r1[1, half, v, n]
                    hi_turned = jnp.where(fx, hi[1 - n], hi[n])
                    left = jnp.where(x0, packed if h == 0 else sub_roll(packed, -2), sub_roll(hi_turned, 2))
                    ghost = jnp.where(fx, right[1 - n], right[n])
                    wx[v, 0, b, h] = wx[v, 0, b, h] - LIFT * left
                    wx[v, 3, b, h] = wx[v, 3, b, h] + LIFT * ghost
                    acc[v, 0, b, h] = acc[v, 0, b, h] + lift_damp * left
                    acc[v, 3, b, h] = acc[v, 3, b, h] + lift_damp * ghost

        for b in nodes:
            mix_at(b, (0, 3), (0,), True)

    def traces_of(field):
        return [
            [[field[v][0][n] for n in range(2)] for v in range(5)],
            [[field[v][1][n] for n in range(2)] for v in range(5)],
            [[field[v][n][0] for n in range(2)] for v in range(5)],
            [[field[v][n][1] for n in range(2)] for v in range(5)],
        ]

    def pack_traces(traces, target, turn):
        for v in range(5):
            for side in range(4):
                pair = traces[side][v]
                if turn and side % 2 == 1:
                    flip = fx if side < 2 else fy
                    pair = [jnp.where(flip, pair[1 - n], pair[n]) for n in range(2)]
                target[side, v] = pack_side(side, pair[0], pair[1])

    traces = [[None] * 5 for _ in range(4)]
    for v in range(5):
        restrict_c_into(v, (0, 3))
        for slot, a in ((0, 0), (1, 3)):
            traces[slot][v] = restrict_line([rcs[v, a, b] for b in range(4)])
        for slot, b in ((2, 0), (3, 3)):
            traces[slot][v] = restrict_line([rcs[v, a, b] for a in range(4)])
    pack_traces(traces, s2, True)

    for copy in sends2:
        copy.start()

    def inner_ghosts(lo, hi, mask, step, flip):
        right = [jnp.where(mask, sub_roll(value, -step), zero) for value in lo]
        right = [jnp.where(flip, right[1 - n], right[n]) for n in range(2)]
        hi = [jnp.where(flip, hi[1 - n], hi[n]) for n in range(2)]
        left = [jnp.where(mask, zero, sub_roll(value, step)) for value in hi]
        return left, right

    def coarse_sweep():
        total = [[[crhs[v, i, j] for j in range(2)] for i in range(2)] for v in range(5)]
        for d in range(3):
            for vi in range(5):
                flux = [[wc[d, vi, i, j] for j in range(2)] for i in range(2)]
                for vo in range(5):
                    weight = jn[25 * d + 5 * vo + vi]
                    for i in range(2):
                        for j in range(2):
                            total[vo][i][j] = total[vo][i][j] + weight * flux[i][j]
        outs = [[[None, None] for _ in range(2)] for _ in range(5)]
        for vo in range(5):
            for vi in range(5):
                for i in range(2):
                    for j in range(2):
                        term = csf[5 * vo + vi, i, j] * total[vi][i][j]
                        outs[vo][i][j] = term if vi == 0 else outs[vo][i][j] + term
        return outs

    e_ends = halves(EDGE[0, 0], EDGE[1, 3])
    e_ends_sw = halves(EDGE[0, 3], EDGE[1, 0])
    e_inner = halves(EDGE[0, 1], EDGE[1, 2])
    e_inner_sw = halves(EDGE[0, 2], EDGE[1, 1])
    z_lift = halves(-LIFT, LIFT)

    for v in range(5):
        rbc = [restrict_line([rcs[v, a, b] for b in range(4)]) for a in range(4)]
        rac = [restrict_line([rcs[v, a, b] for a in range(4)]) for b in range(4)]
        ra = [[restrict_line([q[v, a, b, h] for a in range(4)]) for b in range(4)] for h in range(2)]
        ends_of = [[None, None], [None, None]]
        rhs = [[None, None], [None, None]]
        w = [[[None, None], [None, None]] for _ in range(3)]
        for i in range(2):
            first = restrict_line([ra[0][b][i] for b in range(4)])
            second = restrict_line([ra[1][b][i] for b in range(4)])
            for j in range(2):
                w[0][i][j] = dot_terms(EDGE[i], [rbc[a][j] for a in range(4)])
                w[1][i][j] = dot_terms(EDGE[j], [rac[b][i] for b in range(4)])
                ends, inner, inner_sw, full = restrict_c(first[j], second[j])
                ends_of[j][i] = ends
                w[2][i][j] = (
                    e_ends * ends + e_ends_sw * sub_roll(ends, 4) + e_inner * inner + e_inner_sw * inner_sw
                )
                rhs[i][j] = rsrc[v, i, j] - (OMEGA * SHIFT) * full
        for j in range(2):
            ghosts = z_ghosts(ends_of[j], fz)
            for i in range(2):
                w[2][i][j] = w[2][i][j] + z_lift * ghosts[i]
                rhs[i][j] = rhs[i][j] + lift_damp * (ghosts[i] - ends_of[j][i])
        left, right = inner_ghosts(traces[0][v], traces[1][v], x0, 2, fx)
        for j in range(2):
            w[0][0][j] = w[0][0][j] - LIFT * left[j]
            w[0][1][j] = w[0][1][j] + LIFT * right[j]
            rhs[0][j] = rhs[0][j] + lift_damp * (left[j] - traces[0][v][j])
            rhs[1][j] = rhs[1][j] + lift_damp * (right[j] - traces[1][v][j])
        left, right = inner_ghosts(traces[2][v], traces[3][v], y0, 1, fy)
        for i in range(2):
            w[1][i][0] = w[1][i][0] - LIFT * left[i]
            w[1][i][1] = w[1][i][1] + LIFT * right[i]
            rhs[i][0] = rhs[i][0] + lift_damp * (left[i] - traces[2][v][i])
            rhs[i][1] = rhs[i][1] + lift_damp * (right[i] - traces[3][v][i])
        for i in range(2):
            for j in range(2):
                crhs[v, i, j] = rhs[i][j]
                for d in range(3):
                    wc[d, v, i, j] = w[d][i][j]

    outs = coarse_sweep()
    for v in range(5):
        for i in range(2):
            for j in range(2):
                cloc[v, i, j] = outs[v][i][j]

    @pl.loop(0, 20, unroll=4)
    def _(t):
        v, b = t // 4, t % 4
        for a in range(4):
            for h in range(2):
                out[v, a, b, h] = OMEGA * q[v, a, b, h]

    def face_product(ref, side, vectors):
        outs = []
        for vo in range(5):
            total = ref[side, 5 * vo] * vectors[0]
            for vi in range(1, 5):
                total = total + ref[side, 5 * vo + vi] * vectors[vi]
            outs.append(total)
        return outs

    def own_ghost(side, value):
        if side % 2 == 0:
            return value
        return jnp.where(sg[side, 25] == 1.0, swap_rows(value, 2 if side < 2 else 1), value)

    def face_terms(ghosts):
        pairs = [[None] * 5 for _ in range(4)]
        for side in range(4):
            mask, step = (x0, 2) if side < 2 else (y0, 1)
            for v, delta in enumerate(face_product(sg, side, ghosts[side])):
                if side % 2 == 0:
                    pairs[side][v] = [
                        jnp.where(mask, delta, zero), jnp.where(mask, sub_roll(delta, -step), zero)
                    ]
                else:
                    pairs[side][v] = [
                        jnp.where(mask, zero, sub_roll(delta, step)), jnp.where(mask, zero, delta)
                    ]
        return [[[pairs[i][v][j] + pairs[2 + j][v][i] for j in range(2)] for i in range(2)] for v in range(5)]

    def inner_operator(field):
        for v in range(5):
            here = field[v]
            rhs = [[(-k_coarse) * here[i][j] for j in range(2)] for i in range(2)]
            for j in range(2):
                ghosts = z_ghosts([here[i][j] for i in range(2)], fz)
                for i in range(2):
                    swapped = sub_roll(here[i][j], 4)
                    wc[2, v, i, j] = jnp.where(low, 0.5, -0.5) * (swapped - ghosts[i])
                    rhs[i][j] = rhs[i][j] + half_damp * ghosts[i]
            left, right = inner_ghosts(here[0], here[1], x0, 2, fx)
            for j in range(2):
                wc[0, v, 0, j] = 0.5 * (here[1][j] - left[j])
                wc[0, v, 1, j] = 0.5 * (right[j] - here[0][j])
                rhs[0][j] = rhs[0][j] + half_damp * left[j]
                rhs[1][j] = rhs[1][j] + half_damp * right[j]
            left, right = inner_ghosts([here[i][0] for i in range(2)], [here[i][1] for i in range(2)], y0, 1, fy)
            for i in range(2):
                wc[1, v, i, 0] = 0.5 * (here[i][1] - left[i])
                wc[1, v, i, 1] = 0.5 * (right[i] - here[i][0])
                rhs[i][0] = rhs[i][0] + half_damp * left[i]
                rhs[i][1] = rhs[i][1] + half_damp * right[i]
            for i in range(2):
                for j in range(2):
                    crhs[v, i, j] = rhs[i][j]
        return coarse_sweep()

    def combine(function, *fields):
        return [
            [[function(*(f[v][i][j] for f in fields)) for j in range(2)] for i in range(2)] for v in range(5)
        ]

    def load_field(ref):
        return [[[ref[v, i, j] for j in range(2)] for i in range(2)] for v in range(5)]

    for copy in sends2:
        copy.wait_recv()
    terms = face_terms([[own_ghost(side, r2[side ^ 1, v]) for v in range(5)] for side in range(4)])
    coarse = combine(lambda x, y: x + 6.0 * y, load_field(cloc), terms)
    pack_traces(traces_of(coarse), s3, True)
    for copy in sends3:
        copy.start()

    for copy in sends_face:
        copy.wait_recv()

    added = []
    for side in range(4):
        mine = [s3[side, v] for v in range(5)]
        if side % 2 == 0:
            turn = rg[side ^ 1, 25] == 1.0
            mine = [jnp.where(turn, swap_rows(value, 2 if side < 2 else 1), value) for value in mine]
        added.append(face_product(rg, side ^ 1, mine))
    for k, (along_y, along_x, y_row, x_row) in enumerate(CORNERS):
        slots = []
        for v in range(5):
            slots += [(added[along_y][v], y_row), (added[along_x][v], x_row)]
        for n in range(3):
            tile = zero
            for place, (value, source) in enumerate(slots[4 * n : 4 * n + 4]):
                tile = jnp.where(row4 == place, sub_roll(value, place - source), tile)
            sd[k, n] = tile

    for copy in sends_corner:
        copy.start()

    outs = inner_operator(coarse)
    partial = combine(lambda x, y: 2.0 * x + y, coarse, outs)
    pack_traces(traces_of(partial), sp, False)

    for copy in sends_part:
        copy.start()

    for v in range(5):
        for side in range(4):
            gcor[side, v] = added[side][v]
        for i in range(2):
            for j in range(2):
                cloc[v, i, j] = coarse[v][i][j]
                cpart[v, i, j] = partial[v][i][j]

    for copy in sends3:
        copy.wait_recv()

    terms = face_terms([[own_ghost(side, r3[side ^ 1, v]) for v in range(5)] for side in range(4)])
    middle = combine(lambda x, y: x + y, load_field(cpart), terms)
    outs = inner_operator(middle)
    coarse = combine(lambda x, y, z: x + y + z, load_field(cloc), middle, outs)

    for copy in sends_corner:
        copy.wait_recv()

    def corner_rows(side, v):
        lower, upper = ((3, 1), (2, 0), (3, 2), (1, 0))[side]
        slot = 2 * v + (0 if side < 2 else 1)
        tile, place = slot // 4, slot % 4
        lower, upper = sub_roll(rd[lower, tile], -place), sub_roll(rd[upper, tile], 3 - place)
        return jnp.where(row4 == 0, lower, jnp.where(row4 == 3, upper, zero))

    beside = [[corner_rows(side, v) for v in range(5)] for side in range(4)]

    for copy in sends_part:
        copy.wait_recv()

    ghosts = []
    for side in range(4):
        values = [rp[side ^ 1, v] + (gcor[side, v] + beside[side][v]) for v in range(5)]
        if side % 2 == 0:
            turn = rg[side ^ 1, 25] == 1.0
            values = [jnp.where(turn, swap_rows(value, 2 if side < 2 else 1), value) for value in values]
        else:
            values = [own_ghost(side, value) for value in values]
        ghosts.append(values)
    coarse = combine(lambda x, y: x + y, coarse, face_terms(ghosts))

    t_first = [halves(OMEGA, OMEGA * P_FAR), halves(0.0, OMEGA * P_NEAR)]
    t_second = [halves(OMEGA * P_FAR, OMEGA), halves(OMEGA * P_NEAR, 0.0)]

    for v in range(5):
        by_a = [prolong_line([coarse[v][i][j] for i in range(2)]) for j in range(2)]
        for a in range(4):
            for b, value in enumerate(prolong_line([by_a[j][a] for j in range(2)])):
                swapped = sub_roll(value, 4)
                out[v, a, b, 0] = out[v, a, b, 0] + (t_first[0] * value + t_first[1] * swapped)
                out[v, a, b, 1] = out[v, a, b, 1] + (t_second[0] * value + t_second[1] * swapped)

    for copy in started:
        copy.wait_send()


def body(source, jacobian, damping, orient, smoother, coarse_smoother):
    field = (5, 4, 4, 2, 8, 128)
    vmem = pltpu.VMEM
    hbm = pl.BlockSpec(memory_space=pltpu.HBM)
    out = pl.pallas_call(
        kernel,
        out_shape=pltpu.VMEM(field, F32),
        in_specs=[hbm] * 6,
        out_specs=pl.BlockSpec(memory_space=pltpu.VMEM),
        scratch_shapes=[
            vmem(field, F32),
            vmem((25, 4, 4, 16, 128), jnp.bfloat16),
            vmem((25, 2, 16, 128), jnp.bfloat16),
            vmem((75, 4, 128), F32),
            vmem((75, 8, 128), F32),
            vmem((4, 128), F32),
            vmem((3, 4, 128), jnp.int32),
            vmem((3, 8, 128), jnp.int32),
            vmem((5, 8, 128), F32),
            vmem((4, 2, 2, 8, 128), F32),
            vmem((25, 2, 2, 8, 128), F32),
            vmem((25, 8, 128), F32),
            vmem(field, F32),
            vmem(field, F32),
            vmem(field, F32),
            vmem(field, F32),
            vmem(field, F32),
            vmem((5, 2, 2, 8, 128), F32),
            vmem((5, 4, 4, 8, 128), F32),
            vmem((5, 2, 2, 8, 128), F32),
            vmem((5, 2, 2, 8, 128), F32),
            vmem((4, 5, 8, 128), F32),
            vmem((3, 5, 2, 2, 8, 128), F32),
            vmem((5, 2, 2, 8, 128), F32),
            vmem((4, 2, 5, 2, 8, 128), F32),
            vmem((4, 2, 5, 2, 8, 128), F32),
            vmem((4, 5, 8, 128), F32),
            vmem((4, 5, 8, 128), F32),
            vmem((4, 5, 8, 128), F32),
            vmem((4, 5, 8, 128), F32),
            vmem((4, 5, 8, 128), F32),
            vmem((4, 5, 8, 128), F32),
            vmem((4, 3, 8, 128), F32),
            vmem((4, 3, 8, 128), F32),
            vmem((4, 26, 8, 128), F32),
            vmem((4, 26, 8, 128), F32),
            pltpu.SemaphoreType.DMA((12,)),
            pltpu.SemaphoreType.DMA((28,)),
            pltpu.SemaphoreType.DMA((28,)),
        ],
        compiler_params=pltpu.CompilerParams(collective_id=0, has_side_effects=True),
    )(
        source.reshape(field),
        jacobian.reshape(75, 4, 128),
        damping.reshape(4, 128),
        orient.reshape(3, 4, 128),
        smoother.reshape(25, 4, 4, 16, 128),
        coarse_smoother.reshape(25, 2, 16, 128),
    )
    return out.reshape(5, 4, 4, 4, 2, 2, 128)


def solution(mesh):
    in_specs = (
        P(None, None, None, None, "gx", "gy", None),
        P(None, None, None, "gx", "gy", None),
        P("gx", "gy", None),
        P(None, "gx", "gy", None),
        P(None, None, None, None, None, "gx", "gy", None),
        P(None, None, None, None, None, "gx", "gy", None),
    )
    out_specs = P(None, None, None, None, "gx", "gy", None)
    return jax.shard_map(body, mesh=mesh, in_specs=in_specs, out_specs=out_specs, check_vma=False)
```

```python
import functools
import math

import jax
import jax.numpy as jnp
import numpy as np
from jax import lax
from jax.experimental import pallas as pl
from jax.experimental.pallas import tpu as pltpu
from jax.sharding import PartitionSpec as P

MESH = pl.DeviceIdType.MESH
OMEGA = 0.8
SHIFT = 2.0
F32 = jnp.float32


def lobatto4():
    points = np.array([-1.0, -1.0 / math.sqrt(5.0), 1.0 / math.sqrt(5.0), 1.0])
    weights = np.ones(4)
    for row in range(4):
        for col in range(4):
            if row != col:
                weights[row] /= points[row] - points[col]
    slopes = np.zeros((4, 4))
    for row in range(4):
        for col in range(4):
            if row != col:
                slopes[row, col] = weights[col] / weights[row] / (points[row] - points[col])
        slopes[row, row] = -np.sum(slopes[row])
    return points, slopes


POINTS, SLOPES = lobatto4()
INTERP = np.stack([(1.0 - POINTS) / 2.0, (1.0 + POINTS) / 2.0], 1)
OPEN = SLOPES.copy()
OPEN[0, 0] = OPEN[3, 3] = OPEN[1, 1] = OPEN[2, 2] = 0.0
LIFT = 3.0
EDGE = INTERP.T @ OPEN
P_NEAR, P_FAR = float(INTERP[1, 0]), float(INTERP[2, 0])


def dot_terms(coefs, values):
    total = None
    for coef, value in zip(coefs, values):
        coef = float(coef)
        if coef == 0.0:
            continue
        term = value if coef == 1.0 else coef * value
        total = term if total is None else total + term
    return total


def rows():
    return lax.broadcasted_iota(jnp.int32, (8, 128), 0)


def halves(top, bottom):
    return jnp.where(rows() < 4, jnp.full((8, 128), float(top), F32), jnp.full((8, 128), float(bottom), F32))


def sub_roll(value, shift):
    return pltpu.roll(value, shift % 8, 0)


def lane_roll(value, shift):
    return pltpu.roll(value, shift % 128, 1)


def pack_low(first, second, mask, step):
    return jnp.where(mask, first, sub_roll(second, step))


def pack_high(first, second, mask, step):
    return jnp.where(mask, sub_roll(first, -step), second)


def z_ghosts(traces, turned):
    count = len(traces)
    low = rows() < 4
    flip = jnp.logical_and(turned, rows() >= 4)
    out = []
    for a in range(count):
        swapped = sub_roll(jnp.where(flip, traces[count - 1 - a], traces[a]), 4)
        out.append(jnp.where(low, lane_roll(swapped, 1), lane_roll(swapped, -1)))
    return [jnp.where(flip, out[count - 1 - a], out[a]) for a in range(count)]


def restrict_c(first, second):
    low = rows() < 4
    ends = jnp.where(low, first, second)
    inner_swapped = jnp.where(low, second, first)
    inner = sub_roll(inner_swapped, 4)
    return ends, inner, inner_swapped, ends + P_NEAR * inner + P_FAR * inner_swapped


def restrict_line(values):
    low = values[0] + P_NEAR * values[1] + P_FAR * values[2]
    high = values[3] + P_NEAR * values[2] + P_FAR * values[1]
    return [low, high]


def prolong_line(values):
    return [
        values[0],
        P_NEAR * values[0] + P_FAR * values[1],
        P_FAR * values[0] + P_NEAR * values[1],
        values[1],
    ]


CORNERS = ((2, 0, 0, 0), (2, 1, 3, 0), (3, 0, 0, 3), (3, 1, 3, 3))


def swap_rows(value, step):
    return jnp.where((rows() & step) == 0, sub_roll(value, -step), sub_roll(value, step))


def kernel(
    src_hbm, jac_hbm, damp_hbm, flag_hbm, smo_hbm, csm_hbm, out,
    src, smo, csm, jraw, jn, draw, fraw, flags, dmp, kfine, csf, kface,
    q, acc, wx, wy, wz, rsrc, rcs, cloc, cpart, gcor, wc, crhs,
    s1, r1, s2, r2, s3, r3, sp, rp, sd, rd, sg, rg, in_sem, send_sem, recv_sem,
):
    nx, ny = lax.axis_size("gx"), lax.axis_size("gy")
    ix, iy = lax.axis_index("gx"), lax.axis_index("gy")
    x_next, x_prev = lax.rem(ix + 1, nx), lax.rem(ix + nx - 1, nx)
    y_next, y_prev = lax.rem(iy + 1, ny), lax.rem(iy + ny - 1, ny)
    partners = [(x_prev, iy), (x_next, iy), (ix, y_prev), (ix, y_next)]
    corners = [(x_prev, y_prev), (x_next, y_prev), (x_prev, y_next), (x_next, y_next)]

    barrier = pltpu.get_barrier_semaphore()
    for partner in partners:
        pl.semaphore_signal(barrier, inc=1, device_id=partner, device_id_type=MESH)

    loads = []

    def load(source, target):
        copy = pltpu.make_async_copy(source, target, in_sem.at[len(loads)])
        copy.start()
        loads.append(copy)
        return copy

    parts = {}
    flag_load = load(flag_hbm, fraw)
    damp_load = load(damp_hbm, draw)
    jac_load = load(jac_hbm, jraw)
    csm_load = load(csm_hbm, csm)
    for a in (0, 3, 1, 2):
        parts[a] = (load(src_hbm.at[:, a], src.at[:, a]), load(smo_hbm.at[:, a], smo.at[:, a]))

    started = []

    def remote(source, target, number, partner):
        copy = pltpu.make_async_remote_copy(
            src_ref=source, dst_ref=target, send_sem=send_sem.at[number], recv_sem=recv_sem.at[number],
            device_id=partner, device_id_type=MESH,
        )
        started.append(copy)
        return copy

    sends1 = [[remote(s1.at[k, h], r1.at[k, h], 2 * k + h, partners[k]) for h in range(2)] for k in range(2)]
    sends1 += [[remote(s1.at[k], r1.at[k], 2 * k, partners[k])] for k in range(2, 4)]
    sends2 = [remote(s2.at[k], r2.at[k], 8 + k, partners[k]) for k in range(4)]
    sends3 = [remote(s3.at[k], r3.at[k], 12 + k, partners[k]) for k in range(4)]
    sends_part = [remote(sp.at[k], rp.at[k], 16 + k, partners[k]) for k in range(4)]
    sends_corner = [remote(sd.at[k], rd.at[k], 20 + k, corners[k]) for k in range(4)]
    sends_face = [remote(sg.at[k], rg.at[k], 24 + k, partners[k]) for k in range(4)]

    low = rows() < 4
    x0 = (rows() & 2) == 0
    y0 = (rows() & 1) == 0
    zero = jnp.zeros((8, 128), F32)
    row4 = rows() & 3

    def smooth(a, b, fields):
        outs = []
        for vo in range(5):
            pair = [None, None]
            for vi in range(5):
                block = smo[5 * vo + vi, a, b].astype(F32)
                for half in range(2):
                    term = block[8 * half : 8 * half + 8] * fields[vi][half]
                    pair[half] = term if vi == 0 else pair[half] + term
            outs.append(pair)
        return outs

    def first_pass(a, b):
        fields = [[src[v, a, b, 0], src[v, a, b, 1]] for v in range(5)]
        outs = smooth(a, b, fields)
        for v in range(5):
            q[v, a, b, 0] = outs[v][0]
            q[v, a, b, 1] = outs[v][1]

    flag_load.wait()
    damp_load.wait()
    for d in range(3):
        flags[d] = jnp.concatenate([fraw[d], fraw[d]], axis=0)
    fx, fy, fz = (flags[d] == 1 for d in range(3))
    damping = jnp.concatenate([draw[...], draw[...]], axis=0)
    dmp[0] = (OMEGA * LIFT) * damping
    dmp[1] = (OMEGA * 0.5) * damping
    dmp[2] = OMEGA * SHIFT + (OMEGA * 1.5) * damping
    dmp[3] = jnp.where(low, (OMEGA * LIFT) * damping, 0.0)
    dmp[4] = jnp.where(low, 0.0, (OMEGA * LIFT) * damping)
    for b in range(4):
        for a_end in range(2):
            faces = a_end + (1 if b in (0, 3) else 0)
            base = OMEGA * SHIFT + (OMEGA * LIFT * faces) * damping
            kfine[b, a_end, 0] = base + dmp[3]
            kfine[b, a_end, 1] = base + dmp[4]

    jac_load.wait()

    @pl.loop(0, 75, unroll=15)
    def _(i):
        block = jraw[i]
        jn[i] = (-OMEGA) * jnp.concatenate([block, block], axis=0)

    csm_load.wait()

    @pl.loop(0, 25, unroll=5)
    def _(i):
        for n in range(2):
            block = csm[i, n].astype(F32)
            csf[i, n, 0] = block[:8]
            csf[i, n, 1] = block[8:]

    half_damp, k_coarse, lift_damp = dmp[1], dmp[2], dmp[0]

    def pack_side(side, first, second):
        mask, step = (x0, 2) if side < 2 else (y0, 1)
        return (pack_low if side % 2 == 0 else pack_high)(first, second, mask, step)

    for side in range(4):
        own = 0 if side < 2 else 1
        sign = -0.5 if side % 2 == 0 else 0.5

        @pl.loop(0, 5, unroll=True)
        def _(row, side=side, own=own, sign=sign):
            for col in range(5):
                diag = jnp.where(row == col, half_damp, zero)
                face = diag + sign * jn[25 * own + 5 * row + col]
                kface[5 * row + col] = pack_side(side, face, face)

        @pl.loop(0, 5, unroll=True)
        def _(vo, side=side):
            blocks = []
            for m in range(5):
                if side < 2:
                    pair = [csf[5 * vo + m, side, j] for j in range(2)]
                else:
                    pair = [csf[5 * vo + m, i, side - 2] for i in range(2)]
                blocks.append(pack_side(side, pair[0], pair[1]))
            for vi in range(5):
                total = blocks[0] * kface[vi]
                for m in range(1, 5):
                    total = total + blocks[m] * kface[5 * m + vi]
                sg[side, 5 * vo + vi] = total

        flag = jnp.where(flags[own] == 1, 1.0, 0.0)
        sg[side, 25] = pack_side(side, flag, flag)

    for a in (0, 3):
        for copy in parts[a]:
            copy.wait()

        @pl.loop(0, 4)
        def _(b, a=a):
            first_pass(a, b)

    HALF = {0: (0, 0), 3: (0, 1), 1: (1, 0), 2: (1, 1)}

    @pl.loop(0, 5, unroll=True)
    def _(v):
        for b in range(4):
            half, place = HALF[b]
            s1[0, half, v, place] = pack_low(q[v, 0, b, 0], q[v, 0, b, 1], x0, 2)
            hi = [jnp.where(fx, q[v, 3, 3 - b, h], q[v, 3, b, h]) for h in range(2)]
            s1[1, half, v, place] = pack_high(hi[0], hi[1], x0, 2)

    pl.semaphore_wait(barrier, 4)
    for half in range(2):
        for k in range(2):
            sends1[k][half].start()

    for a in (1, 2):
        for copy in parts[a]:
            copy.wait()

        @pl.loop(0, 4)
        def _(b, a=a):
            first_pass(a, b)

    @pl.loop(0, 5, unroll=True)
    def _(v):
        for a in range(4):
            s1[2, a // 2, v, a % 2] = pack_low(q[v, a, 0, 0], q[v, a, 0, 1], y0, 1)
            hi = [jnp.where(fy, q[v, 3 - a, 3, h], q[v, a, 3, h]) for h in range(2)]
            s1[3, a // 2, v, a % 2] = pack_high(hi[0], hi[1], y0, 1)

    sends1[2][0].start()
    sends1[3][0].start()


    c_first = [halves(OPEN[0, 1], OPEN[1, 0]), halves(OPEN[0, 2], OPEN[1, 3]), halves(OPEN[0, 3], OPEN[1, 2])]
    c_second = [halves(OPEN[2, 3], OPEN[3, 2]), halves(OPEN[2, 0], OPEN[3, 1]), halves(OPEN[2, 1], OPEN[3, 0])]
    c_ghost = [halves(-LIFT, 0.0), halves(0.0, LIFT)]

    @pl.loop(0, 20, unroll=4)
    def _(t):
        v, b = t // 4, t % 4
        first = [q[v, a, b, 0] for a in range(4)]
        second = [q[v, a, b, 1] for a in range(4)]
        for a in range(4):
            for h, line in enumerate((first, second)):
                wx[v, a, b, h] = dot_terms(OPEN[a], line)
        ghosts = z_ghosts([jnp.where(low, first[a], second[a]) for a in range(4)], fz)
        for a in range(4):
            a_end = 1 if a in (0, 3) else 0
            first_sw, second_sw = sub_roll(first[a], 4), sub_roll(second[a], 4)
            wz[v, a, b, 0] = (
                c_first[0] * first_sw + c_first[1] * second[a] + c_first[2] * second_sw + c_ghost[0] * ghosts[a]
            )
            wz[v, a, b, 1] = (
                c_second[0] * second_sw + c_second[1] * first[a] + c_second[2] * first_sw + c_ghost[1] * ghosts[a]
            )
            acc[v, a, b, 0] = src[v, a, b, 0] - kfine[b, a_end, 0] * first[a] + dmp[3] * ghosts[a]
            acc[v, a, b, 1] = src[v, a, b, 1] - kfine[b, a_end, 1] * second[a] + dmp[4] * ghosts[a]

    @pl.loop(0, 20, unroll=4)
    def _(t):
        v, a = t // 4, t % 4
        for h in range(2):
            line = [q[v, a, b, h] for b in range(4)]
            for b in range(4):
                wy[v, a, b, h] = dot_terms(OPEN[b], line)

    def mix_at(b, pair, directions, last):
        total = [[[acc[v, a, b, h] for h in range(2)] for a in pair] for v in range(5)]
        for d in directions:
            w = (wx, wy, wz)[d]
            for vi in range(5):
                flux = [[w[vi, a, b, h] for h in range(2)] for a in pair]
                for vo in range(5):
                    weight = jn[25 * d + 5 * vo + vi]
                    for n in range(2):
                        for h in range(2):
                            total[vo][n][h] = total[vo][n][h] + weight * flux[n][h]
        for n, a in enumerate(pair):
            if last:
                outs = smooth(a, b, [total[v][n] for v in range(5)])
            for v in range(5):
                for h in range(2):
                    if last:
                        q[v, a, b, h] = q[v, a, b, h] + outs[v][h]
                    else:
                        acc[v, a, b, h] = total[v][n][h]

    def mix(first, step, pair, directions, last):
        @pl.loop(0, 2)
        def _(t):
            mix_at(first + step * t, pair, directions, last)

    mix(0, 3, (0, 3), (2,), False)
    mix(0, 3, (1, 2), (0, 2), False)

    for copy in sends_face:
        copy.start()

    @pl.loop(0, 5, unroll=True)
    def _(v):
        by_a = []
        for a in range(4):
            by_a.append(restrict_line([restrict_c(src[v, a, b, 0], src[v, a, b, 1])[3] for b in range(4)]))
        for j in range(2):
            for i, value in enumerate(restrict_line([by_a[a][j] for a in range(4)])):
                rsrc[v, i, j] = value

    mix(1, 1, (0, 3), (1, 2), False)
    mix(1, 1, (1, 2), (0, 1, 2), True)

    sends1[2][0].wait_recv()
    sends1[3][0].wait_recv()

    @pl.loop(0, 5, unroll=True)
    def _(v):
        for h in range(2):
            lo = [q[v, a, 0, h] for a in range(4)]
            hi = [q[v, a, 3, h] for a in range(4)]
            right = []
            for a in range(4):
                packed = r1[2, a // 2, v, a % 2]
                right.append(jnp.where(y0, sub_roll(lo[a], -1), sub_roll(packed, 1) if h == 0 else packed))
            for a in range(4):
                packed = r1[3, a // 2, v, a % 2]
                hi_turned = jnp.where(fy, hi[3 - a], hi[a])
                left = jnp.where(y0, packed if h == 0 else sub_roll(packed, -1), sub_roll(hi_turned, 1))
                ghost = jnp.where(fy, right[3 - a], right[a])
                wy[v, a, 0, h] = wy[v, a, 0, h] - LIFT * left
                wy[v, a, 3, h] = wy[v, a, 3, h] + LIFT * ghost
                acc[v, a, 0, h] = acc[v, a, 0, h] + lift_damp * left
                acc[v, a, 3, h] = acc[v, a, 3, h] + lift_damp * ghost

    mix(0, 3, (0, 3), (1,), False)
    mix(0, 3, (1, 2), (1,), True)

    def restrict_c_into(v, a_list):
        for a in a_list:
            for b in range(4):
                rcs[v, a, b] = restrict_c(q[v, a, b, 0], q[v, a, b, 1])[3]

    @pl.loop(0, 5, unroll=True)
    def _(v):
        restrict_c_into(v, (1, 2))

    for half, nodes in enumerate(((0, 3), (1, 2))):
        sends1[0][half].wait_recv()
        sends1[1][half].wait_recv()

        @pl.loop(0, 5, unroll=True)
        def _(v, half=half, nodes=nodes):
            for h in range(2):
                lo = [q[v, 0, b, h] for b in nodes]
                hi = [q[v, 3, b, h] for b in nodes]
                right = []
                for n in range(2):
                    packed = r1[0, half, v, n]
                    right.append(jnp.where(x0, sub_roll(lo[n], -2), sub_roll(packed, 2) if h == 0 else packed))
                for n, b in enumerate(nodes):
                    packed = r1[1, half, v, n]
                    hi_turned = jnp.where(fx, hi[1 - n], hi[n])
                    left = jnp.where(x0, packed if h == 0 else sub_roll(packed, -2), sub_roll(hi_turned, 2))
                    ghost = jnp.where(fx, right[1 - n], right[n])
                    wx[v, 0, b, h] = wx[v, 0, b, h] - LIFT * left
                    wx[v, 3, b, h] = wx[v, 3, b, h] + LIFT * ghost
                    acc[v, 0, b, h] = acc[v, 0, b, h] + lift_damp * left
                    acc[v, 3, b, h] = acc[v, 3, b, h] + lift_damp * ghost

        for b in nodes:
            mix_at(b, (0, 3), (0,), True)

    def traces_of(field):
        return [
            [[field[v][0][n] for n in range(2)] for v in range(5)],
            [[field[v][1][n] for n in range(2)] for v in range(5)],
            [[field[v][n][0] for n in range(2)] for v in range(5)],
            [[field[v][n][1] for n in range(2)] for v in range(5)],
        ]

    def pack_traces(traces, target, turn):
        for v in range(5):
            for side in range(4):
                pair = traces[side][v]
                if turn and side % 2 == 1:
                    flip = fx if side < 2 else fy
                    pair = [jnp.where(flip, pair[1 - n], pair[n]) for n in range(2)]
                target[side, v] = pack_side(side, pair[0], pair[1])

    traces = [[None] * 5 for _ in range(4)]
    for v in range(5):
        restrict_c_into(v, (0, 3))
        for slot, a in ((0, 0), (1, 3)):
            traces[slot][v] = restrict_line([rcs[v, a, b] for b in range(4)])
        for slot, b in ((2, 0), (3, 3)):
            traces[slot][v] = restrict_line([rcs[v, a, b] for a in range(4)])
    pack_traces(traces, s2, True)

    for copy in sends2:
        copy.start()

    def inner_ghosts(lo, hi, mask, step, flip):
        right = [jnp.where(mask, sub_roll(value, -step), zero) for value in lo]
        right = [jnp.where(flip, right[1 - n], right[n]) for n in range(2)]
        hi = [jnp.where(flip, hi[1 - n], hi[n]) for n in range(2)]
        left = [jnp.where(mask, zero, sub_roll(value, step)) for value in hi]
        return left, right

    def coarse_sweep():
        total = [[[crhs[v, i, j] for j in range(2)] for i in range(2)] for v in range(5)]
        for d in range(3):
            for vi in range(5):
                flux = [[wc[d, vi, i, j] for j in range(2)] for i in range(2)]
                for vo in range(5):
                    weight = jn[25 * d + 5 * vo + vi]
                    for i in range(2):
                        for j in range(2):
                            total[vo][i][j] = total[vo][i][j] + weight * flux[i][j]
        outs = [[[None, None] for _ in range(2)] for _ in range(5)]
        for vo in range(5):
            for vi in range(5):
                for i in range(2):
                    for j in range(2):
                        term = csf[5 * vo + vi, i, j] * total[vi][i][j]
                        outs[vo][i][j] = term if vi == 0 else outs[vo][i][j] + term
        return outs

    e_ends = halves(EDGE[0, 0], EDGE[1, 3])
    e_ends_sw = halves(EDGE[0, 3], EDGE[1, 0])
    e_inner = halves(EDGE[0, 1], EDGE[1, 2])
    e_inner_sw = halves(EDGE[0, 2], EDGE[1, 1])
    z_lift = halves(-LIFT, LIFT)

    for v in range(5):
        rbc = [restrict_line([rcs[v, a, b] for b in range(4)]) for a in range(4)]
        rac = [restrict_line([rcs[v, a, b] for a in range(4)]) for b in range(4)]
        ra = [[restrict_line([q[v, a, b, h] for a in range(4)]) for b in range(4)] for h in range(2)]
        ends_of = [[None, None], [None, None]]
        rhs = [[None, None], [None, None]]
        w = [[[None, None], [None, None]] for _ in range(3)]
        for i in range(2):
            first = restrict_line([ra[0][b][i] for b in range(4)])
            second = restrict_line([ra[1][b][i] for b in range(4)])
            for j in range(2):
                w[0][i][j] = dot_terms(EDGE[i], [rbc[a][j] for a in range(4)])
                w[1][i][j] = dot_terms(EDGE[j], [rac[b][i] for b in range(4)])
                ends, inner, inner_sw, full = restrict_c(first[j], second[j])
                ends_of[j][i] = ends
                w[2][i][j] = (
                    e_ends * ends + e_ends_sw * sub_roll(ends, 4) + e_inner * inner + e_inner_sw * inner_sw
                )
                rhs[i][j] = rsrc[v, i, j] - (OMEGA * SHIFT) * full
        for j in range(2):
            ghosts = z_ghosts(ends_of[j], fz)
            for i in range(2):
                w[2][i][j] = w[2][i][j] + z_lift * ghosts[i]
                rhs[i][j] = rhs[i][j] + lift_damp * (ghosts[i] - ends_of[j][i])
        left, right = inner_ghosts(traces[0][v], traces[1][v], x0, 2, fx)
        for j in range(2):
            w[0][0][j] = w[0][0][j] - LIFT * left[j]
            w[0][1][j] = w[0][1][j] + LIFT * right[j]
            rhs[0][j] = rhs[0][j] + lift_damp * (left[j] - traces[0][v][j])
            rhs[1][j] = rhs[1][j] + lift_damp * (right[j] - traces[1][v][j])
        left, right = inner_ghosts(traces[2][v], traces[3][v], y0, 1, fy)
        for i in range(2):
            w[1][i][0] = w[1][i][0] - LIFT * left[i]
            w[1][i][1] = w[1][i][1] + LIFT * right[i]
            rhs[i][0] = rhs[i][0] + lift_damp * (left[i] - traces[2][v][i])
            rhs[i][1] = rhs[i][1] + lift_damp * (right[i] - traces[3][v][i])
        for i in range(2):
            for j in range(2):
                crhs[v, i, j] = rhs[i][j]
                for d in range(3):
                    wc[d, v, i, j] = w[d][i][j]

    outs = coarse_sweep()
    for v in range(5):
        for i in range(2):
            for j in range(2):
                cloc[v, i, j] = outs[v][i][j]

    @pl.loop(0, 20, unroll=4)
    def _(t):
        v, b = t // 4, t % 4
        for a in range(4):
            for h in range(2):
                out[v, a, b, h] = OMEGA * q[v, a, b, h]

    def face_product(ref, side, vectors):
        outs = []
        for vo in range(5):
            total = ref[side, 5 * vo] * vectors[0]
            for vi in range(1, 5):
                total = total + ref[side, 5 * vo + vi] * vectors[vi]
            outs.append(total)
        return outs

    def own_ghost(side, value):
        if side % 2 == 0:
            return value
        return jnp.where(sg[side, 25] == 1.0, swap_rows(value, 2 if side < 2 else 1), value)

    def face_terms(ghosts):
        pairs = [[None] * 5 for _ in range(4)]
        for side in range(4):
            mask, step = (x0, 2) if side < 2 else (y0, 1)
            for v, delta in enumerate(face_product(sg, side, ghosts[side])):
                if side % 2 == 0:
                    pairs[side][v] = [
                        jnp.where(mask, delta, zero), jnp.where(mask, sub_roll(delta, -step), zero)
                    ]
                else:
                    pairs[side][v] = [
                        jnp.where(mask, zero, sub_roll(delta, step)), jnp.where(mask, zero, delta)
                    ]
        return [[[pairs[i][v][j] + pairs[2 + j][v][i] for j in range(2)] for i in range(2)] for v in range(5)]

    def inner_operator(field):
        for v in range(5):
            here = field[v]
            rhs = [[(-k_coarse) * here[i][j] for j in range(2)] for i in range(2)]
            for j in range(2):
                ghosts = z_ghosts([here[i][j] for i in range(2)], fz)
                for i in range(2):
                    swapped = sub_roll(here[i][j], 4)
                    wc[2, v, i, j] = jnp.where(low, 0.5, -0.5) * (swapped - ghosts[i])
                    rhs[i][j] = rhs[i][j] + half_damp * ghosts[i]
            left, right = inner_ghosts(here[0], here[1], x0, 2, fx)
            for j in range(2):
                wc[0, v, 0, j] = 0.5 * (here[1][j] - left[j])
                wc[0, v, 1, j] = 0.5 * (right[j] - here[0][j])
                rhs[0][j] = rhs[0][j] + half_damp * left[j]
                rhs[1][j] = rhs[1][j] + half_damp * right[j]
            left, right = inner_ghosts([here[i][0] for i in range(2)], [here[i][1] for i in range(2)], y0, 1, fy)
            for i in range(2):
                wc[1, v, i, 0] = 0.5 * (here[i][1] - left[i])
                wc[1, v, i, 1] = 0.5 * (right[i] - here[i][0])
                rhs[i][0] = rhs[i][0] + half_damp * left[i]
                rhs[i][1] = rhs[i][1] + half_damp * right[i]
            for i in range(2):
                for j in range(2):
                    crhs[v, i, j] = rhs[i][j]
        return coarse_sweep()

    def combine(function, *fields):
        return [
            [[function(*(f[v][i][j] for f in fields)) for j in range(2)] for i in range(2)] for v in range(5)
        ]

    def load_field(ref):
        return [[[ref[v, i, j] for j in range(2)] for i in range(2)] for v in range(5)]

    for copy in sends2:
        copy.wait_recv()
    terms = face_terms([[own_ghost(side, r2[side ^ 1, v]) for v in range(5)] for side in range(4)])
    coarse = combine(lambda x, y: x + 6.0 * y, load_field(cloc), terms)
    pack_traces(traces_of(coarse), s3, True)
    for copy in sends3[:2]:
        copy.start()

    for copy in sends_face:
        copy.wait_recv()

    added = []
    for side in range(4):
        mine = [s3[side, v] for v in range(5)]
        if side % 2 == 0:
            turn = rg[side ^ 1, 25] == 1.0
            mine = [jnp.where(turn, swap_rows(value, 2 if side < 2 else 1), value) for value in mine]
        added.append(face_product(rg, side ^ 1, mine))
    for k, (along_y, along_x, y_row, x_row) in enumerate(CORNERS):
        slots = []
        for v in range(5):
            slots += [(added[along_y][v], y_row), (added[along_x][v], x_row)]
        for n in range(3):
            tile = zero
            for place, (value, source) in enumerate(slots[4 * n : 4 * n + 4]):
                tile = jnp.where(row4 == place, sub_roll(value, place - source), tile)
            sd[k, n] = tile

    for copy in sends_corner + sends3[2:]:
        copy.start()

    outs = inner_operator(coarse)
    partial = combine(lambda x, y: 2.0 * x + y, coarse, outs)
    pack_traces(traces_of(partial), sp, False)

    for copy in sends_part:
        copy.start()

    for v in range(5):
        for side in range(4):
            gcor[side, v] = added[side][v]
        for i in range(2):
            for j in range(2):
                cloc[v, i, j] = coarse[v][i][j]
                cpart[v, i, j] = partial[v][i][j]

    for copy in sends3:
        copy.wait_recv()

    terms = face_terms([[own_ghost(side, r3[side ^ 1, v]) for v in range(5)] for side in range(4)])
    middle = combine(lambda x, y: x + y, load_field(cpart), terms)
    outs = inner_operator(middle)
    coarse = combine(lambda x, y, z: x + y + z, load_field(cloc), middle, outs)

    for copy in sends_corner:
        copy.wait_recv()

    def corner_rows(side, v):
        lower, upper = ((3, 1), (2, 0), (3, 2), (1, 0))[side]
        slot = 2 * v + (0 if side < 2 else 1)
        tile, place = slot // 4, slot % 4
        lower, upper = sub_roll(rd[lower, tile], -place), sub_roll(rd[upper, tile], 3 - place)
        return jnp.where(row4 == 0, lower, jnp.where(row4 == 3, upper, zero))

    beside = [[corner_rows(side, v) for v in range(5)] for side in range(4)]

    for copy in sends_part:
        copy.wait_recv()

    ghosts = []
    for side in range(4):
        values = [rp[side ^ 1, v] + (gcor[side, v] + beside[side][v]) for v in range(5)]
        if side % 2 == 0:
            turn = rg[side ^ 1, 25] == 1.0
            values = [jnp.where(turn, swap_rows(value, 2 if side < 2 else 1), value) for value in values]
        else:
            values = [own_ghost(side, value) for value in values]
        ghosts.append(values)
    coarse = combine(lambda x, y: x + y, coarse, face_terms(ghosts))

    t_first = [halves(OMEGA, OMEGA * P_FAR), halves(0.0, OMEGA * P_NEAR)]
    t_second = [halves(OMEGA * P_FAR, OMEGA), halves(OMEGA * P_NEAR, 0.0)]

    for v in range(5):
        by_a = [prolong_line([coarse[v][i][j] for i in range(2)]) for j in range(2)]
        for a in range(4):
            for b, value in enumerate(prolong_line([by_a[j][a] for j in range(2)])):
                swapped = sub_roll(value, 4)
                out[v, a, b, 0] = out[v, a, b, 0] + (t_first[0] * value + t_first[1] * swapped)
                out[v, a, b, 1] = out[v, a, b, 1] + (t_second[0] * value + t_second[1] * swapped)

    for copy in started:
        copy.wait_send()


def body(source, jacobian, damping, orient, smoother, coarse_smoother):
    field = (5, 4, 4, 2, 8, 128)
    vmem = pltpu.VMEM
    hbm = pl.BlockSpec(memory_space=pltpu.HBM)
    out = pl.pallas_call(
        kernel,
        out_shape=pltpu.VMEM(field, F32),
        in_specs=[hbm] * 6,
        out_specs=pl.BlockSpec(memory_space=pltpu.VMEM),
        scratch_shapes=[
            vmem(field, F32),
            vmem((25, 4, 4, 16, 128), jnp.bfloat16),
            vmem((25, 2, 16, 128), jnp.bfloat16),
            vmem((75, 4, 128), F32),
            vmem((75, 8, 128), F32),
            vmem((4, 128), F32),
            vmem((3, 4, 128), jnp.int32),
            vmem((3, 8, 128), jnp.int32),
            vmem((5, 8, 128), F32),
            vmem((4, 2, 2, 8, 128), F32),
            vmem((25, 2, 2, 8, 128), F32),
            vmem((25, 8, 128), F32),
            vmem(field, F32),
            vmem(field, F32),
            vmem(field, F32),
            vmem(field, F32),
            vmem(field, F32),
            vmem((5, 2, 2, 8, 128), F32),
            vmem((5, 4, 4, 8, 128), F32),
            vmem((5, 2, 2, 8, 128), F32),
            vmem((5, 2, 2, 8, 128), F32),
            vmem((4, 5, 8, 128), F32),
            vmem((3, 5, 2, 2, 8, 128), F32),
            vmem((5, 2, 2, 8, 128), F32),
            vmem((4, 2, 5, 2, 8, 128), F32),
            vmem((4, 2, 5, 2, 8, 128), F32),
            vmem((4, 5, 8, 128), F32),
            vmem((4, 5, 8, 128), F32),
            vmem((4, 5, 8, 128), F32),
            vmem((4, 5, 8, 128), F32),
            vmem((4, 5, 8, 128), F32),
            vmem((4, 5, 8, 128), F32),
            vmem((4, 3, 8, 128), F32),
            vmem((4, 3, 8, 128), F32),
            vmem((4, 26, 8, 128), F32),
            vmem((4, 26, 8, 128), F32),
            pltpu.SemaphoreType.DMA((12,)),
            pltpu.SemaphoreType.DMA((28,)),
            pltpu.SemaphoreType.DMA((28,)),
        ],
        compiler_params=pltpu.CompilerParams(collective_id=0, has_side_effects=True),
    )(
        source.reshape(field),
        jacobian.reshape(75, 4, 128),
        damping.reshape(4, 128),
        orient.reshape(3, 4, 128),
        smoother.reshape(25, 4, 4, 16, 128),
        coarse_smoother.reshape(25, 2, 16, 128),
    )
    return out.reshape(5, 4, 4, 4, 2, 2, 128)


def solution(mesh):
    in_specs = (
        P(None, None, None, None, "gx", "gy", None),
        P(None, None, None, "gx", "gy", None),
        P("gx", "gy", None),
        P(None, "gx", "gy", None),
        P(None, None, None, None, None, "gx", "gy", None),
        P(None, None, None, None, None, "gx", "gy", None),
    )
    out_specs = P(None, None, None, None, "gx", "gy", None)
    return jax.shard_map(body, mesh=mesh, in_specs=in_specs, out_specs=out_specs, check_vma=False)
```

```python
import functools
import math

import jax
import jax.numpy as jnp
import numpy as np
from jax import lax
from jax.experimental import pallas as pl
from jax.experimental.pallas import tpu as pltpu
from jax.sharding import PartitionSpec as P

MESH = pl.DeviceIdType.MESH
OMEGA = 0.8
SHIFT = 2.0
F32 = jnp.float32


def lobatto4():
    points = np.array([-1.0, -1.0 / math.sqrt(5.0), 1.0 / math.sqrt(5.0), 1.0])
    weights = np.ones(4)
    for row in range(4):
        for col in range(4):
            if row != col:
                weights[row] /= points[row] - points[col]
    slopes = np.zeros((4, 4))
    for row in range(4):
        for col in range(4):
            if row != col:
                slopes[row, col] = weights[col] / weights[row] / (points[row] - points[col])
        slopes[row, row] = -np.sum(slopes[row])
    return points, slopes


POINTS, SLOPES = lobatto4()
INTERP = np.stack([(1.0 - POINTS) / 2.0, (1.0 + POINTS) / 2.0], 1)
OPEN = SLOPES.copy()
OPEN[0, 0] = OPEN[3, 3] = OPEN[1, 1] = OPEN[2, 2] = 0.0
LIFT = 3.0
EDGE = INTERP.T @ OPEN
P_NEAR, P_FAR = float(INTERP[1, 0]), float(INTERP[2, 0])


def dot_terms(coefs, values):
    total = None
    for coef, value in zip(coefs, values):
        coef = float(coef)
        if coef == 0.0:
            continue
        term = value if coef == 1.0 else coef * value
        total = term if total is None else total + term
    return total


def rows():
    return lax.broadcasted_iota(jnp.int32, (8, 128), 0)


def halves(top, bottom):
    return jnp.where(rows() < 4, jnp.full((8, 128), float(top), F32), jnp.full((8, 128), float(bottom), F32))


def sub_roll(value, shift):
    return pltpu.roll(value, shift % 8, 0)


def lane_roll(value, shift):
    return pltpu.roll(value, shift % 128, 1)


def pack_low(first, second, mask, step):
    return jnp.where(mask, first, sub_roll(second, step))


def pack_high(first, second, mask, step):
    return jnp.where(mask, sub_roll(first, -step), second)


def z_ghosts(traces, turned):
    count = len(traces)
    low = rows() < 4
    flip = jnp.logical_and(turned, rows() >= 4)
    out = []
    for a in range(count):
        swapped = sub_roll(jnp.where(flip, traces[count - 1 - a], traces[a]), 4)
        out.append(jnp.where(low, lane_roll(swapped, 1), lane_roll(swapped, -1)))
    return [jnp.where(flip, out[count - 1 - a], out[a]) for a in range(count)]


def restrict_c(first, second):
    low = rows() < 4
    ends = jnp.where(low, first, second)
    inner_swapped = jnp.where(low, second, first)
    inner = sub_roll(inner_swapped, 4)
    return ends, inner, inner_swapped, ends + P_NEAR * inner + P_FAR * inner_swapped


def restrict_line(values):
    low = values[0] + P_NEAR * values[1] + P_FAR * values[2]
    high = values[3] + P_NEAR * values[2] + P_FAR * values[1]
    return [low, high]


def prolong_line(values):
    return [
        values[0],
        P_NEAR * values[0] + P_FAR * values[1],
        P_FAR * values[0] + P_NEAR * values[1],
        values[1],
    ]


CORNERS = ((2, 0, 0, 0), (2, 1, 3, 0), (3, 0, 0, 3), (3, 1, 3, 3))


def swap_rows(value, step):
    return jnp.where((rows() & step) == 0, sub_roll(value, -step), sub_roll(value, step))


def kernel(
    src_hbm, jac_hbm, damp_hbm, flag_hbm, smo_hbm, csm_hbm, out,
    src, smo, csm, jraw, jn, draw, fraw, flags, dmp, kfine, csf, kface,
    q, acc, wx, wy, wz, rsrc, rcs, cloc, cpart, gcor, wc, crhs,
    s1, r1, s2, r2, s3, r3, sp, rp, sd, rd, sg, rg, in_sem, send_sem, recv_sem,
):
    nx, ny = lax.axis_size("gx"), lax.axis_size("gy")
    ix, iy = lax.axis_index("gx"), lax.axis_index("gy")
    x_next, x_prev = lax.rem(ix + 1, nx), lax.rem(ix + nx - 1, nx)
    y_next, y_prev = lax.rem(iy + 1, ny), lax.rem(iy + ny - 1, ny)
    partners = [(x_prev, iy), (x_next, iy), (ix, y_prev), (ix, y_next)]
    corners = [(x_prev, y_prev), (x_next, y_prev), (x_prev, y_next), (x_next, y_next)]

    barrier = pltpu.get_barrier_semaphore()
    for partner in partners:
        pl.semaphore_signal(barrier, inc=1, device_id=partner, device_id_type=MESH)

    loads = []

    def load(source, target):
        copy = pltpu.make_async_copy(source, target, in_sem.at[len(loads)])
        copy.start()
        loads.append(copy)
        return copy

    parts = {}
    flag_load = load(flag_hbm, fraw)
    damp_load = load(damp_hbm, draw)
    jac_load = load(jac_hbm, jraw)
    csm_load = load(csm_hbm, csm)
    for a in (0, 3, 1, 2):
        parts[a] = (load(src_hbm.at[:, a], src.at[:, a]), load(smo_hbm.at[:, a], smo.at[:, a]))

    started = []

    def remote(source, target, number, partner):
        copy = pltpu.make_async_remote_copy(
            src_ref=source, dst_ref=target, send_sem=send_sem.at[number], recv_sem=recv_sem.at[number],
            device_id=partner, device_id_type=MESH,
        )
        started.append(copy)
        return copy

    sends1 = [[remote(s1.at[k, h], r1.at[k, h], 2 * k + h, partners[k]) for h in range(2)] for k in range(2)]
    sends1 += [[remote(s1.at[k], r1.at[k], 2 * k, partners[k])] for k in range(2, 4)]
    sends2 = [remote(s2.at[k], r2.at[k], 8 + k, partners[k]) for k in range(4)]
    sends3 = [remote(s3.at[k], r3.at[k], 12 + k, partners[k]) for k in range(4)]
    sends_part = [remote(sp.at[k], rp.at[k], 16 + k, partners[k]) for k in range(4)]
    sends_corner = [remote(sd.at[k], rd.at[k], 20 + k, corners[k]) for k in range(4)]
    sends_face = [remote(sg.at[k], rg.at[k], 24 + k, partners[k]) for k in range(4)]

    low = rows() < 4
    x0 = (rows() & 2) == 0
    y0 = (rows() & 1) == 0
    zero = jnp.zeros((8, 128), F32)
    row4 = rows() & 3

    def smooth(a, b, fields):
        outs = []
        for vo in range(5):
            pair = [None, None]
            for vi in range(5):
                block = smo[5 * vo + vi, a, b].astype(F32)
                for half in range(2):
                    term = block[8 * half : 8 * half + 8] * fields[vi][half]
                    pair[half] = term if vi == 0 else pair[half] + term
            outs.append(pair)
        return outs

    def first_pass(a, b):
        fields = [[src[v, a, b, 0], src[v, a, b, 1]] for v in range(5)]
        outs = smooth(a, b, fields)
        for v in range(5):
            q[v, a, b, 0] = outs[v][0]
            q[v, a, b, 1] = outs[v][1]

    flag_load.wait()
    damp_load.wait()
    for d in range(3):
        flags[d] = jnp.concatenate([fraw[d], fraw[d]], axis=0)
    fx, fy, fz = (flags[d] == 1 for d in range(3))
    damping = jnp.concatenate([draw[...], draw[...]], axis=0)
    dmp[0] = (OMEGA * LIFT) * damping
    dmp[1] = (OMEGA * 0.5) * damping
    dmp[2] = OMEGA * SHIFT + (OMEGA * 1.5) * damping
    dmp[3] = jnp.where(low, (OMEGA * LIFT) * damping, 0.0)
    dmp[4] = jnp.where(low, 0.0, (OMEGA * LIFT) * damping)
    for b in range(4):
        for a_end in range(2):
            faces = a_end + (1 if b in (0, 3) else 0)
            base = OMEGA * SHIFT + (OMEGA * LIFT * faces) * damping
            kfine[b, a_end, 0] = base + dmp[3]
            kfine[b, a_end, 1] = base + dmp[4]

    jac_load.wait()

    @pl.loop(0, 75, unroll=15)
    def _(i):
        block = jraw[i]
        jn[i] = (-OMEGA) * jnp.concatenate([block, block], axis=0)

    csm_load.wait()

    @pl.loop(0, 25, unroll=5)
    def _(i):
        for n in range(2):
            block = csm[i, n].astype(F32)
            csf[i, n, 0] = block[:8]
            csf[i, n, 1] = block[8:]

    half_damp, k_coarse, lift_damp = dmp[1], dmp[2], dmp[0]

    def pack_side(side, first, second):
        mask, step = (x0, 2) if side < 2 else (y0, 1)
        return (pack_low if side % 2 == 0 else pack_high)(first, second, mask, step)

    for side in range(4):
        own = 0 if side < 2 else 1
        sign = -0.5 if side % 2 == 0 else 0.5

        @pl.loop(0, 5, unroll=True)
        def _(row, side=side, own=own, sign=sign):
            for col in range(5):
                diag = jnp.where(row == col, half_damp, zero)
                face = diag + sign * jn[25 * own + 5 * row + col]
                kface[5 * row + col] = pack_side(side, face, face)

        @pl.loop(0, 5, unroll=True)
        def _(vo, side=side):
            blocks = []
            for m in range(5):
                if side < 2:
                    pair = [csf[5 * vo + m, side, j] for j in range(2)]
                else:
                    pair = [csf[5 * vo + m, i, side - 2] for i in range(2)]
                blocks.append(pack_side(side, pair[0], pair[1]))
            for vi in range(5):
                total = blocks[0] * kface[vi]
                for m in range(1, 5):
                    total = total + blocks[m] * kface[5 * m + vi]
                sg[side, 5 * vo + vi] = total

        flag = jnp.where(flags[own] == 1, 1.0, 0.0)
        sg[side, 25] = pack_side(side, flag, flag)

    for a in (0, 3):
        for copy in parts[a]:
            copy.wait()

        @pl.loop(0, 4)
        def _(b, a=a):
            first_pass(a, b)

    HALF = {0: (0, 0), 3: (0, 1), 1: (1, 0), 2: (1, 1)}

    @pl.loop(0, 5, unroll=True)
    def _(v):
        for b in range(4):
            half, place = HALF[b]
            s1[0, half, v, place] = pack_low(q[v, 0, b, 0], q[v, 0, b, 1], x0, 2)
            hi = [jnp.where(fx, q[v, 3, 3 - b, h], q[v, 3, b, h]) for h in range(2)]
            s1[1, half, v, place] = pack_high(hi[0], hi[1], x0, 2)

    pl.semaphore_wait(barrier, 4)
    for half in range(2):
        for k in range(2):
            sends1[k][half].start()

    for a in (1, 2):
        for copy in parts[a]:
            copy.wait()

        @pl.loop(0, 4)
        def _(b, a=a):
            first_pass(a, b)

    @pl.loop(0, 5, unroll=True)
    def _(v):
        for a in range(4):
            s1[2, a // 2, v, a % 2] = pack_low(q[v, a, 0, 0], q[v, a, 0, 1], y0, 1)
            hi = [jnp.where(fy, q[v, 3 - a, 3, h], q[v, a, 3, h]) for h in range(2)]
            s1[3, a // 2, v, a % 2] = pack_high(hi[0], hi[1], y0, 1)

    sends1[2][0].start()
    sends1[3][0].start()


    c_first = [halves(OPEN[0, 1], OPEN[1, 0]), halves(OPEN[0, 2], OPEN[1, 3]), halves(OPEN[0, 3], OPEN[1, 2])]
    c_second = [halves(OPEN[2, 3], OPEN[3, 2]), halves(OPEN[2, 0], OPEN[3, 1]), halves(OPEN[2, 1], OPEN[3, 0])]
    c_ghost = [halves(-LIFT, 0.0), halves(0.0, LIFT)]

    @pl.loop(0, 20, unroll=4)
    def _(t):
        v, b = t // 4, t % 4
        first = [q[v, a, b, 0] for a in range(4)]
        second = [q[v, a, b, 1] for a in range(4)]
        for a in range(4):
            for h, line in enumerate((first, second)):
                wx[v, a, b, h] = dot_terms(OPEN[a], line)
        ghosts = z_ghosts([jnp.where(low, first[a], second[a]) for a in range(4)], fz)
        for a in range(4):
            a_end = 1 if a in (0, 3) else 0
            first_sw, second_sw = sub_roll(first[a], 4), sub_roll(second[a], 4)
            wz[v, a, b, 0] = (
                c_first[0] * first_sw + c_first[1] * second[a] + c_first[2] * second_sw + c_ghost[0] * ghosts[a]
            )
            wz[v, a, b, 1] = (
                c_second[0] * second_sw + c_second[1] * first[a] + c_second[2] * first_sw + c_ghost[1] * ghosts[a]
            )
            acc[v, a, b, 0] = src[v, a, b, 0] - kfine[b, a_end, 0] * first[a] + dmp[3] * ghosts[a]
            acc[v, a, b, 1] = src[v, a, b, 1] - kfine[b, a_end, 1] * second[a] + dmp[4] * ghosts[a]

    @pl.loop(0, 20, unroll=4)
    def _(t):
        v, a = t // 4, t % 4
        for h in range(2):
            line = [q[v, a, b, h] for b in range(4)]
            for b in range(4):
                wy[v, a, b, h] = dot_terms(OPEN[b], line)

    def mix_at(b, pair, directions, last):
        total = [[[acc[v, a, b, h] for h in range(2)] for a in pair] for v in range(5)]
        for d in directions:
            w = (wx, wy, wz)[d]
            for vi in range(5):
                flux = [[w[vi, a, b, h] for h in range(2)] for a in pair]
                for vo in range(5):
                    weight = jn[25 * d + 5 * vo + vi]
                    for n in range(2):
                        for h in range(2):
                            total[vo][n][h] = total[vo][n][h] + weight * flux[n][h]
        for n, a in enumerate(pair):
            if last:
                outs = smooth(a, b, [total[v][n] for v in range(5)])
            for v in range(5):
                for h in range(2):
                    if last:
                        q[v, a, b, h] = q[v, a, b, h] + outs[v][h]
                    else:
                        acc[v, a, b, h] = total[v][n][h]

    def mix(first, step, pair, directions, last):
        @pl.loop(0, 2)
        def _(t):
            mix_at(first + step * t, pair, directions, last)

    mix(0, 3, (0, 3), (2,), False)
    mix(0, 3, (1, 2), (0, 2), False)

    for copy in sends_face:
        copy.start()

    @pl.loop(0, 5, unroll=True)
    def _(v):
        by_a = []
        for a in range(4):
            by_a.append(restrict_line([restrict_c(src[v, a, b, 0], src[v, a, b, 1])[3] for b in range(4)]))
        for j in range(2):
            for i, value in enumerate(restrict_line([by_a[a][j] for a in range(4)])):
                rsrc[v, i, j] = value

    mix(1, 1, (0, 3), (1, 2), False)
    mix(1, 1, (1, 2), (0, 1, 2), True)

    sends1[2][0].wait_recv()
    sends1[3][0].wait_recv()

    @pl.loop(0, 5, unroll=True)
    def _(v):
        for h in range(2):
            lo = [q[v, a, 0, h] for a in range(4)]
            hi = [q[v, a, 3, h] for a in range(4)]
            right = []
            for a in range(4):
                packed = r1[2, a // 2, v, a % 2]
                right.append(jnp.where(y0, sub_roll(lo[a], -1), sub_roll(packed, 1) if h == 0 else packed))
            for a in range(4):
                packed = r1[3, a // 2, v, a % 2]
                hi_turned = jnp.where(fy, hi[3 - a], hi[a])
                left = jnp.where(y0, packed if h == 0 else sub_roll(packed, -1), sub_roll(hi_turned, 1))
                ghost = jnp.where(fy, right[3 - a], right[a])
                wy[v, a, 0, h] = wy[v, a, 0, h] - LIFT * left
                wy[v, a, 3, h] = wy[v, a, 3, h] + LIFT * ghost
                acc[v, a, 0, h] = acc[v, a, 0, h] + lift_damp * left
                acc[v, a, 3, h] = acc[v, a, 3, h] + lift_damp * ghost

    mix(0, 3, (0, 3), (1,), False)
    mix(0, 3, (1, 2), (1,), True)

    def restrict_c_into(v, a_list):
        for a in a_list:
            for b in range(4):
                rcs[v, a, b] = restrict_c(q[v, a, b, 0], q[v, a, b, 1])[3]

    @pl.loop(0, 5, unroll=True)
    def _(v):
        restrict_c_into(v, (1, 2))

    for half, nodes in enumerate(((0, 3), (1, 2))):
        sends1[0][half].wait_recv()
        sends1[1][half].wait_recv()

        @pl.loop(0, 5, unroll=True)
        def _(v, half=half, nodes=nodes):
            for h in range(2):
                lo = [q[v, 0, b, h] for b in nodes]
                hi = [q[v, 3, b, h] for b in nodes]
                right = []
                for n in range(2):
                    packed = r1[0, half, v, n]
                    right.append(jnp.where(x0, sub_roll(lo[n], -2), sub_roll(packed, 2) if h == 0 else packed))
                for n, b in enumerate(nodes):
                    packed = r1[1, half, v, n]
                    hi_turned = jnp.where(fx, hi[1 - n], hi[n])
                    left = jnp.where(x0, packed if h == 0 else sub_roll(packed, -2), sub_roll(hi_turned, 2))
                    ghost = jnp.where(fx, right[1 - n], right[n])
                    wx[v, 0, b, h] = wx[v, 0, b, h] - LIFT * left
                    wx[v, 3, b, h] = wx[v, 3, b, h] + LIFT * ghost
                    acc[v, 0, b, h] = acc[v, 0, b, h] + lift_damp * left
                    acc[v, 3, b, h] = acc[v, 3, b, h] + lift_damp * ghost

        for b in nodes:
            mix_at(b, (0, 3), (0,), True)

    def traces_of(field):
        return [
            [[field[v][0][n] for n in range(2)] for v in range(5)],
            [[field[v][1][n] for n in range(2)] for v in range(5)],
            [[field[v][n][0] for n in range(2)] for v in range(5)],
            [[field[v][n][1] for n in range(2)] for v in range(5)],
        ]

    def pack_traces(traces, target, turn):
        for v in range(5):
            for side in range(4):
                pair = traces[side][v]
                if turn and side % 2 == 1:
                    flip = fx if side < 2 else fy
                    pair = [jnp.where(flip, pair[1 - n], pair[n]) for n in range(2)]
                target[side, v] = pack_side(side, pair[0], pair[1])

    traces = [[None] * 5 for _ in range(4)]
    for v in range(5):
        restrict_c_into(v, (0, 3))
        for slot, a in ((0, 0), (1, 3)):
            traces[slot][v] = restrict_line([rcs[v, a, b] for b in range(4)])
        for slot, b in ((2, 0), (3, 3)):
            traces[slot][v] = restrict_line([rcs[v, a, b] for a in range(4)])
    pack_traces(traces, s2, True)

    for copy in sends2:
        copy.start()

    def inner_ghosts(lo, hi, mask, step, flip):
        right = [jnp.where(mask, sub_roll(value, -step), zero) for value in lo]
        right = [jnp.where(flip, right[1 - n], right[n]) for n in range(2)]
        hi = [jnp.where(flip, hi[1 - n], hi[n]) for n in range(2)]
        left = [jnp.where(mask, zero, sub_roll(value, step)) for value in hi]
        return left, right

    def coarse_sweep():
        total = [[[crhs[v, i, j] for j in range(2)] for i in range(2)] for v in range(5)]
        for d in range(3):
            for vi in range(5):
                flux = [[wc[d, vi, i, j] for j in range(2)] for i in range(2)]
                for vo in range(5):
                    weight = jn[25 * d + 5 * vo + vi]
                    for i in range(2):
                        for j in range(2):
                            total[vo][i][j] = total[vo][i][j] + weight * flux[i][j]
        outs = [[[None, None] for _ in range(2)] for _ in range(5)]
        for vo in range(5):
            for vi in range(5):
                for i in range(2):
                    for j in range(2):
                        term = csf[5 * vo + vi, i, j] * total[vi][i][j]
                        outs[vo][i][j] = term if vi == 0 else outs[vo][i][j] + term
        return outs

    e_ends = halves(EDGE[0, 0], EDGE[1, 3])
    e_ends_sw = halves(EDGE[0, 3], EDGE[1, 0])
    e_inner = halves(EDGE[0, 1], EDGE[1, 2])
    e_inner_sw = halves(EDGE[0, 2], EDGE[1, 1])
    z_lift = halves(-LIFT, LIFT)

    for v in range(5):
        rbc = [restrict_line([rcs[v, a, b] for b in range(4)]) for a in range(4)]
        rac = [restrict_line([rcs[v, a, b] for a in range(4)]) for b in range(4)]
        ra = [[restrict_line([q[v, a, b, h] for a in range(4)]) for b in range(4)] for h in range(2)]
        ends_of = [[None, None], [None, None]]
        rhs = [[None, None], [None, None]]
        w = [[[None, None], [None, None]] for _ in range(3)]
        for i in range(2):
            first = restrict_line([ra[0][b][i] for b in range(4)])
            second = restrict_line([ra[1][b][i] for b in range(4)])
            for j in range(2):
                w[0][i][j] = dot_terms(EDGE[i], [rbc[a][j] for a in range(4)])
                w[1][i][j] = dot_terms(EDGE[j], [rac[b][i] for b in range(4)])
                ends, inner, inner_sw, full = restrict_c(first[j], second[j])
                ends_of[j][i] = ends
                w[2][i][j] = (
                    e_ends * ends + e_ends_sw * sub_roll(ends, 4) + e_inner * inner + e_inner_sw * inner_sw
                )
                rhs[i][j] = rsrc[v, i, j] - (OMEGA * SHIFT) * full
        for j in range(2):
            ghosts = z_ghosts(ends_of[j], fz)
            for i in range(2):
                w[2][i][j] = w[2][i][j] + z_lift * ghosts[i]
                rhs[i][j] = rhs[i][j] + lift_damp * (ghosts[i] - ends_of[j][i])
        left, right = inner_ghosts(traces[0][v], traces[1][v], x0, 2, fx)
        for j in range(2):
            w[0][0][j] = w[0][0][j] - LIFT * left[j]
            w[0][1][j] = w[0][1][j] + LIFT * right[j]
            rhs[0][j] = rhs[0][j] + lift_damp * (left[j] - traces[0][v][j])
            rhs[1][j] = rhs[1][j] + lift_damp * (right[j] - traces[1][v][j])
        left, right = inner_ghosts(traces[2][v], traces[3][v], y0, 1, fy)
        for i in range(2):
            w[1][i][0] = w[1][i][0] - LIFT * left[i]
            w[1][i][1] = w[1][i][1] + LIFT * right[i]
            rhs[i][0] = rhs[i][0] + lift_damp * (left[i] - traces[2][v][i])
            rhs[i][1] = rhs[i][1] + lift_damp * (right[i] - traces[3][v][i])
        for i in range(2):
            for j in range(2):
                crhs[v, i, j] = rhs[i][j]
                for d in range(3):
                    wc[d, v, i, j] = w[d][i][j]

    outs = coarse_sweep()
    for v in range(5):
        for i in range(2):
            for j in range(2):
                cloc[v, i, j] = outs[v][i][j]

    @pl.loop(0, 20, unroll=4)
    def _(t):
        v, b = t // 4, t % 4
        for a in range(4):
            for h in range(2):
                out[v, a, b, h] = OMEGA * q[v, a, b, h]

    def face_product(ref, side, vectors):
        outs = []
        for vo in range(5):
            total = ref[side, 5 * vo] * vectors[0]
            for vi in range(1, 5):
                total = total + ref[side, 5 * vo + vi] * vectors[vi]
            outs.append(total)
        return outs

    def own_ghost(side, value):
        if side % 2 == 0:
            return value
        return jnp.where(sg[side, 25] == 1.0, swap_rows(value, 2 if side < 2 else 1), value)

    def face_terms(ghosts):
        pairs = [[None] * 5 for _ in range(4)]
        for side in range(4):
            mask, step = (x0, 2) if side < 2 else (y0, 1)
            for v, delta in enumerate(face_product(sg, side, ghosts[side])):
                if side % 2 == 0:
                    pairs[side][v] = [
                        jnp.where(mask, delta, zero), jnp.where(mask, sub_roll(delta, -step), zero)
                    ]
                else:
                    pairs[side][v] = [
                        jnp.where(mask, zero, sub_roll(delta, step)), jnp.where(mask, zero, delta)
                    ]
        return [[[pairs[i][v][j] + pairs[2 + j][v][i] for j in range(2)] for i in range(2)] for v in range(5)]

    def inner_operator(field):
        for v in range(5):
            here = field[v]
            rhs = [[(-k_coarse) * here[i][j] for j in range(2)] for i in range(2)]
            for j in range(2):
                ghosts = z_ghosts([here[i][j] for i in range(2)], fz)
                for i in range(2):
                    swapped = sub_roll(here[i][j], 4)
                    wc[2, v, i, j] = jnp.where(low, 0.5, -0.5) * (swapped - ghosts[i])
                    rhs[i][j] = rhs[i][j] + half_damp * ghosts[i]
            left, right = inner_ghosts(here[0], here[1], x0, 2, fx)
            for j in range(2):
                wc[0, v, 0, j] = 0.5 * (here[1][j] - left[j])
                wc[0, v, 1, j] = 0.5 * (right[j] - here[0][j])
                rhs[0][j] = rhs[0][j] + half_damp * left[j]
                rhs[1][j] = rhs[1][j] + half_damp * right[j]
            left, right = inner_ghosts([here[i][0] for i in range(2)], [here[i][1] for i in range(2)], y0, 1, fy)
            for i in range(2):
                wc[1, v, i, 0] = 0.5 * (here[i][1] - left[i])
                wc[1, v, i, 1] = 0.5 * (right[i] - here[i][0])
                rhs[i][0] = rhs[i][0] + half_damp * left[i]
                rhs[i][1] = rhs[i][1] + half_damp * right[i]
            for i in range(2):
                for j in range(2):
                    crhs[v, i, j] = rhs[i][j]
        return coarse_sweep()

    def combine(function, *fields):
        return [
            [[function(*(f[v][i][j] for f in fields)) for j in range(2)] for i in range(2)] for v in range(5)
        ]

    def load_field(ref):
        return [[[ref[v, i, j] for j in range(2)] for i in range(2)] for v in range(5)]

    for copy in sends2:
        copy.wait_recv()
    terms = face_terms([[own_ghost(side, r2[side ^ 1, v]) for v in range(5)] for side in range(4)])
    coarse = combine(lambda x, y: x + 6.0 * y, load_field(cloc), terms)
    pack_traces(traces_of(coarse), s3, True)

    for copy in sends_face:
        copy.wait_recv()

    added = []
    for side in range(4):
        mine = [s3[side, v] for v in range(5)]
        if side % 2 == 0:
            turn = rg[side ^ 1, 25] == 1.0
            mine = [jnp.where(turn, swap_rows(value, 2 if side < 2 else 1), value) for value in mine]
        added.append(face_product(rg, side ^ 1, mine))
    for k, (along_y, along_x, y_row, x_row) in enumerate(CORNERS):
        slots = []
        for v in range(5):
            slots += [(added[along_y][v], y_row), (added[along_x][v], x_row)]
        for n in range(3):
            tile = zero
            for place, (value, source) in enumerate(slots[4 * n : 4 * n + 4]):
                tile = jnp.where(row4 == place, sub_roll(value, place - source), tile)
            sd[k, n] = tile

    for copy in sends_corner + sends3:
        copy.start()

    outs = inner_operator(coarse)
    partial = combine(lambda x, y: 2.0 * x + y, coarse, outs)
    pack_traces(traces_of(partial), sp, False)

    for copy in sends_part:
        copy.start()

    for v in range(5):
        for side in range(4):
            gcor[side, v] = added[side][v]
        for i in range(2):
            for j in range(2):
                cloc[v, i, j] = coarse[v][i][j]
                cpart[v, i, j] = partial[v][i][j]

    for copy in sends3:
        copy.wait_recv()

    terms = face_terms([[own_ghost(side, r3[side ^ 1, v]) for v in range(5)] for side in range(4)])
    middle = combine(lambda x, y: x + y, load_field(cpart), terms)
    outs = inner_operator(middle)
    coarse = combine(lambda x, y, z: x + y + z, load_field(cloc), middle, outs)

    for copy in sends_corner:
        copy.wait_recv()

    def corner_rows(side, v):
        lower, upper = ((3, 1), (2, 0), (3, 2), (1, 0))[side]
        slot = 2 * v + (0 if side < 2 else 1)
        tile, place = slot // 4, slot % 4
        lower, upper = sub_roll(rd[lower, tile], -place), sub_roll(rd[upper, tile], 3 - place)
        return jnp.where(row4 == 0, lower, jnp.where(row4 == 3, upper, zero))

    beside = [[corner_rows(side, v) for v in range(5)] for side in range(4)]

    for copy in sends_part:
        copy.wait_recv()

    ghosts = []
    for side in range(4):
        values = [rp[side ^ 1, v] + (gcor[side, v] + beside[side][v]) for v in range(5)]
        if side % 2 == 0:
            turn = rg[side ^ 1, 25] == 1.0
            values = [jnp.where(turn, swap_rows(value, 2 if side < 2 else 1), value) for value in values]
        else:
            values = [own_ghost(side, value) for value in values]
        ghosts.append(values)
    coarse = combine(lambda x, y: x + y, coarse, face_terms(ghosts))

    t_first = [halves(OMEGA, OMEGA * P_FAR), halves(0.0, OMEGA * P_NEAR)]
    t_second = [halves(OMEGA * P_FAR, OMEGA), halves(OMEGA * P_NEAR, 0.0)]

    for v in range(5):
        by_a = [prolong_line([coarse[v][i][j] for i in range(2)]) for j in range(2)]
        for a in range(4):
            for b, value in enumerate(prolong_line([by_a[j][a] for j in range(2)])):
                swapped = sub_roll(value, 4)
                out[v, a, b, 0] = out[v, a, b, 0] + (t_first[0] * value + t_first[1] * swapped)
                out[v, a, b, 1] = out[v, a, b, 1] + (t_second[0] * value + t_second[1] * swapped)

    for copy in started:
        copy.wait_send()


def body(source, jacobian, damping, orient, smoother, coarse_smoother):
    field = (5, 4, 4, 2, 8, 128)
    vmem = pltpu.VMEM
    hbm = pl.BlockSpec(memory_space=pltpu.HBM)
    out = pl.pallas_call(
        kernel,
        out_shape=pltpu.VMEM(field, F32),
        in_specs=[hbm] * 6,
        out_specs=pl.BlockSpec(memory_space=pltpu.VMEM),
        scratch_shapes=[
            vmem(field, F32),
            vmem((25, 4, 4, 16, 128), jnp.bfloat16),
            vmem((25, 2, 16, 128), jnp.bfloat16),
            vmem((75, 4, 128), F32),
            vmem((75, 8, 128), F32),
            vmem((4, 128), F32),
            vmem((3, 4, 128), jnp.int32),
            vmem((3, 8, 128), jnp.int32),
            vmem((5, 8, 128), F32),
            vmem((4, 2, 2, 8, 128), F32),
            vmem((25, 2, 2, 8, 128), F32),
            vmem((25, 8, 128), F32),
            vmem(field, F32),
            vmem(field, F32),
            vmem(field, F32),
            vmem(field, F32),
            vmem(field, F32),
            vmem((5, 2, 2, 8, 128), F32),
            vmem((5, 4, 4, 8, 128), F32),
            vmem((5, 2, 2, 8, 128), F32),
            vmem((5, 2, 2, 8, 128), F32),
            vmem((4, 5, 8, 128), F32),
            vmem((3, 5, 2, 2, 8, 128), F32),
            vmem((5, 2, 2, 8, 128), F32),
            vmem((4, 2, 5, 2, 8, 128), F32),
            vmem((4, 2, 5, 2, 8, 128), F32),
            vmem((4, 5, 8, 128), F32),
            vmem((4, 5, 8, 128), F32),
            vmem((4, 5, 8, 128), F32),
            vmem((4, 5, 8, 128), F32),
            vmem((4, 5, 8, 128), F32),
            vmem((4, 5, 8, 128), F32),
            vmem((4, 3, 8, 128), F32),
            vmem((4, 3, 8, 128), F32),
            vmem((4, 26, 8, 128), F32),
            vmem((4, 26, 8, 128), F32),
            pltpu.SemaphoreType.DMA((12,)),
            pltpu.SemaphoreType.DMA((28,)),
            pltpu.SemaphoreType.DMA((28,)),
        ],
        compiler_params=pltpu.CompilerParams(collective_id=0, has_side_effects=True),
    )(
        source.reshape(field),
        jacobian.reshape(75, 4, 128),
        damping.reshape(4, 128),
        orient.reshape(3, 4, 128),
        smoother.reshape(25, 4, 4, 16, 128),
        coarse_smoother.reshape(25, 2, 16, 128),
    )
    return out.reshape(5, 4, 4, 4, 2, 2, 128)


def solution(mesh):
    in_specs = (
        P(None, None, None, None, "gx", "gy", None),
        P(None, None, None, "gx", "gy", None),
        P("gx", "gy", None),
        P(None, "gx", "gy", None),
        P(None, None, None, None, None, "gx", "gy", None),
        P(None, None, None, None, None, "gx", "gy", None),
    )
    out_specs = P(None, None, None, None, "gx", "gy", None)
    return jax.shard_map(body, mesh=mesh, in_specs=in_specs, out_specs=out_specs, check_vma=False)
```
